32 devices in a mesh: dp: 8 (over z, core), fsdp: 4 (over y, x).
Axes of the slice: x: 2, y: 2, z: 4, core: 2. Of those that a mesh axis runs over, the one named last changes fastest.
Arguments:
- tokens: bfloat16 [32, 320, 1024], P(('dp', 'fsdp')), may hold values from -6 to 6
- cotangent: bfloat16 [32, 320, 1024], P(('dp', 'fsdp')), may hold values from -6 to 6
- counts: int32 [32], P(('dp', 'fsdp')), may hold values from 64 to 320, as said below
- w_qkv: float32 [1024, 3072], P(('dp', 'fsdp')), may hold values from -0.3125 to 0.3125
- w_out: float32 [1024, 1024], P(None, ('dp', 'fsdp')), may hold values from -0.75 to 0.75
- w_up: float32 [1024, 4096], P(('dp', 'fsdp')), may hold values from -0.1875 to 0.1875
- w_down: float32 [4096, 1024], P(None, ('dp', 'fsdp')), may hold values from -0.09375 to 0.09375
- vectors: float32 [12, 1024], P(None, ('dp', 'fsdp')), may hold values from -0.9 to 1.4
- mean_qkv: float32 [1024, 3072], P(('dp', 'fsdp')), may hold values from -28 to 28
- mean_out: float32 [1024, 1024], P(None, ('dp', 'fsdp')), may hold values from -16 to 16
- mean_up: float32 [1024, 4096], P(('dp', 'fsdp')), may hold values from -16 to 16
- mean_down: float32 [4096, 1024], P(None, ('dp', 'fsdp')), may hold values from -32 to 32
- mean_vectors: float32 [12, 1024], P(None, ('dp', 'fsdp')), may hold values from -40 to 40
- square_qkv: float32 [1024, 3072], P(('dp', 'fsdp')), may hold values from 81.92 to 327.68
- square_out: float32 [1024, 1024], P(None, ('dp', 'fsdp')), may hold values from 29.696 to 116.736
- square_up: float32 [1024, 4096], P(('dp', 'fsdp')), may hold values from 29.696 to 116.736
- square_down: float32 [4096, 1024], P(None, ('dp', 'fsdp')), may hold values from 117.76 to 471.04
- square_vectors: float32 [12, 1024], P(None, ('dp', 'fsdp')), may hold values from 204.8 to 819.2
Outputs:
- result: bfloat16 [32, 320, 1024], P(('dp', 'fsdp'))
- token_grad: bfloat16 [32, 320, 1024], P(('dp', 'fsdp'))
- head_peak: float32 [16], replicated
- new_mean_qkv: float32 [1024, 3072], P(('dp', 'fsdp'))
- new_square_qkv: float32 [1024, 3072], P(('dp', 'fsdp'))
- new_w_qkv: float32 [1024, 3072], P(('dp', 'fsdp'))
- new_mean_out: float32 [1024, 1024], P(None, ('dp', 'fsdp'))
- new_square_out: float32 [1024, 1024], P(None, ('dp', 'fsdp'))
- new_w_out: float32 [1024, 1024], P(None, ('dp', 'fsdp'))
- new_mean_up: float32 [1024, 4096], P(('dp', 'fsdp'))
- new_square_up: float32 [1024, 4096], P(('dp', 'fsdp'))
- new_w_up: float32 [1024, 4096], P(('dp', 'fsdp'))
- new_mean_down: float32 [4096, 1024], P(None, ('dp', 'fsdp'))
- new_square_down: float32 [4096, 1024], P(None, ('dp', 'fsdp'))
- new_w_down: float32 [4096, 1024], P(None, ('dp', 'fsdp'))
- new_mean_vectors: float32 [12, 1024], P(None, ('dp', 'fsdp'))
- new_square_vectors: float32 [12, 1024], P(None, ('dp', 'fsdp'))
- new_vectors: float32 [12, 1024], P(None, ('dp', 'fsdp'))
The draws below stay inside these ranges and needn't reach their ends.
Inputs may be any that keep to these rules, and one draw needn't show every extreme that they name: `counts`: in every draw some sequence keeps all 320 slots.
All inputs are finite; a program needn't handle non-finite values.
Results may differ from the reference program's by a relative error of at most 0.012.
The reference program's roundings to bfloat16 on the way count: a program that leaves them out, or rounds other values in their place, can miss the bound.
Values may be sent and summed in bfloat16 or wider, within the bound.
No kernel may reach another device: no remote copies, remote signals or barrier semaphores. Data moves between devices by JAX's collectives and lax.ppermute only.
A program may use at most 192 MiB of HBM per device.

```python
import math
import jax
import jax.numpy as jnp
from jax import lax

D = 1024
H = 16
FF = 4096
SLOTS = 320
STEP = 10
SEQS = 32


def draw_counts(key, part):
    key = jax.random.fold_in(key, 11)
    first_key, second_key = jax.random.split(key)
    rising = jnp.arange(SEQS, dtype=jnp.int32)
    floor_part = SLOTS // 5 + rising * (3 * SLOTS // 5) // (SEQS - 1)
    jitter = jax.random.randint(first_key, (SEQS,), 0, SLOTS // 5 + 1, dtype=jnp.int32)
    counts = jnp.minimum(floor_part + jitter, SLOTS)
    chosen = jax.random.randint(second_key, (), 0, SEQS, dtype=jnp.int32)
    return jnp.where(rising == chosen, SLOTS, counts).astype(jnp.int32)


def draw_w_qkv(key, part):
    key = jax.random.fold_in(key, 23)
    base_key, scale_key = jax.random.split(key)
    entries = jnp.clip(jax.random.normal(base_key, (D, 3 * D), jnp.float32), -4.0, 4.0)
    head_scale = jnp.exp(jax.random.uniform(scale_key, (H,), jnp.float32, 0.0, math.log(2.5)))
    column_scale = jnp.concatenate([jnp.repeat(head_scale, D // H), jnp.ones((2 * D,), jnp.float32)])
    return entries * column_scale[None, :] / math.sqrt(D)


def draw_vectors(key, part):
    key = jax.random.fold_in(key, 37)
    gain_key, shift_key = jax.random.split(key)
    shift_count = 6 + FF // D
    gain_rows = 1.0 + 0.2 * jnp.clip(jax.random.normal(gain_key, (2, D), jnp.float32), -2.0, 2.0)
    shifts = 0.3 * jnp.clip(jax.random.normal(shift_key, (shift_count, D), jnp.float32), -3.0, 3.0)
    return jnp.concatenate([gain_rows[0:1], shifts[0:1], gain_rows[1:2], shifts[1:]], 0)


def spiked(values, key, source, target, blocks, factor):
    def block_of(position):
        return (jnp.arange(values.shape[position]) // (values.shape[position] // blocks)).reshape((-1,) + (1,) * (values.ndim - 1 - position))

    first = jax.random.permutation(key, blocks)[block_of(target)]
    far = (block_of(target) + blocks // 2) % blocks
    return jnp.where((block_of(source) == first) | (block_of(source) == far), factor * values, values)


def shard_levels(rng, shape, shards, low, top_value):
    loudness = 1.0
    for axis_at, parts in shards:
        steps = jax.random.uniform(jax.random.fold_in(jax.random.fold_in(rng, 6), axis_at), (parts,), jnp.float32, low / len(shards), top_value / len(shards))
        loudness = loudness * jnp.repeat(jnp.exp(steps), shape[axis_at] // parts).reshape((-1,) + (1,) * (len(shape) - 1 - axis_at))
    return loudness


def gaussian(stream_key, dims, width, most, cuts=(), kind=jnp.bfloat16):
    factor_of = shard_levels(stream_key, dims, cuts, -0.22, 0.18) if cuts else 1.0
    values = jax.random.normal(stream_key, dims, jnp.float32) * width * factor_of
    return jnp.minimum(jnp.maximum(values, -most), most).astype(kind)


def bell_draw_with(stream_key, extent, scale, bound, pieces, heavy, kind=jnp.bfloat16):
    values = scale * jax.random.normal(stream_key, extent, jnp.float32)
    if pieces:
        values = values * shard_levels(stream_key, extent, pieces, -0.22, 0.18)
    return jnp.clip(spiked(values, jax.random.fold_in(stream_key, 3), *heavy), -bound, bound).astype(kind)


def setup_inputs(seed: int = 0) -> dict:
    key_list = jax.random.split(jax.random.key(seed), 19)
    tokens = bell_draw_with(key_list[0], (SEQS, SLOTS, D), 1.0, 6.0, ((0, 32),), (0, 2, 32, 2.75))
    cotangent = bell_draw_with(key_list[1], (SEQS, SLOTS, D), 1.0, 6.0, ((0, 32),), (0, 2, 32, 2.75))
    counts = draw_counts(jax.random.fold_in(key_list[18], 71), 0)
    w_qkv = draw_w_qkv(jax.random.fold_in(key_list[18], 71), 0)
    w_out = gaussian(key_list[4], (D, D), (D // 16) ** -0.5, 0.75, ((1, 32),), jnp.float32)
    w_up = gaussian(key_list[5], (D, FF), D ** -0.5, 0.1875, ((0, 32),), jnp.float32)
    w_down = gaussian(key_list[6], (FF, D), FF ** -0.5, 0.09375, ((1, 32),), jnp.float32)
    vectors = draw_vectors(jax.random.fold_in(key_list[18], 71), 0)
    mean_qkv = gaussian(key_list[8], (D, 3 * D), (0.043 * (SLOTS * SEQS) ** 0.5), 28.0, ((0, 32),), jnp.float32)
    mean_out = gaussian(key_list[9], (D, D), (0.026 * (SLOTS * SEQS) ** 0.5), 16.0, ((1, 32),), jnp.float32)
    mean_up = gaussian(key_list[10], (D, FF), (0.026 * (SLOTS * SEQS) ** 0.5), 16.0, ((0, 32),), jnp.float32)
    mean_down = gaussian(key_list[11], (FF, D), (0.051 * (SLOTS * SEQS) ** 0.5), 32.0, ((1, 32),), jnp.float32)
    mean_vectors = gaussian(key_list[12], (8 + FF // D, D), (0.068 * (SLOTS * SEQS) ** 0.5), 40.0, ((1, 32),), jnp.float32)
    square_qkv = jnp.clip(jnp.exp(math.log(327.68) - 1.3862944 * jax.random.uniform(key_list[13], (D, 3 * D), jnp.float32) ** shard_levels(key_list[13], (D, 3 * D), ((0, 32),), -0.2, 0.2)), 81.92, 327.68)
    square_out = jnp.clip(jnp.exp(math.log(116.736) - 1.36890265 * jax.random.uniform(key_list[14], (D, D), jnp.float32) ** shard_levels(key_list[14], (D, D), ((1, 32),), -0.2, 0.2)), 29.696, 116.736)
    square_up = jnp.clip(jnp.exp(math.log(116.736) - 1.36890265 * jax.random.uniform(key_list[15], (D, FF), jnp.float32) ** shard_levels(key_list[15], (D, FF), ((0, 32),), -0.2, 0.2)), 29.696, 116.736)
    square_down = jnp.clip(jnp.exp(math.log(471.04) - 1.3862944 * jax.random.uniform(key_list[16], (FF, D), jnp.float32) ** shard_levels(key_list[16], (FF, D), ((1, 32),), -0.2, 0.2)), 117.76, 471.04)
    square_vectors = jnp.clip(jnp.exp(math.log(819.2) - 1.3862944 * jax.random.uniform(key_list[17], (8 + FF // D, D), jnp.float32) ** shard_levels(key_list[17], (8 + FF // D, D), ((1, 32),), -0.2, 0.2)), 204.8, 819.2)
    return dict(tokens=tokens, cotangent=cotangent, counts=counts, w_qkv=w_qkv, w_out=w_out, w_up=w_up, w_down=w_down, vectors=vectors, mean_qkv=mean_qkv, mean_out=mean_out, mean_up=mean_up, mean_down=mean_down, mean_vectors=mean_vectors, square_qkv=square_qkv, square_out=square_out, square_up=square_up, square_down=square_down, square_vectors=square_vectors)


@jax.custom_vjp
def low(v):
    return lax.optimization_barrier(v.astype(jnp.bfloat16)).astype(jnp.float32)

@jax.custom_vjp
def low_back(v):
    return v

def low_keep(v):
    return (low(v), None)

def low_pass(kept, grad):
    return (grad,)

def back_keep(v):
    return (v, None)

def back_low(kept, grad):
    return (low(grad),)
low.defvjp(low_keep, low_pass)
low_back.defvjp(back_keep, back_low)
beta_one = 0.9
beta_two = 0.95
adam_epsilon = 1e-08
weight_decay = 0.1
matrix_rate = 0.1
vector_rate = 0.5
clip_limit = 8.0
norm_epsilon = 1e-06
masked_value = -1e+30

def layer_norm(values, gain_row, shift_row):
    centered = values - lax.optimization_barrier(jnp.mean(values, -1, keepdims=True))
    spread = lax.optimization_barrier(jnp.mean(centered * centered, -1, keepdims=True))
    return centered * lax.rsqrt(spread + norm_epsilon) * gain_row + shift_row

def adam_step(weight, gradient, mean_old, square_old, step_rate, decay_rate):
    mean_new = beta_one * mean_old + (1.0 - beta_one) * gradient
    square_new = beta_two * square_old + (1.0 - beta_two) * gradient * gradient
    fix_one = 1.0 - beta_one ** STEP
    fix_two = 1.0 - beta_two ** STEP
    stepped = weight - step_rate * (mean_new / fix_one / (jnp.sqrt(square_new / fix_two) + adam_epsilon) + decay_rate * weight)
    return (mean_new, square_new, stepped)

def group_forward(params, inputs, group_counts):
    w_qkv, w_out, w_up, w_down, vectors = params
    precise = lax.Precision.HIGHEST
    low_qkv = low(w_qkv)
    low_out = low(w_out)
    low_up = low(w_up)
    low_down = low(w_down)
    low_vectors = low(vectors)
    head_width = D // H
    score_scale = head_width ** (-0.5)
    groups = inputs.shape[0]
    slot_count = inputs.shape[1]
    keep_mask = (jnp.arange(slot_count, dtype=jnp.int32)[None, :] < group_counts[:, None]).astype(jnp.float32)
    normed = low(layer_norm(inputs, low_vectors[0], low_vectors[1]))
    projected = jnp.einsum('gtd,de->gte', normed, low_qkv, precision=precise)
    queries = low_back(low(projected[..., :D] + low_vectors[4])).reshape(groups, slot_count, H, head_width)
    key_part = low_back(low(projected[..., D:2 * D])).reshape(groups, slot_count, H, head_width)
    values_part = low_back(low(projected[..., 2 * D:] + low_vectors[5])).reshape(groups, slot_count, H, head_width)
    raw_scores = jnp.einsum('gqhc,gkhc->ghqk', queries, key_part, precision=precise) * score_scale
    valid_key = keep_mask[:, None, None, :] > 0.5
    valid_pair = valid_key & (keep_mask[:, None, :, None] > 0.5)
    group_peak = lax.optimization_barrier(jnp.max(jnp.where(valid_pair, raw_scores, masked_value), axis=(0, 2, 3)))
    scores = jnp.where(valid_key, low_back(raw_scores), masked_value)
    row_top = lax.optimization_barrier(jnp.max(scores, -1, keepdims=True))
    exponent = jnp.exp(scores - row_top)
    attention_probs = low(exponent / lax.optimization_barrier(jnp.sum(exponent, -1, keepdims=True)))
    attended = jnp.einsum('ghqk,gkhc->gqhc', attention_probs, values_part, precision=precise).reshape(groups, slot_count, D)
    attended = low_back(low(attended))
    branch = low_back(jnp.einsum('gtd,de->gte', attended, low_out, precision=precise) + low_vectors[6])
    middle = inputs + branch
    normed_two = low(layer_norm(middle, low_vectors[2], low_vectors[3]))
    bias_up = low_vectors[8:].reshape(-1)
    hidden_pre = low_back(jnp.einsum('gtd,df->gtf', normed_two, low_up, precision=precise) + bias_up)
    hidden = low(jax.nn.gelu(hidden_pre, approximate=False))
    down_part = low_back(jnp.einsum('gtf,fd->gtd', hidden, low_down, precision=precise) + low_vectors[7])
    return (keep_mask[..., None] * (middle + down_part), group_peak)

def reference(tokens, cotangent, counts, w_qkv, w_out, w_up, w_down, vectors, mean_qkv, mean_out, mean_up, mean_down, mean_vectors, square_qkv, square_out, square_up, square_down, square_vectors):
    group_size = 8
    params = (w_qkv, w_out, w_up, w_down, vectors)
    inputs = tokens.astype(jnp.float32).reshape(SEQS // group_size, group_size, SLOTS, D)
    grouped_counts = counts.reshape(SEQS // group_size, group_size)

    def run_layer(params, inputs):

        def run_group(group_pair):
            return jax.checkpoint(group_forward)(params, group_pair[0], group_pair[1])
        results, group_peaks = lax.map(run_group, (inputs, grouped_counts))
        return (results, lax.optimization_barrier(jnp.max(group_peaks, 0)))
    results, pullback, head_peak = jax.vjp(run_layer, params, inputs, has_aux=True)
    gradients, token_grads = pullback(cotangent.astype(jnp.float32).reshape(inputs.shape))
    result = results.reshape(SEQS, SLOTS, D).astype(jnp.bfloat16)
    token_grad = token_grads.reshape(SEQS, SLOTS, D).astype(jnp.bfloat16)
    grad_qkv, grad_out, grad_up, grad_down, grad_vectors = gradients
    mean_q, square_q, stepped_qkv = adam_step(w_qkv, grad_qkv, mean_qkv, square_qkv, matrix_rate, weight_decay)
    mean_o, square_o, new_out = adam_step(w_out, grad_out, mean_out, square_out, matrix_rate, weight_decay)
    mean_u, square_u, new_up = adam_step(w_up, grad_up, mean_up, square_up, matrix_rate, weight_decay)
    mean_d, square_d, new_down = adam_step(w_down, grad_down, mean_down, square_down, matrix_rate, weight_decay)
    mean_v, square_v, stepped_vectors = adam_step(vectors, grad_vectors, mean_vectors, square_vectors, vector_rate, 0.0)
    shrink = jnp.sqrt(clip_limit / jnp.maximum(head_peak, clip_limit))
    head_cols = jnp.repeat(shrink, D // H)
    qkv_scale = jnp.concatenate([head_cols, head_cols, jnp.ones((D,), jnp.float32)])
    new_qkv = stepped_qkv * qkv_scale[None, :]
    row_pick = (jnp.arange(vectors.shape[0], dtype=jnp.int32) == 4)[:, None]
    new_vectors = jnp.where(row_pick, stepped_vectors * head_cols[None, :], stepped_vectors)
    return (result, token_grad, head_peak, mean_q, square_q, new_qkv, mean_o, square_o, new_out, mean_u, square_u, new_up, mean_d, square_d, new_down, mean_v, square_v, new_vectors)
```

```python
from functools import partial

import jax
import jax.numpy as jnp
import numpy as np
from jax import lax
from jax.experimental import pallas as pl
from jax.experimental.pallas import tpu as pltpu
from jax.sharding import PartitionSpec as P

H = 16
STEP = 10


beta_one = 0.9
beta_two = 0.95
adam_epsilon = 1e-08
weight_decay = 0.1
matrix_rate = 0.1
vector_rate = 0.5
clip_limit = 8.0
norm_epsilon = 1e-06
masked_value = -1e30
TILE = 512
PAIR = 128
HALF_ROOT = 0.5**0.5
DENSITY = 0.3989422804014327
F32 = jnp.float32
BF16 = jnp.bfloat16


def adam_step(weight, gradient, mean_old, square_old, step_rate, decay_rate):
    mean_new = beta_one * mean_old + (1.0 - beta_one) * gradient
    square_new = beta_two * square_old + (1.0 - beta_two) * gradient * gradient
    fix_one = 1.0 - beta_one**STEP
    fix_two = 1.0 - beta_two**STEP
    stepped = weight - step_rate * (
        mean_new / fix_one / (jnp.sqrt(square_new / fix_two) + adam_epsilon) + decay_rate * weight
    )
    return (mean_new, square_new, stepped)


def bit_names(letter, count):
    return tuple(letter + str(at) for at in range(count))


class Links:
    def __init__(self, dp_count, inner_count):
        self.device_count = dp_count * inner_count
        inner_bits = inner_count.bit_length() - 1
        z_bits = bit_names("z", dp_count.bit_length() - 2)
        x_bits = bit_names("x", inner_bits // 2)
        y_bits = bit_names("y", inner_bits - inner_bits // 2)
        self.place = {"c": ("dp", dp_count, 0)}
        self.place.update({bit: ("dp", dp_count, at + 1) for at, bit in enumerate(z_bits)})
        self.place.update({bit: ("fsdp", inner_count, at) for at, bit in enumerate(x_bits)})
        self.place.update(
            {bit: ("fsdp", inner_count, at + len(x_bits)) for at, bit in enumerate(y_bits)}
        )
        self.bits = ("c",) + y_bits + x_bits + z_bits
        self.orders = (y_bits + x_bits, x_bits + y_bits)
        self.z_bits = z_bits
        self.y_bits = y_bits
        self.inner_bits = inner_bits

    def true_block(self):
        masks = []
        for block in range(self.device_count):
            mask = 0
            for at, bit in enumerate(reversed(self.bits)):
                if block >> at & 1:
                    axis, _, place = self.place[bit]
                    mask |= 1 << (place + (self.inner_bits if axis == "dp" else 0))
            masks.append(mask)
        return lax.axis_index(("dp", "fsdp")) ^ jnp.array(masks, jnp.int32)

    def exchange(self, values, bit):
        axis, count, place = self.place[bit]
        return lax.ppermute(values, axis, [(at, at ^ (1 << place)) for at in range(count)])


class Order:
    def __init__(self):
        self.ended = ()

    def __call__(self, call, *operands):
        operands, _ = lax.optimization_barrier((operands, self.ended))
        result = call(*operands)
        self.ended = result
        return result

    def settle(self, value):
        return self(lambda come: come, value)


def run(body, operands, outs, grid=(), in_specs=None, out_specs=None, scratch=()):
    whole = pl.BlockSpec(memory_space=pltpu.VMEM)
    return pl.pallas_call(
        body,
        out_shape=[jax.ShapeDtypeStruct(shape, kind) for shape, kind in outs],
        grid=grid,
        in_specs=in_specs or [whole] * len(operands),
        out_specs=out_specs or [whole] * len(outs),
        scratch_shapes=scratch,
        compiler_params=pltpu.CompilerParams(vmem_limit_bytes=12 * 2**20),
        cost_estimate=pl.CostEstimate(flops=30 * 10**9, bytes_accessed=1000, transcendentals=0),
    )(*operands)


def fixed(shape):
    return pl.BlockSpec(shape, lambda j: (0,) * len(shape))


def mm(first, second):
    return lax.dot_general(first, second, (((1,), (0,)), ((), ())), preferred_element_type=F32)


def mm_turned(first, second):
    return lax.dot_general(first, second, (((1,), (1,)), ((), ())), preferred_element_type=F32)


def mm_rows(first, second):
    return lax.dot_general(first, second, (((0,), (0,)), ((), ())), preferred_element_type=F32)


def pieces(values, count=3):
    out = []
    for _ in range(count):
        piece = values.astype(BF16)
        out.append(piece)
        values = values - piece.astype(F32)
    return out


def normalized(values):
    centered = values - jnp.mean(values, -1, keepdims=True)
    scale = lax.rsqrt(jnp.mean(centered * centered, -1, keepdims=True) + norm_epsilon)
    return centered * scale, scale


def norm_back(grad, values, gain):
    unit, scale = normalized(values)
    inner = grad * gain
    d_values = scale * (
        inner
        - jnp.mean(inner, -1, keepdims=True)
        - unit * jnp.mean(inner * unit, -1, keepdims=True)
    )
    return (
        d_values,
        jnp.sum(grad * unit, 0, keepdims=True),
        jnp.sum(grad, 0, keepdims=True),
    )


def first_norm(inputs, mine, other, to_relative):
    rows, width = inputs.shape
    half = width // 2

    def body(
        x_ref, mine_ref, other_ref, turn_ref, low_ref, high_ref, lowt_ref, hight_ref, rel_ref, true_ref
    ):
        turned = jnp.concatenate(
            [mine_ref[...].astype(F32).T, other_ref[...].astype(F32).T], 1
        )[:16]
        rel_ref[...] = turned
        true_ref[...] = mm_turned(turned.astype(BF16), turn_ref[...])
        unit, _ = normalized(x_ref[...].astype(F32))
        normed = (unit * turned[0:1] + turned[1:2]).astype(BF16)
        low_ref[...] = normed[:, :half]
        high_ref[...] = normed[:, half:]
        lowt_ref[...] = normed[:, :half].T
        hight_ref[...] = normed[:, half:].T

    vectors_at = mine.shape[1] // PAIR - 1
    weights = pl.BlockSpec((half, PAIR), lambda j: (0, vectors_at))
    return run(
        body,
        (inputs, mine, other, to_relative),
        [((rows, half), BF16)] * 2 + [((half, rows), BF16)] * 2 + [((16, width), F32)] * 2,
        (1,),
        [fixed(inputs.shape), weights, weights, fixed(to_relative.shape)],
        [fixed((rows, half))] * 2 + [fixed((half, rows))] * 2 + [fixed((16, width))] * 2,
    )


def project(at, low, high, mine, other, true_vectors):
    rows, half = low.shape

    def body(low_ref, high_ref, mine_ref, other_ref, vec_ref, out_ref):
        j = pl.program_id(0)
        bias = jnp.where(j == 0, vec_ref[4:5, :], jnp.where(j == 2, vec_ref[5:6, :], 0.0))
        value = mm(low_ref[...], mine_ref[...]) + mm(high_ref[...], other_ref[...])
        out_ref[0] = (value + bias).astype(BF16)

    weights = pl.BlockSpec((half, TILE), lambda j: (0, j))
    return run(
        body,
        (low, high, mine, other, true_vectors),
        [((3, rows, TILE), BF16)],
        (3,),
        [fixed(low.shape)] * 2 + [weights] * 2 + [pl.BlockSpec((16, TILE), lambda j: (0, at))],
        [pl.BlockSpec((1, rows, TILE), lambda j: (j, 0, 0))],
    )[0]


def head_mask(rows, side):
    lane = lax.broadcasted_iota(jnp.int32, (rows, PAIR), 1)
    return lane < PAIR // 2 if side == 0 else lane >= PAIR // 2


def attend(projected, counts):
    _, rows, width = projected[0].shape
    steps = width // PAIR

    def body(count_ref, *refs):
        *ins, out_ref, peak_ref = refs
        j = pl.program_id(0)

        def heads(q_ref, k_ref, v_ref):
            count = count_ref[0]
            key_ok = lax.broadcasted_iota(jnp.int32, (rows, rows), 1) < count
            row_ok = lax.broadcasted_iota(jnp.int32, (rows, 1), 0) < count
            queries = q_ref[0]
            out = None
            for side in (0, 1):
                chosen = head_mask(rows, side)
                scores = mm_turned(jnp.where(chosen, queries, 0), k_ref[0]) * (PAIR // 2) ** -0.5
                scores = jnp.where(key_ok, scores, masked_value)
                top = jnp.max(scores, -1, keepdims=True)
                peak = jnp.max(jnp.where(row_ok, top, masked_value))
                peak_ref[pl.ds(j * 2 + side, 1), :] = jnp.full((1, PAIR), peak)
                exponent = jnp.exp(scores - top)
                probs = exponent * (1.0 / jnp.sum(exponent, -1, keepdims=True))
                value = mm(probs.astype(BF16), v_ref[0])
                out = value if side == 0 else jnp.where(chosen, value, out)
            out_ref[...] = out.astype(BF16)

        @pl.when(j < steps)
        def _():
            heads(*ins[:3])

        @pl.when(j >= steps)
        def _():
            heads(*ins[3:])

    def part(index, at):
        return pl.BlockSpec(
            (1, rows, PAIR), lambda j: (index, 0, jnp.clip(j - at * steps, 0, steps - 1))
        )

    return run(
        body,
        (counts, *[projected[0]] * 3, *[projected[1]] * 3),
        [((rows, 2 * width), BF16), ((4 * steps, PAIR), F32)],
        (2 * steps,),
        [pl.BlockSpec(memory_space=pltpu.SMEM)]
        + [part(index, at) for at in (0, 1) for index in range(3)],
        [pl.BlockSpec((rows, PAIR), lambda j: (0, j)), fixed((4 * steps, PAIR))],
    )


def attend_back(projected, d_out, counts):
    _, rows, width = projected.shape
    steps = width // PAIR
    scale = (PAIR // 2) ** -0.5

    def body(count_ref, q_ref, k_ref, v_ref, d_ref, out_ref, sum_ref):
        key_ok = lax.broadcasted_iota(jnp.int32, (rows, rows), 0) < count_ref[0]
        queries, keys, values, grad = q_ref[0], k_ref[0], v_ref[0], d_ref[...]
        parts = [None] * 3
        for side in (0, 1):
            chosen = head_mask(rows, side)
            scores = mm_turned(jnp.where(chosen, keys, 0), queries) * scale
            scores = jnp.where(key_ok, scores, masked_value)
            exponent = jnp.exp(scores - jnp.max(scores, 0, keepdims=True))
            probs = exponent * (1.0 / jnp.sum(exponent, 0, keepdims=True))
            d_probs = mm_turned(jnp.where(chosen, values, 0), grad)
            inner = jnp.sum(probs * d_probs, 0, keepdims=True)
            d_scores = (probs * (d_probs - inner)).astype(BF16)
            new = [
                mm_rows(d_scores, keys) * scale,
                mm(d_scores, queries) * scale,
                mm(probs.astype(BF16), grad),
            ]
            parts = new if side == 0 else [jnp.where(chosen, n, p) for n, p in zip(new, parts)]
        low = [part.astype(BF16) for part in parts]
        for at in range(3):
            out_ref[at] = low[at]
        sum_ref[0:1, :] = jnp.sum(low[0].astype(F32), 0, keepdims=True)
        sum_ref[1:2, :] = jnp.sum(low[2].astype(F32), 0, keepdims=True)

    def part(index):
        return pl.BlockSpec((1, rows, PAIR), lambda j: (index, 0, j))

    columns = pl.BlockSpec((rows, PAIR), lambda j: (0, j))
    return run(
        body,
        (counts, projected, projected, projected, d_out),
        [((3, rows, width), BF16), ((8, width), F32)],
        (steps,),
        [pl.BlockSpec(memory_space=pltpu.SMEM), part(0), part(1), part(2), columns],
        [
            pl.BlockSpec((3, rows, PAIR), lambda j: (0, 0, j)),
            pl.BlockSpec((8, PAIR), lambda j: (0, j)),
        ],
    )


def second_norm(inputs, attended, weights, vectors):
    rows, width = inputs.shape
    half = width // 2

    def body(x_ref, a_ref, b_ref, wa_ref, wa2_ref, wb_ref, wb2_ref, vec_ref, mid_ref, low_ref, high_ref, lowt_ref, hight_ref):
        first, second = a_ref[...], b_ref[...]
        branch = jnp.concatenate(
            [
                mm_turned(first, wa_ref[...]) + mm_turned(second, wb_ref[...]),
                mm_turned(first, wa2_ref[...]) + mm_turned(second, wb2_ref[...]),
            ],
            1,
        )
        middle = x_ref[...].astype(F32) + branch + vec_ref[6:7, :]
        mid_ref[...] = middle
        unit, _ = normalized(middle)
        normed = (unit * vec_ref[2:3, :] + vec_ref[3:4, :]).astype(BF16)
        low_ref[...] = normed[:, :half]
        high_ref[...] = normed[:, half:]
        lowt_ref[...] = normed[:, :half].T
        hight_ref[...] = normed[:, half:].T

    block = pl.BlockSpec((half, TILE), lambda j: (0, 0))
    return run(
        body,
        (inputs, attended, attended, *weights[0], *weights[1], vectors),
        [((rows, width), F32)] + [((rows, half), BF16)] * 2 + [((half, rows), BF16)] * 2,
        (1,),
        [fixed(inputs.shape)]
        + [pl.BlockSpec((rows, TILE), lambda j, at=at: (0, at)) for at in (0, 1)]
        + [block] * 4
        + [fixed(vectors.shape)],
        [fixed((rows, width))] + [fixed((rows, half))] * 2 + [fixed((half, rows))] * 2,
    )


def expand(at, low, high, mine, other, true_vectors):
    rows, half = low.shape
    count = mine.shape[1] - TILE
    per_row = true_vectors.shape[1] // TILE
    first_row = 8 + at * count // true_vectors.shape[1]

    def body(low_ref, high_ref, mine_ref, other_ref, vec_ref, out_ref, slope_ref):
        row = first_row + pl.program_id(0) // per_row
        pre = mm(low_ref[...], mine_ref[...]) + mm(high_ref[...], other_ref[...])
        pre = pre + vec_ref[pl.ds(row, 1), :]
        below = 0.5 * (1.0 + lax.erf(pre * HALF_ROOT))
        out_ref[...] = (pre * below).astype(BF16)
        slope = below + pre * (DENSITY * jnp.exp(-0.5 * pre * pre))
        slope_ref[...] = slope.astype(BF16)

    weights = pl.BlockSpec((half, TILE), lambda j: (0, j + 1))
    columns = pl.BlockSpec((rows, TILE), lambda j: (0, j))
    return run(
        body,
        (low, high, mine, other, true_vectors),
        [((rows, count), BF16)] * 2,
        (count // TILE,),
        [fixed(low.shape)] * 2
        + [weights] * 2
        + [pl.BlockSpec((16, TILE), lambda j: (0, j % per_row))],
        [columns, columns],
    )


def expand_back(low, high, first, second, slopes):
    rows, half = low.shape
    count = slopes[0].shape[1]
    steps = count // TILE

    def body(
        low_ref, high_ref, wa_ref, wa2_ref, wb_ref, wb2_ref, sa_ref, sb_ref, out_ref, sum_ref
    ):
        def part(mine_ref, other_ref, slope_ref):
            value = mm(low_ref[...], mine_ref[...]) + mm(high_ref[...], other_ref[...])
            value = (value * slope_ref[...].astype(F32)).astype(BF16)
            out_ref[...] = value
            sum_ref[...] = jnp.sum(value.astype(F32), 0, keepdims=True)

        @pl.when(pl.program_id(0) < steps)
        def _():
            part(wa_ref, wa2_ref, sa_ref)

        @pl.when(pl.program_id(0) >= steps)
        def _():
            part(wb_ref, wb2_ref, sb_ref)

    def before(shape):
        return pl.BlockSpec(shape, lambda j: (0, jnp.minimum(j, steps - 1)))

    def behind(shape):
        return pl.BlockSpec(shape, lambda j: (0, jnp.maximum(j - steps, 0)))

    return run(
        body,
        (low, high, *first, *second, *slopes),
        [((rows, 2 * count), BF16), ((1, 2 * count), F32)],
        (2 * steps,),
        [fixed(low.shape)] * 2
        + [before((half, TILE))] * 2
        + [behind((half, TILE))] * 2
        + [before((rows, TILE)), behind((rows, TILE))],
        [pl.BlockSpec((rows, TILE), lambda j: (0, j)), pl.BlockSpec((1, TILE), lambda j: (0, j))],
    )


def contract_first(d_pre, mine, other):
    rows, count = d_pre.shape
    half = mine.shape[0]
    count = count // 2

    def body(d_ref, mine_ref, other_ref, out_ref):
        @pl.when(pl.program_id(0) == 0)
        def _():
            out_ref[...] = jnp.zeros_like(out_ref)

        out_ref[:, :half] += mm_turned(d_ref[...], mine_ref[...])
        out_ref[:, half:] += mm_turned(d_ref[...], other_ref[...])

    weights = pl.BlockSpec((half, TILE), lambda j: (0, j + 1))
    return run(
        body,
        (d_pre, mine, other),
        [((rows, 2 * half), F32)],
        (count // TILE,),
        [pl.BlockSpec((rows, TILE), lambda j: (0, j)), weights, weights],
        [fixed((rows, 2 * half))],
    )[0]


def contract_second(d_pre, weights, partial_sum, middle, d_result, vectors):
    rows, count = d_pre.shape
    half = weights[0][0].shape[0]
    width = 2 * half
    steps = count // 2 // TILE

    def body(
        d_ref, mine_ref, other_ref, wa_ref, wa2_ref, wb_ref, wb2_ref, sum_ref, mid_ref, res_ref,
        vec_ref, dm_ref, low_ref, high_ref, outa_ref, outb_ref, grads_ref, total,
    ):
        j = pl.program_id(0)

        @pl.when(j == 0)
        def _():
            total[...] = sum_ref[...]

        total[:, :half] += mm_turned(d_ref[...], mine_ref[...])
        total[:, half:] += mm_turned(d_ref[...], other_ref[...])

        @pl.when(j == steps - 1)
        def _():
            d_values, d_gain, d_shift = norm_back(total[...], mid_ref[...], vec_ref[2:3, :])
            result_grad = res_ref[...].astype(F32)
            d_middle = result_grad + d_values
            branch = d_middle.astype(BF16)
            dm_ref[...] = d_middle
            first, second = branch[:, :half], branch[:, half:]
            low_ref[...] = first.T
            high_ref[...] = second.T
            outa_ref[...] = (mm(first, wa_ref[...]) + mm(second, wa2_ref[...])).astype(BF16)
            outb_ref[...] = (mm(first, wb_ref[...]) + mm(second, wb2_ref[...])).astype(BF16)
            grads_ref[0:1, :] = d_gain
            grads_ref[1:2, :] = d_shift
            grads_ref[2:3, :] = jnp.sum(branch.astype(F32), 0, keepdims=True)
            grads_ref[3:4, :] = jnp.sum(result_grad, 0, keepdims=True)

    tile = pl.BlockSpec((half, TILE), lambda j: (0, j + 1))
    block = pl.BlockSpec((half, TILE), lambda j: (0, 0))
    return run(
        body,
        (d_pre, *weights[1], *weights[0], *weights[1], partial_sum, middle, d_result, vectors),
        [((rows, width), F32)]
        + [((half, rows), BF16)] * 2
        + [((rows, TILE), BF16)] * 2
        + [((8, width), F32)],
        (steps,),
        [pl.BlockSpec((rows, TILE), lambda j: (0, steps + j)), tile, tile]
        + [block] * 4
        + [fixed((rows, width))] * 3
        + [fixed(vectors.shape)],
        [fixed((rows, width))]
        + [fixed((half, rows))] * 2
        + [fixed((rows, TILE))] * 2
        + [fixed((8, width))],
        [pltpu.VMEM((rows, width), F32)],
    )


def input_back_first(d_projected, mine, other):
    rows = d_projected.shape[1]
    half = mine.shape[0]

    def body(d_ref, mine_ref, other_ref, out_ref):
        @pl.when(pl.program_id(0) == 0)
        def _():
            out_ref[...] = jnp.zeros_like(out_ref)

        out_ref[:, :half] += mm_turned(d_ref[0], mine_ref[...])
        out_ref[:, half:] += mm_turned(d_ref[0], other_ref[...])

    weights = pl.BlockSpec((half, TILE), lambda j: (0, j))
    return run(
        body,
        (d_projected, mine, other),
        [((rows, 2 * half), F32)],
        (3,),
        [pl.BlockSpec((1, rows, TILE), lambda j: (j, 0, 0)), weights, weights],
        [fixed((rows, 2 * half))],
    )[0]


def input_back_second(
    d_projected, mine, other, partial_sum, inputs, d_middle, grads, head_sums, d_pre_sums, vectors, to_relative
):
    rows = d_projected.shape[1]
    half = mine.shape[0]
    width = 2 * half

    def body(
        d_ref, mine_ref, other_ref, sum_ref, x_ref, dm_ref, grads_ref, heada_ref, headb_ref, pre_ref,
        vec_ref, turn_ref, out_ref, low_ref, high_ref, total, true_rows, all_rows,
    ):
        j = pl.program_id(0)

        @pl.when(j == 0)
        def _():
            total[...] = sum_ref[...]

        total[:, :half] += mm_turned(d_ref[0], mine_ref[...])
        total[:, half:] += mm_turned(d_ref[0], other_ref[...])

        @pl.when(j == 2)
        def _():
            d_values, d_gain, d_shift = norm_back(total[...], x_ref[...].astype(F32), vec_ref[0:1, :])
            low = (dm_ref[...] + d_values).astype(BF16)
            out_ref[...] = mm_turned(low, turn_ref[...]).astype(BF16)
            true_rows[...] = jnp.zeros_like(true_rows)
            for at, ref in enumerate((heada_ref, headb_ref)):
                true_rows[0:2, at * TILE : (at + 1) * TILE] = ref[0:2, :]
            for part in range(pre_ref.shape[1] // width):
                row = 2 + part
                true_rows[row : row + 1, :] = pre_ref[:, part * width : (part + 1) * width]
            turned = sum(mm(part, turn_ref[...]) for part in pieces(true_rows[...]))
            all_rows[...] = jnp.zeros_like(all_rows)
            all_rows[0:1, :] = d_gain
            all_rows[1:2, :] = d_shift
            all_rows[2:4, :] = grads_ref[0:2, :]
            all_rows[4:6, :] = turned[0:2]
            all_rows[6:8, :] = grads_ref[2:4, :]
            all_rows[8:14, :] = turned[2:8]
            columns = all_rows[...].T
            low_ref[...] = columns[:half]
            high_ref[...] = columns[half:]

    weights = pl.BlockSpec((half, TILE), lambda j: (0, j))
    operands = (
        d_projected,
        mine,
        other,
        partial_sum,
        inputs,
        d_middle,
        grads,
        *head_sums,
        d_pre_sums,
        vectors,
        to_relative,
    )
    return run(
        body,
        operands,
        [((rows, width), BF16)] + [((half, PAIR), F32)] * 2,
        (3,),
        [pl.BlockSpec((1, rows, TILE), lambda j: (j, 0, 0)), weights, weights]
        + [fixed(operand.shape) for operand in operands[3:]],
        [fixed((rows, width))] + [fixed((half, PAIR))] * 2,
        [pltpu.VMEM((rows, width), F32), pltpu.VMEM((8, width), F32), pltpu.VMEM((PAIR, width), F32)],
    )


def finish(middle, hidden, weights, vectors, to_relative, counts):
    rows, width = middle.shape
    half = width // 2
    steps = hidden[0].shape[1] // TILE

    def body(
        count_ref, a_ref, b_ref, wa_ref, wa2_ref, wb_ref, wb2_ref, mid_ref, vec_ref, turn_ref, out_ref, total
    ):
        j = pl.program_id(0)

        @pl.when(j == 0)
        def _():
            total[...] = mid_ref[...] + vec_ref[7:8, :]

        first, second = a_ref[...], b_ref[...]
        total[:, :half] += mm_turned(first, wa_ref[...]) + mm_turned(second, wb_ref[...])
        total[:, half:] += mm_turned(first, wa2_ref[...]) + mm_turned(second, wb2_ref[...])

        @pl.when(j == steps - 1)
        def _():
            kept = lax.broadcasted_iota(jnp.int32, (rows, 1), 0) < count_ref[0]
            low = jnp.where(kept, total[...], 0.0).astype(BF16)
            out_ref[...] = mm_turned(low, turn_ref[...]).astype(BF16)

    columns = pl.BlockSpec((rows, TILE), lambda j: (0, j))
    tile = pl.BlockSpec((half, TILE), lambda j: (0, j))
    return run(
        body,
        (counts, *hidden, *weights[0], *weights[1], middle, vectors, to_relative),
        [((rows, width), BF16)],
        (steps,),
        [pl.BlockSpec(memory_space=pltpu.SMEM), columns, columns]
        + [tile] * 4
        + [fixed((rows, width)), fixed(vectors.shape), fixed(to_relative.shape)],
        [fixed((rows, width))],
        [pltpu.VMEM((rows, width), F32)],
    )[0]


def product(slowest, tiles):
    count, rows = tiles[0][0].shape
    operands, specs = [], []
    for *both, width, place in tiles:
        operands += both
        specs += [fixed((count, rows))] * 2
        shape = (1,) * (len(place) - 2) + (rows, width)
        specs += [pl.BlockSpec(shape, lambda j, place=place: place)] * 2

    def body(*refs):
        *ins, sent_ref, kept_ref = refs
        first = 0
        for at, tile in enumerate(tiles):
            left, left_other, right, right_other = (
                ref[0] if len(ref.shape) == 3 else ref[...] for ref in ins[4 * at : 4 * at + 4]
            )
            value = (mm(left, right) + mm(left_other, right_other)).astype(BF16)
            columns = slice(first, first + tile[4])
            first += tile[4]
            cut_rows(value, slowest, sent_ref, kept_ref, columns)

    out = (count // 2, sum(tile[4] for tile in tiles))
    return run(body, operands, [(out, BF16)] * 2, (1,), specs, [fixed(out)] * 2)


def cut_rows(value, slowest, sent_ref, kept_ref, columns):
    part = value.shape[0] // 2 // slowest
    for group in range(slowest):
        low = 2 * group * part
        rows = slice(group * part, (group + 1) * part)
        kept_ref[rows, columns] = value[low : low + part]
        sent_ref[rows, columns] = value[low + part : low + 2 * part]


def vector_rows_cut(slowest, mine, other):
    def body(mine_ref, other_ref, sent_ref, kept_ref):
        value = (mine_ref[...] + other_ref[...]).astype(BF16)
        cut_rows(value, slowest, sent_ref, kept_ref, slice(None))

    return run(body, (mine, other), [((mine.shape[0] // 2, mine.shape[1]), BF16)] * 2)


def product_wide(slowest, first, width, left, left_other, right, right_other):
    rows = right.shape[0]
    count = left.shape[0]

    def body(left_ref, left_other_ref, right_ref, right_other_ref, sent_ref, kept_ref):
        value = mm(left_ref[...], right_ref[...]) + mm(left_other_ref[...], right_other_ref[...])
        cut_rows(value.astype(BF16), slowest, sent_ref, kept_ref, slice(None))

    columns = pl.BlockSpec((rows, TILE), lambda j: (0, first // TILE + j))
    out_columns = pl.BlockSpec((count // 2, TILE), lambda j: (0, j))
    return run(
        body,
        (left, left_other, right, right_other),
        [((count // 2, width), BF16)] * 2,
        (width // TILE,),
        [fixed(left.shape)] * 2 + [columns] * 2,
        [out_columns] * 2,
    )


def added(first, second, kind=BF16):
    return (first.astype(F32) + second.astype(F32)).astype(kind)


def halved(pairs, joined):
    half = pairs[0][0].shape[0] // 2
    widths = [mine.shape[1] for mine, _ in pairs]
    if half % 16:
        totals = [added(*pair) for pair in pairs]
        if joined:
            totals = [jnp.concatenate(totals, 1)]
        return [(total[half:], total[:half]) for total in totals]

    def body(*refs):
        ins, outs = refs[: 2 * len(pairs)], refs[2 * len(pairs) :]
        for at in range(len(pairs)):
            mine, got = ins[2 * at], ins[2 * at + 1]
            sent_ref, kept_ref = outs[:2] if joined else outs[2 * at : 2 * at + 2]
            first = sum(widths[:at]) if joined else 0
            columns = slice(first, first + widths[at])
            sent_ref[:, columns] = added(mine[half:, :], got[half:, :])
            kept_ref[:, columns] = added(mine[:half, :], got[:half, :])

    out_widths = [sum(widths)] if joined else widths
    outs = [((half, width), BF16) for width in out_widths for _ in range(2)]
    outs = run(body, [v for pair in pairs for v in pair], outs)
    return [tuple(outs[at : at + 2]) for at in range(0, len(outs), 2)]


def joined(places, middle, count, mine, got):
    wide = mine[0].shape[-1] if len(mine) == 1 else sum(value.shape[-1] for value in mine)
    parts = (slice(0, middle), slice(middle, wide))
    pairs = list(zip(places, mine, got))
    shapes = [(*value.shape[:at], 2, *value.shape[at:]) for at, value, _ in pairs]

    def widths(shape):
        if count == 1:
            return [(*shape[:-1], wide)]
        return [(*shape[:-1], part.stop - part.start) for part in parts]

    out_shapes = shapes if len(mine) == count else widths(shapes[0])
    if mine[0].shape[-2] % 16:
        both = [jnp.stack([value, come], at) for at, value, come in pairs]
        if len(mine) == count:
            return both
        if count == 1:
            rest = both[0].shape[:-1]
            return [jnp.concatenate([value.reshape(*rest, -1) for value in both], -1)]
        return [both[0][..., part] for part in parts]

    def body(*refs):
        outs = refs[2 * len(mine) :]
        for at, (place, value, _) in enumerate(pairs):
            for side in (0, 1):
                ref = refs[at + side * len(mine)]
                lead = (slice(None),) * place + (side,) + (slice(None),) * (value.ndim - 1 - place)
                if len(mine) == count:
                    outs[at][(*lead, slice(None))] = ref[...]
                elif count == 1:
                    outs[0][(*lead, parts[at])] = ref[...]
                else:
                    for out_ref, part in zip(outs, parts):
                        out_ref[(*lead, slice(None))] = ref[..., part]

    outs = [(shape, BF16) for shape in out_shapes]
    dims = mine[0].ndim - 2
    if dims < 3:
        return run(body, [*mine, *got], outs)
    def in_spec(shape):
        return pl.BlockSpec((1, 1, *shape[2:]), lambda i, j: (i, j) + (0,) * (len(shape) - 2))

    def out_spec(shape, place):
        block, at = [1, 1, *shape[3:]], lambda i, j: [i, j] + [0] * (len(shape) - 3)
        return pl.BlockSpec(
            (*block[:place], 2, *block[place:]),
            lambda i, j: (*at(i, j)[:place], 0, *at(i, j)[place:]),
        )

    return run(
        body,
        [*mine, *got],
        outs,
        mine[0].shape[:2],
        [in_spec(value.shape) for value in [*mine, *got]],
        [out_spec(shape, places[at if len(mine) == count else 0]) for at, shape in enumerate(out_shapes)],
    )


class Sum:
    def __init__(self, links, firsts):
        self.links = links
        self.left, self.pairs = [], []
        self.z_left = links.z_bits
        for parts, order in zip(firsts, links.orders):
            self.add(parts, order)

    def add(self, parts, order):
        sent, kept = parts
        self.left.append(order[1:])
        self.pairs.append((kept, self.links.exchange(sent, order[0])))

    def step(self, order):
        inner = bool(self.left[0])
        joined = not inner and len(self.pairs) > 1
        parts = order(partial(halved, joined=joined), self.pairs)
        if inner:
            bits = [left[0] for left in self.left]
            self.left = [left[1:] for left in self.left]
        else:
            bits = [self.z_left[0]]
            self.z_left = self.z_left[1:]
        self.pairs = [
            (kept, self.links.exchange(sent, bit)) for (sent, kept), bit in zip(parts, bits)
        ]

    def settle(self, order):
        self.pairs = [(kept, order.settle(got)) for kept, got in self.pairs]

    def total(self):
        return added(*self.pairs[0], F32)


class Gather:
    def __init__(self, links, shards, middle):
        self.links, self.middle = links, middle
        steps = [tuple(reversed(order)) for order in links.orders]
        steps = list(zip(*steps))
        between = len(steps) // 2 if len(shards) == 2 else 0
        z_steps = [(bit,) for bit in reversed(links.z_bits)]
        self.steps = steps[:between] + z_steps + steps[between:] + [("c", "c")]
        self.blocks = list(shards)
        self.bits = [(), ()]
        self.send()

    def send(self):
        self.got = [
            self.links.exchange(block, bit) for block, bit in zip(self.blocks, self.steps[0])
        ]

    def join(self, order):
        done, *self.steps = self.steps
        bits = done * 2 if len(done) == 1 else done
        places = []
        for at, bit in enumerate(bits):
            held = sorted((*self.bits[at], bit), key=self.links.bits.index)
            self.bits[at] = tuple(held)
            places.append(held.index(bit))
        self.blocks = order(
            partial(joined, places, self.middle, len(self.steps[0])), self.blocks, self.got
        )
        if self.steps[0][0] == "c":
            self.blocks = [block.reshape(-1, block.shape[-1]) for block in self.blocks]

    def step(self, order):
        self.join(order)
        self.send()

    def settle(self, order):
        self.got = order.settle(self.got)

    def halves(self):
        return list(zip(self.blocks, self.got))


def last_update(late, last, spans, scale, moments, vector_scale, vector_moments):
    spans, vectors_at = spans
    rows, width = moments[0].shape
    count = vector_moments[0].shape[0]

    def body(*refs):
        late_kept, late_got, last_kept, last_got, scale_ref = refs[:5]
        weight_ref, mean_ref, square_ref, vscale_ref, vector_ref, vmean_ref, vsquare_ref = refs[5:12]
        outs = refs[12:]
        sums = [added(late_kept[...], late_got[...], F32), added(last_kept[...], last_got[...], F32)]
        for of_last, first, place, size in spans:
            columns = slice(place, place + size)
            mean, square, stepped = adam_step(
                weight_ref[:, columns],
                sums[of_last][:, first : first + size],
                mean_ref[:, columns],
                square_ref[:, columns],
                matrix_rate,
                weight_decay,
            )
            outs[0][:, columns] = mean
            outs[1][:, columns] = square
            outs[2][:, columns] = stepped * scale_ref[:, columns]
        grads = sums[1][:, vectors_at : vectors_at + PAIR].T[:count]
        mean, square, stepped = adam_step(
            vector_ref[...], grads, vmean_ref[...], vsquare_ref[...], vector_rate, 0.0
        )
        outs[3][...] = mean
        outs[4][...] = square
        row = lax.broadcasted_iota(jnp.int32, stepped.shape, 0)
        outs[5][...] = jnp.where(row == 4, stepped * vscale_ref[...], stepped)

    return run(
        body,
        (*late, *last, scale, *moments, vector_scale, *vector_moments),
        [((rows, width), F32)] * 3 + [(vector_moments[0].shape, F32)] * 3,
    )


def local(
    links,
    tokens,
    cotangent,
    counts,
    w_qkv,
    w_out,
    w_up,
    w_down,
    vectors,
    mean_qkv,
    mean_out,
    mean_up,
    mean_down,
    mean_vectors,
    square_qkv,
    square_out,
    square_up,
    square_down,
    square_vectors,
):
    seq_count, slot_count, model_width = tokens.shape
    rows = seq_count * slot_count
    head_width = model_width // H
    wide = w_down.shape[0]
    vector_count, shard_width = vectors.shape
    half = model_width // 2
    order = Order()

    low_qkv = w_qkv.astype(BF16)
    thirds = [low_qkv[:, at * half : (at + 1) * half] for at in range(6)]
    shard_vectors = jnp.pad(vectors.astype(BF16).T, ((0, 0), (0, PAIR - vector_count)))
    shard_qkv = jnp.concatenate([*thirds[0::2], shard_vectors, *thirds[1::2]], 1)
    low_out, low_up = w_out.astype(BF16).T, w_up.astype(BF16)
    shard_up = jnp.concatenate(
        [low_out[:, :half], low_up[:, : wide // 2], low_out[:, half:], low_up[:, wide // 2 :]], 1
    )
    shard_down = w_down.astype(BF16).T
    gather_qkv = Gather(links, [shard_qkv], 3 * half + PAIR)
    gather_down = Gather(
        links, [shard_down[:, : wide // 2], shard_down[:, wide // 2 :]], wide // 2
    )

    true_rows = (
        links.true_block()[:, None] * shard_width + jnp.arange(shard_width, dtype=jnp.int32)
    ).reshape(1, model_width)
    to_relative = (
        lax.broadcasted_iota(jnp.int32, (model_width, model_width), 0) == true_rows
    ).astype(BF16)
    keep_rows = lax.broadcasted_iota(jnp.int32, (rows, 1), 0) < counts[0]
    d_result = jnp.where(keep_rows, cotangent.reshape(rows, model_width), 0).astype(BF16)
    inputs = mm(tokens.reshape(rows, model_width), to_relative).astype(BF16)
    d_result_turned = mm(d_result, to_relative).astype(BF16)
    d_columns = lax.dot_general(
        to_relative, d_result, (((0,), (1,)), ((), ())), preferred_element_type=F32
    ).astype(BF16)

    def longer(gather, count):
        while len(gather.steps) > count:
            gather.step(order)

    inputs, d_result_turned, d_columns, to_relative = order.settle(
        (inputs, d_result_turned, d_columns, to_relative)
    )
    d_low, d_high = d_result_turned[:, :half], d_result_turned[:, half:]
    longer(gather_qkv, 5)
    gather_qkv.step(order)
    gather_down.settle(order)
    d_other = order.settle(links.exchange(d_columns[half:], "c"))
    d_mine = d_columns[:half]
    gather_qkv.step(order)
    gather_up = Gather(
        links, [order(lambda values: values + 0, shard_up)], half + wide // 2
    )
    gather_qkv.step(order)
    longer(gather_up, 5)
    gather_up.step(order)
    gather_qkv.step(order)
    gather_up.step(order)
    longer(gather_down, 5)
    gather_down.step(order)
    halves_qkv = gather_qkv.halves()
    normed_low, normed_high, normed_mine, normed_send, vector_rows, true_vectors = order(
        first_norm, inputs, *halves_qkv[0], to_relative
    )
    normed_other = links.exchange(normed_send, "c")
    projected = [
        order(partial(project, at), normed_low, normed_high, *halves_qkv[at], true_vectors)
        for at in (0, 1)
    ]
    normed_other = order.settle(normed_other)
    gather_up.step(order)
    shared, peak = order(attend, projected, counts)
    gather_down.step(order)
    shared_other = links.exchange(shared, "c")
    peak, peak_got = [peak], []

    def peak_send(bit):
        sent = order.settle(peak[0])
        peak_got.append(links.exchange(sent, bit))

    def peak_take():
        peak[0] = order(jnp.maximum, peak[0], peak_got.pop())

    first_bit, *more_bits = links.bits
    peak_send(first_bit)
    peak_take()
    for bit in more_bits[4:]:
        peak_send(bit)
        peak_take()
    peak_send(more_bits[0])
    gather_up.step(order)
    shared_other = order.settle(shared_other)
    peak_take()
    peak_send(more_bits[1])
    peak_take()
    peak_send(more_bits[2])
    gather_down.step(order)
    peak_take()
    peak_send(more_bits[3])
    halves_up = gather_up.halves()
    middle, normed_two_low, normed_two_high, normed_two_mine, normed_two_send = order(
        second_norm, inputs, shared, halves_up, vector_rows
    )
    peak_take()
    normed_two_other = links.exchange(normed_two_send, "c")
    hidden, slope, hidden_other = [], [], []
    for at in (0, 1):
        out, out_slope = order(
            partial(expand, at), normed_two_low, normed_two_high, *halves_up[at], true_vectors
        )
        hidden.append(out)
        slope.append(out_slope)
        hidden_other.append(links.exchange(out, "c"))
        if at == 0:
            normed_two_other = order.settle(normed_two_other)
    slowest = [1, 2 ** len(links.y_bits)]

    down_parts = [
        order(
            partial(product_wide, slowest[at], 0, wide // 2),
            d_mine,
            d_other,
            hidden[at],
            hidden_other[at],
        )
        for at in (0, 1)
    ]
    gather_down.step(order)
    sum_down = Sum(links, order.settle(down_parts))
    halves_down = gather_down.halves()
    d_pre, d_pre_sums = order(expand_back, d_low, d_high, *halves_down, slope)
    d_pre_other = links.exchange(d_pre, "c")
    partial_sum = order(contract_first, d_pre, *halves_up[0])
    result = order(finish, middle, hidden, halves_down, vector_rows, to_relative, counts)
    result_out = result.reshape(seq_count, slot_count, model_width)
    for _ in links.orders[0][1:]:
        sum_down.step(order)
    sum_up = Sum(
        links,
        [
            order(
                partial(product_wide, slowest[at], at * wide // 2, wide // 2),
                normed_two_mine,
                normed_two_other,
                d_pre,
                d_pre_other,
            )
            for at in (0, 1)
        ],
    )
    d_middle, d_branch_low, d_branch_high, d_out_one, d_out_two, grads = order(
        contract_second, d_pre, halves_up, partial_sum, middle, d_result_turned, vector_rows
    )
    d_branch_other = links.exchange(d_branch_high, "c")
    sum_down.step(order)
    d_branch_other = order.settle(d_branch_other)
    d_projected, d_projected_other, head_sums = [], [], []
    for at, d_out in enumerate((d_out_one, d_out_two)):
        out, sums = order(attend_back, projected[at], d_out, counts)
        d_projected.append(out)
        d_projected_other.append(links.exchange(out, "c"))
        head_sums.append(sums)


    def out_tile(at):
        return (d_branch_low, d_branch_other, shared, shared_other, half, (0, at))

    def qkv_tile(at, part, width, column):
        return (
            normed_mine,
            normed_other,
            d_projected[at],
            d_projected_other[at],
            width,
            (part, 0, column),
        )

    def late_product(at, tiles):
        def call(*operands):
            return product(
                slowest[at],
                [(*operands[4 * i : 4 * i + 4], *tile[4:]) for i, tile in enumerate(tiles)],
            )

        return order(call, *[operand for tile in tiles for operand in tile[:4]])

    partial_sum = order(input_back_first, d_projected[0], *halves_qkv[0])
    for _ in links.z_bits[1:]:
        sum_down.step(order)
    for _ in links.orders[0][1:]:
        sum_up.step(order)
    d_projected_other = order.settle(d_projected_other)
    quarter = half // 2
    sum_late = Sum(
        links,
        [
            late_product(at, [out_tile(at), qkv_tile(0, at, half, 0), qkv_tile(0, 2, quarter, at)])
            for at in (0, 1)
        ],
    )
    last = [
        late_product(at, [qkv_tile(1, at, half, 0), qkv_tile(1, 2, quarter, at)]) for at in (0, 1)
    ]
    sum_down.settle(order)
    sum_up.step(order)
    sum_last = Sum(links, last)
    token_grad, vectors_low, vectors_high = order(
        input_back_second,
        d_projected[1],
        *halves_qkv[1],
        partial_sum,
        inputs,
        d_middle,
        grads,
        head_sums,
        d_pre_sums,
        vector_rows,
        to_relative,
    )
    token_grad = token_grad.reshape(seq_count, slot_count, model_width)
    for _ in links.orders[0][1:]:
        sum_late.step(order)
    vectors_other = order.settle(links.exchange(vectors_high, "c"))
    sum_last.add(
        order(partial(vector_rows_cut, slowest[1]), vectors_low, vectors_other), links.orders[1]
    )
    for _ in links.z_bits[1:]:
        sum_up.step(order)
    for _ in links.orders[0][1:]:
        sum_last.step(order)
    sum_late.step(order)
    sum_up.settle(order)
    sum_last.step(order)
    for _ in links.z_bits[1:]:
        sum_late.step(order)
    head_peak = order.settle(peak[0])[:, 0]
    vectors, mean_vectors, square_vectors, mean_down, first_col = order.settle(
        (
            vectors,
            mean_vectors,
            square_vectors,
            mean_down,
            lax.axis_index(("dp", "fsdp")) * shard_width,
        )
    )
    shrink = jnp.sqrt(clip_limit / jnp.maximum(head_peak, clip_limit))
    head_cols = jnp.repeat(shrink, head_width)
    qkv_scale = jnp.concatenate([head_cols, head_cols, jnp.ones((model_width,), F32)])[None]
    col_head = (first_col + jnp.arange(shard_width, dtype=jnp.int32)) // head_width
    col_shrink = jnp.sum(
        jnp.where(
            col_head[:, None] == jnp.arange(H, dtype=jnp.int32)[None, :], shrink[None, :], 0.0
        ),
        1,
    )[None]
    for _ in links.z_bits[1:]:
        sum_last.step(order)
    sum_late.settle(order)
    spans = (
        (0, half, 0, half),
        (1, 0, half, half),
        (0, half * 3 + quarter, 2 * half, half),
        (1, half + quarter, 3 * half, half),
        (0, 2 * half, 4 * half, quarter),
        (0, 4 * half + quarter, 4 * half + quarter, quarter),
        (1, half, 5 * half, quarter),
        (1, 2 * half + quarter, 5 * half + quarter, quarter),
    )
    vectors_at = 3 * half
    late = sum_late.total()
    reduced_out = jnp.concatenate([late[:, :half], late[:, 2 * half + quarter :][:, :half]], 1).T
    reduced_up = sum_up.total()
    reduced_down = sum_down.total().T
    mean_o, square_o, new_out = adam_step(
        w_out, reduced_out, mean_out, square_out, matrix_rate, weight_decay
    )
    mean_u, square_u, new_up = adam_step(
        w_up, reduced_up, mean_up, square_up, matrix_rate, weight_decay
    )
    mean_d, square_d, new_down = adam_step(
        w_down, reduced_down, mean_down, square_down, matrix_rate, weight_decay
    )
    if shard_width % 8 == 0:
        mean_q, square_q, new_qkv, mean_v, square_v, new_vectors = last_update(
            sum_late.pairs[0],
            sum_last.pairs[0],
            (spans, vectors_at),
            qkv_scale,
            (w_qkv, mean_qkv, square_qkv),
            col_shrink,
            (vectors, mean_vectors, square_vectors),
        )
    else:
        sums = (late, sum_last.total())
        reduced_qkv = jnp.concatenate(
            [sums[which][:, first : first + size] for which, first, _, size in spans], 1
        )
        mean_q, square_q, stepped_qkv = adam_step(
            w_qkv, reduced_qkv, mean_qkv, square_qkv, matrix_rate, weight_decay
        )
        new_qkv = stepped_qkv * qkv_scale
        reduced_vectors = sums[1][:, vectors_at : vectors_at + vector_count].T
        mean_v, square_v, stepped_vectors = adam_step(
            vectors, reduced_vectors, mean_vectors, square_vectors, vector_rate, 0.0
        )
        row_pick = (jnp.arange(vector_count, dtype=jnp.int32) == 4)[:, None]
        new_vectors = jnp.where(row_pick, stepped_vectors * col_shrink, stepped_vectors)
    return (
        result_out,
        token_grad,
        head_peak,
        mean_q,
        square_q,
        new_qkv,
        mean_o,
        square_o,
        new_out,
        mean_u,
        square_u,
        new_up,
        mean_d,
        square_d,
        new_down,
        mean_v,
        square_v,
        new_vectors,
    )


def solution(mesh):
    links = Links(mesh.shape["dp"], mesh.shape["fsdp"])
    return jax.shard_map(
        partial(local, links),
        mesh=mesh,
        in_specs=(
            P(("dp", "fsdp"), None, None),
            P(("dp", "fsdp"), None, None),
            P(("dp", "fsdp")),
            P(("dp", "fsdp"), None),
            P(None, ("dp", "fsdp")),
            P(("dp", "fsdp"), None),
            P(None, ("dp", "fsdp")),
            P(None, ("dp", "fsdp")),
            P(("dp", "fsdp"), None),
            P(None, ("dp", "fsdp")),
            P(("dp", "fsdp"), None),
            P(None, ("dp", "fsdp")),
            P(None, ("dp", "fsdp")),
            P(("dp", "fsdp"), None),
            P(None, ("dp", "fsdp")),
            P(("dp", "fsdp"), None),
            P(None, ("dp", "fsdp")),
            P(None, ("dp", "fsdp")),
        ),
        out_specs=(
            P(("dp", "fsdp"), None, None),
            P(("dp", "fsdp"), None, None),
            P(),
            P(("dp", "fsdp"), None),
            P(("dp", "fsdp"), None),
            P(("dp", "fsdp"), None),
            P(None, ("dp", "fsdp")),
            P(None, ("dp", "fsdp")),
            P(None, ("dp", "fsdp")),
            P(("dp", "fsdp"), None),
            P(("dp", "fsdp"), None),
            P(("dp", "fsdp"), None),
            P(None, ("dp", "fsdp")),
            P(None, ("dp", "fsdp")),
            P(None, ("dp", "fsdp")),
            P(None, ("dp", "fsdp")),
            P(None, ("dp", "fsdp")),
            P(None, ("dp", "fsdp")),
        ),
        check_vma=False,
    )
```

```python
from functools import partial

import jax
import jax.numpy as jnp
import numpy as np
from jax import lax
from jax.experimental import pallas as pl
from jax.experimental.pallas import tpu as pltpu
from jax.sharding import PartitionSpec as P

H = 16
STEP = 10


beta_one = 0.9
beta_two = 0.95
adam_epsilon = 1e-08
weight_decay = 0.1
matrix_rate = 0.1
vector_rate = 0.5
clip_limit = 8.0
norm_epsilon = 1e-06
masked_value = -1e30
TILE = 512
PAIR = 128
HALF_ROOT = 0.5**0.5
DENSITY = 0.3989422804014327
F32 = jnp.float32
BF16 = jnp.bfloat16


def adam_step(weight, gradient, mean_old, square_old, step_rate, decay_rate):
    mean_new = beta_one * mean_old + (1.0 - beta_one) * gradient
    square_new = beta_two * square_old + (1.0 - beta_two) * gradient * gradient
    fix_one = 1.0 - beta_one**STEP
    fix_two = 1.0 - beta_two**STEP
    stepped = weight - step_rate * (
        mean_new / fix_one / (jnp.sqrt(square_new / fix_two) + adam_epsilon) + decay_rate * weight
    )
    return (mean_new, square_new, stepped)


def bit_names(letter, count):
    return tuple(letter + str(at) for at in range(count))


class Links:
    def __init__(self, dp_count, inner_count):
        self.device_count = dp_count * inner_count
        inner_bits = inner_count.bit_length() - 1
        z_bits = bit_names("z", dp_count.bit_length() - 2)
        x_bits = bit_names("x", inner_bits // 2)
        y_bits = bit_names("y", inner_bits - inner_bits // 2)
        self.place = {"c": ("dp", dp_count, 0)}
        self.place.update({bit: ("dp", dp_count, at + 1) for at, bit in enumerate(z_bits)})
        self.place.update({bit: ("fsdp", inner_count, at) for at, bit in enumerate(x_bits)})
        self.place.update(
            {bit: ("fsdp", inner_count, at + len(x_bits)) for at, bit in enumerate(y_bits)}
        )
        self.bits = ("c",) + y_bits + x_bits + z_bits
        self.orders = (y_bits + x_bits, x_bits + y_bits)
        self.z_bits = z_bits
        self.y_bits = y_bits
        self.inner_bits = inner_bits

    def true_block(self):
        masks = []
        for block in range(self.device_count):
            mask = 0
            for at, bit in enumerate(reversed(self.bits)):
                if block >> at & 1:
                    axis, _, place = self.place[bit]
                    mask |= 1 << (place + (self.inner_bits if axis == "dp" else 0))
            masks.append(mask)
        return lax.axis_index(("dp", "fsdp")) ^ jnp.array(masks, jnp.int32)

    def exchange(self, values, bit):
        axis, count, place = self.place[bit]
        return lax.ppermute(values, axis, [(at, at ^ (1 << place)) for at in range(count)])


class Order:
    def __init__(self):
        self.ended = ()

    def __call__(self, call, *operands):
        operands, _ = lax.optimization_barrier((operands, self.ended))
        result = call(*operands)
        self.ended = result
        return result

    def settle(self, value):
        return self(lambda come: come, value)


def run(body, operands, outs, grid=(), in_specs=None, out_specs=None, scratch=()):
    whole = pl.BlockSpec(memory_space=pltpu.VMEM)
    return pl.pallas_call(
        body,
        out_shape=[jax.ShapeDtypeStruct(shape, kind) for shape, kind in outs],
        grid=grid,
        in_specs=in_specs or [whole] * len(operands),
        out_specs=out_specs or [whole] * len(outs),
        scratch_shapes=scratch,
        compiler_params=pltpu.CompilerParams(vmem_limit_bytes=12 * 2**20),
        cost_estimate=pl.CostEstimate(flops=30 * 10**9, bytes_accessed=1000, transcendentals=0),
    )(*operands)


def fixed(shape):
    return pl.BlockSpec(shape, lambda j: (0,) * len(shape))


def mm(first, second):
    return lax.dot_general(first, second, (((1,), (0,)), ((), ())), preferred_element_type=F32)


def mm_turned(first, second):
    return lax.dot_general(first, second, (((1,), (1,)), ((), ())), preferred_element_type=F32)


def mm_rows(first, second):
    return lax.dot_general(first, second, (((0,), (0,)), ((), ())), preferred_element_type=F32)


def pieces(values, count=3):
    out = []
    for _ in range(count):
        piece = values.astype(BF16)
        out.append(piece)
        values = values - piece.astype(F32)
    return out


def normalized(values):
    centered = values - jnp.mean(values, -1, keepdims=True)
    scale = lax.rsqrt(jnp.mean(centered * centered, -1, keepdims=True) + norm_epsilon)
    return centered * scale, scale


def norm_back(grad, values, gain):
    unit, scale = normalized(values)
    inner = grad * gain
    d_values = scale * (
        inner
        - jnp.mean(inner, -1, keepdims=True)
        - unit * jnp.mean(inner * unit, -1, keepdims=True)
    )
    return (
        d_values,
        jnp.sum(grad * unit, 0, keepdims=True),
        jnp.sum(grad, 0, keepdims=True),
    )


def first_norm(inputs, mine, other, to_relative):
    rows, width = inputs.shape
    half = width // 2

    def body(
        x_ref, mine_ref, other_ref, turn_ref, low_ref, high_ref, lowt_ref, hight_ref, rel_ref, true_ref
    ):
        turned = jnp.concatenate(
            [mine_ref[...].astype(F32).T, other_ref[...].astype(F32).T], 1
        )[:16]
        rel_ref[...] = turned
        true_ref[...] = mm_turned(turned.astype(BF16), turn_ref[...])
        unit, _ = normalized(x_ref[...].astype(F32))
        normed = (unit * turned[0:1] + turned[1:2]).astype(BF16)
        low_ref[...] = normed[:, :half]
        high_ref[...] = normed[:, half:]
        lowt_ref[...] = normed[:, :half].T
        hight_ref[...] = normed[:, half:].T

    vectors_at = mine.shape[1] // PAIR - 1
    weights = pl.BlockSpec((half, PAIR), lambda j: (0, vectors_at))
    return run(
        body,
        (inputs, mine, other, to_relative),
        [((rows, half), BF16)] * 2 + [((half, rows), BF16)] * 2 + [((16, width), F32)] * 2,
        (1,),
        [fixed(inputs.shape), weights, weights, fixed(to_relative.shape)],
        [fixed((rows, half))] * 2 + [fixed((half, rows))] * 2 + [fixed((16, width))] * 2,
    )


def project(at, low, high, mine, other, true_vectors):
    rows, half = low.shape

    def body(low_ref, high_ref, mine_ref, other_ref, vec_ref, out_ref):
        j = pl.program_id(0)
        bias = jnp.where(j == 0, vec_ref[4:5, :], jnp.where(j == 2, vec_ref[5:6, :], 0.0))
        value = mm(low_ref[...], mine_ref[...]) + mm(high_ref[...], other_ref[...])
        out_ref[0] = (value + bias).astype(BF16)

    weights = pl.BlockSpec((half, TILE), lambda j: (0, j))
    return run(
        body,
        (low, high, mine, other, true_vectors),
        [((3, rows, TILE), BF16)],
        (3,),
        [fixed(low.shape)] * 2 + [weights] * 2 + [pl.BlockSpec((16, TILE), lambda j: (0, at))],
        [pl.BlockSpec((1, rows, TILE), lambda j: (j, 0, 0))],
    )[0]


def head_mask(rows, side):
    lane = lax.broadcasted_iota(jnp.int32, (rows, PAIR), 1)
    return lane < PAIR // 2 if side == 0 else lane >= PAIR // 2


def attend(projected, counts):
    _, rows, width = projected[0].shape
    steps = width // PAIR

    def body(count_ref, *refs):
        *ins, out_ref, peak_ref = refs
        j = pl.program_id(0)

        def heads(q_ref, k_ref, v_ref):
            count = count_ref[0]
            key_ok = lax.broadcasted_iota(jnp.int32, (rows, rows), 1) < count
            row_ok = lax.broadcasted_iota(jnp.int32, (rows, 1), 0) < count
            queries = q_ref[0]
            out = None
            for side in (0, 1):
                chosen = head_mask(rows, side)
                scores = mm_turned(jnp.where(chosen, queries, 0), k_ref[0]) * (PAIR // 2) ** -0.5
                scores = jnp.where(key_ok, scores, masked_value)
                top = jnp.max(scores, -1, keepdims=True)
                peak = jnp.max(jnp.where(row_ok, top, masked_value))
                peak_ref[pl.ds(j * 2 + side, 1), :] = jnp.full((1, PAIR), peak)
                exponent = jnp.exp(scores - top)
                probs = exponent * (1.0 / jnp.sum(exponent, -1, keepdims=True))
                value = mm(probs.astype(BF16), v_ref[0])
                out = value if side == 0 else jnp.where(chosen, value, out)
            out_ref[...] = out.astype(BF16)

        @pl.when(j < steps)
        def _():
            heads(*ins[:3])

        @pl.when(j >= steps)
        def _():
            heads(*ins[3:])

    def part(index, at):
        return pl.BlockSpec(
            (1, rows, PAIR), lambda j: (index, 0, jnp.clip(j - at * steps, 0, steps - 1))
        )

    return run(
        body,
        (counts, *[projected[0]] * 3, *[projected[1]] * 3),
        [((rows, 2 * width), BF16), ((4 * steps, PAIR), F32)],
        (2 * steps,),
        [pl.BlockSpec(memory_space=pltpu.SMEM)]
        + [part(index, at) for at in (0, 1) for index in range(3)],
        [pl.BlockSpec((rows, PAIR), lambda j: (0, j)), fixed((4 * steps, PAIR))],
    )


def attend_back(projected, d_out, counts):
    _, rows, width = projected.shape
    steps = width // PAIR
    scale = (PAIR // 2) ** -0.5

    def body(count_ref, q_ref, k_ref, v_ref, d_ref, out_ref, sum_ref):
        key_ok = lax.broadcasted_iota(jnp.int32, (rows, rows), 0) < count_ref[0]
        queries, keys, values, grad = q_ref[0], k_ref[0], v_ref[0], d_ref[...]
        parts = [None] * 3
        for side in (0, 1):
            chosen = head_mask(rows, side)
            scores = mm_turned(jnp.where(chosen, keys, 0), queries) * scale
            scores = jnp.where(key_ok, scores, masked_value)
            exponent = jnp.exp(scores - jnp.max(scores, 0, keepdims=True))
            probs = exponent * (1.0 / jnp.sum(exponent, 0, keepdims=True))
            d_probs = mm_turned(jnp.where(chosen, values, 0), grad)
            inner = jnp.sum(probs * d_probs, 0, keepdims=True)
            d_scores = (probs * (d_probs - inner)).astype(BF16)
            new = [
                mm_rows(d_scores, keys) * scale,
                mm(d_scores, queries) * scale,
                mm(probs.astype(BF16), grad),
            ]
            parts = new if side == 0 else [jnp.where(chosen, n, p) for n, p in zip(new, parts)]
        low = [part.astype(BF16) for part in parts]
        for at in range(3):
            out_ref[at] = low[at]
        sum_ref[0:1, :] = jnp.sum(low[0].astype(F32), 0, keepdims=True)
        sum_ref[1:2, :] = jnp.sum(low[2].astype(F32), 0, keepdims=True)

    def part(index):
        return pl.BlockSpec((1, rows, PAIR), lambda j: (index, 0, j))

    columns = pl.BlockSpec((rows, PAIR), lambda j: (0, j))
    return run(
        body,
        (counts, projected, projected, projected, d_out),
        [((3, rows, width), BF16), ((8, width), F32)],
        (steps,),
        [pl.BlockSpec(memory_space=pltpu.SMEM), part(0), part(1), part(2), columns],
        [
            pl.BlockSpec((3, rows, PAIR), lambda j: (0, 0, j)),
            pl.BlockSpec((8, PAIR), lambda j: (0, j)),
        ],
    )


def second_norm(inputs, attended, weights, vectors):
    rows, width = inputs.shape
    half = width // 2

    def body(x_ref, a_ref, b_ref, wa_ref, wa2_ref, wb_ref, wb2_ref, vec_ref, mid_ref, low_ref, high_ref, lowt_ref, hight_ref):
        first, second = a_ref[...], b_ref[...]
        branch = jnp.concatenate(
            [
                mm_turned(first, wa_ref[...]) + mm_turned(second, wb_ref[...]),
                mm_turned(first, wa2_ref[...]) + mm_turned(second, wb2_ref[...]),
            ],
            1,
        )
        middle = x_ref[...].astype(F32) + branch + vec_ref[6:7, :]
        mid_ref[...] = middle
        unit, _ = normalized(middle)
        normed = (unit * vec_ref[2:3, :] + vec_ref[3:4, :]).astype(BF16)
        low_ref[...] = normed[:, :half]
        high_ref[...] = normed[:, half:]
        lowt_ref[...] = normed[:, :half].T
        hight_ref[...] = normed[:, half:].T

    block = pl.BlockSpec((half, TILE), lambda j: (0, 0))
    return run(
        body,
        (inputs, attended, attended, *weights[0], *weights[1], vectors),
        [((rows, width), F32)] + [((rows, half), BF16)] * 2 + [((half, rows), BF16)] * 2,
        (1,),
        [fixed(inputs.shape)]
        + [pl.BlockSpec((rows, TILE), lambda j, at=at: (0, at)) for at in (0, 1)]
        + [block] * 4
        + [fixed(vectors.shape)],
        [fixed((rows, width))] + [fixed((rows, half))] * 2 + [fixed((half, rows))] * 2,
    )


def expand(at, low, high, mine, other, true_vectors):
    rows, half = low.shape
    count = mine.shape[1] - TILE
    per_row = true_vectors.shape[1] // TILE
    first_row = 8 + at * count // true_vectors.shape[1]

    def body(low_ref, high_ref, mine_ref, other_ref, vec_ref, out_ref, slope_ref):
        row = first_row + pl.program_id(0) // per_row
        pre = mm(low_ref[...], mine_ref[...]) + mm(high_ref[...], other_ref[...])
        pre = pre + vec_ref[pl.ds(row, 1), :]
        below = 0.5 * (1.0 + lax.erf(pre * HALF_ROOT))
        out_ref[...] = (pre * below).astype(BF16)
        slope = below + pre * (DENSITY * jnp.exp(-0.5 * pre * pre))
        slope_ref[...] = slope.astype(BF16)

    weights = pl.BlockSpec((half, TILE), lambda j: (0, j + 1))
    columns = pl.BlockSpec((rows, TILE), lambda j: (0, j))
    return run(
        body,
        (low, high, mine, other, true_vectors),
        [((rows, count), BF16)] * 2,
        (count // TILE,),
        [fixed(low.shape)] * 2
        + [weights] * 2
        + [pl.BlockSpec((16, TILE), lambda j: (0, j % per_row))],
        [columns, columns],
    )


def among(count, at, shape):
    return pl.BlockSpec(shape, lambda j: (0, jnp.clip(j - at * count, 0, count - 1)))


def expand_back(low, high, parts, slopes):
    rows, half = low.shape
    steps = parts[0][0].shape[1] // TILE
    slope_steps = slopes[0].shape[1] // TILE

    def body(low_ref, high_ref, *refs):
        weights, slope_refs = refs[: 2 * len(parts)], refs[2 * len(parts) : -2]
        out_ref, sum_ref = refs[-2:]
        j = pl.program_id(0)
        for at in range(len(parts)):

            @pl.when(j // steps == at)
            def _(at=at):
                mine_ref, other_ref = weights[2 * at : 2 * at + 2]
                slope_ref = slope_refs[at * steps // slope_steps]
                value = mm(low_ref[...], mine_ref[...]) + mm(high_ref[...], other_ref[...])
                value = (value * slope_ref[...].astype(F32)).astype(BF16)
                out_ref[...] = value
                sum_ref[...] = jnp.sum(value.astype(F32), 0, keepdims=True)

    count = len(parts) * steps
    return run(
        body,
        (low, high, *[weights for part in parts for weights in part], *slopes),
        [((rows, count * TILE), BF16), ((1, count * TILE), F32)],
        (count,),
        [fixed(low.shape)] * 2
        + [among(steps, at // 2, (half, TILE)) for at in range(2 * len(parts))]
        + [among(slope_steps, at, (rows, TILE)) for at in range(len(slopes))],
        [pl.BlockSpec((rows, TILE), lambda j: (0, j)), pl.BlockSpec((1, TILE), lambda j: (0, j))],
    )


def contract_first(d_pre, mine, other):
    rows, count = d_pre.shape
    half = mine.shape[0]
    count = count // 2

    def body(d_ref, mine_ref, other_ref, out_ref):
        @pl.when(pl.program_id(0) == 0)
        def _():
            out_ref[...] = jnp.zeros_like(out_ref)

        out_ref[:, :half] += mm_turned(d_ref[...], mine_ref[...])
        out_ref[:, half:] += mm_turned(d_ref[...], other_ref[...])

    weights = pl.BlockSpec((half, TILE), lambda j: (0, j + 1))
    return run(
        body,
        (d_pre, mine, other),
        [((rows, 2 * half), F32)],
        (count // TILE,),
        [pl.BlockSpec((rows, TILE), lambda j: (0, j)), weights, weights],
        [fixed((rows, 2 * half))],
    )[0]


def contract_second(d_pre, weights, partial_sum, middle, d_result, vectors):
    rows, count = d_pre.shape
    half = weights[0][0].shape[0]
    width = 2 * half
    steps = count // 2 // TILE

    def body(
        d_ref, mine_ref, other_ref, wa_ref, wa2_ref, wb_ref, wb2_ref, sum_ref, mid_ref, res_ref,
        vec_ref, dm_ref, low_ref, high_ref, outa_ref, outb_ref, grads_ref, total,
    ):
        j = pl.program_id(0)

        @pl.when(j == 0)
        def _():
            total[...] = sum_ref[...]

        total[:, :half] += mm_turned(d_ref[...], mine_ref[...])
        total[:, half:] += mm_turned(d_ref[...], other_ref[...])

        @pl.when(j == steps - 1)
        def _():
            d_values, d_gain, d_shift = norm_back(total[...], mid_ref[...], vec_ref[2:3, :])
            result_grad = res_ref[...].astype(F32)
            d_middle = result_grad + d_values
            branch = d_middle.astype(BF16)
            dm_ref[...] = d_middle
            first, second = branch[:, :half], branch[:, half:]
            low_ref[...] = first.T
            high_ref[...] = second.T
            outa_ref[...] = (mm(first, wa_ref[...]) + mm(second, wa2_ref[...])).astype(BF16)
            outb_ref[...] = (mm(first, wb_ref[...]) + mm(second, wb2_ref[...])).astype(BF16)
            grads_ref[0:1, :] = d_gain
            grads_ref[1:2, :] = d_shift
            grads_ref[2:3, :] = jnp.sum(branch.astype(F32), 0, keepdims=True)
            grads_ref[3:4, :] = jnp.sum(result_grad, 0, keepdims=True)

    tile = pl.BlockSpec((half, TILE), lambda j: (0, j + 1))
    block = pl.BlockSpec((half, TILE), lambda j: (0, 0))
    return run(
        body,
        (d_pre, *weights[1], *weights[0], *weights[1], partial_sum, middle, d_result, vectors),
        [((rows, width), F32)]
        + [((half, rows), BF16)] * 2
        + [((rows, TILE), BF16)] * 2
        + [((8, width), F32)],
        (steps,),
        [pl.BlockSpec((rows, TILE), lambda j: (0, steps + j)), tile, tile]
        + [block] * 4
        + [fixed((rows, width))] * 3
        + [fixed(vectors.shape)],
        [fixed((rows, width))]
        + [fixed((half, rows))] * 2
        + [fixed((rows, TILE))] * 2
        + [fixed((8, width))],
        [pltpu.VMEM((rows, width), F32)],
    )


def input_back_first(d_projected, mine, other):
    rows = d_projected.shape[1]
    half = mine.shape[0]

    def body(d_ref, mine_ref, other_ref, out_ref):
        @pl.when(pl.program_id(0) == 0)
        def _():
            out_ref[...] = jnp.zeros_like(out_ref)

        out_ref[:, :half] += mm_turned(d_ref[0], mine_ref[...])
        out_ref[:, half:] += mm_turned(d_ref[0], other_ref[...])

    weights = pl.BlockSpec((half, TILE), lambda j: (0, j))
    return run(
        body,
        (d_projected, mine, other),
        [((rows, 2 * half), F32)],
        (3,),
        [pl.BlockSpec((1, rows, TILE), lambda j: (j, 0, 0)), weights, weights],
        [fixed((rows, 2 * half))],
    )[0]


def input_back_second(
    d_projected, mine, other, partial_sum, inputs, d_middle, grads, head_sums, d_pre_sums, vectors, to_relative
):
    rows = d_projected.shape[1]
    half = mine.shape[0]
    width = 2 * half

    def body(
        d_ref, mine_ref, other_ref, sum_ref, x_ref, dm_ref, grads_ref, heada_ref, headb_ref, pre_ref,
        vec_ref, turn_ref, out_ref, low_ref, high_ref, total, true_rows, all_rows,
    ):
        j = pl.program_id(0)

        @pl.when(j == 0)
        def _():
            total[...] = sum_ref[...]

        total[:, :half] += mm_turned(d_ref[0], mine_ref[...])
        total[:, half:] += mm_turned(d_ref[0], other_ref[...])

        @pl.when(j == 2)
        def _():
            d_values, d_gain, d_shift = norm_back(total[...], x_ref[...].astype(F32), vec_ref[0:1, :])
            low = (dm_ref[...] + d_values).astype(BF16)
            out_ref[...] = mm_turned(low, turn_ref[...]).astype(BF16)
            true_rows[...] = jnp.zeros_like(true_rows)
            for at, ref in enumerate((heada_ref, headb_ref)):
                true_rows[0:2, at * TILE : (at + 1) * TILE] = ref[0:2, :]
            for part in range(pre_ref.shape[1] // width):
                row = 2 + part
                true_rows[row : row + 1, :] = pre_ref[:, part * width : (part + 1) * width]
            turned = sum(mm(part, turn_ref[...]) for part in pieces(true_rows[...]))
            all_rows[...] = jnp.zeros_like(all_rows)
            all_rows[0:1, :] = d_gain
            all_rows[1:2, :] = d_shift
            all_rows[2:4, :] = grads_ref[0:2, :]
            all_rows[4:6, :] = turned[0:2]
            all_rows[6:8, :] = grads_ref[2:4, :]
            all_rows[8:14, :] = turned[2:8]
            columns = all_rows[...].T
            low_ref[...] = columns[:half]
            high_ref[...] = columns[half:]

    weights = pl.BlockSpec((half, TILE), lambda j: (0, j))
    operands = (
        d_projected,
        mine,
        other,
        partial_sum,
        inputs,
        d_middle,
        grads,
        *head_sums,
        d_pre_sums,
        vectors,
        to_relative,
    )
    return run(
        body,
        operands,
        [((rows, width), BF16)] + [((half, PAIR), F32)] * 2,
        (3,),
        [pl.BlockSpec((1, rows, TILE), lambda j: (j, 0, 0)), weights, weights]
        + [fixed(operand.shape) for operand in operands[3:]],
        [fixed((rows, width))] + [fixed((half, PAIR))] * 2,
        [pltpu.VMEM((rows, width), F32), pltpu.VMEM((8, width), F32), pltpu.VMEM((PAIR, width), F32)],
    )


def contract_hidden(hidden, parts, total):
    half = total.shape[1] // 2
    steps = len(parts) // 2
    per_part = pl.num_programs(0) // steps
    for at in range(steps):

        @pl.when(pl.program_id(0) // per_part == at)
        def _(at=at):
            total[:, :half] += mm_turned(hidden[...], parts[2 * at][...])
            total[:, half:] += mm_turned(hidden[...], parts[2 * at + 1][...])


def finish_first(middle, hidden, parts, vectors):
    rows, width = middle.shape
    steps = hidden.shape[1] // TILE

    def body(hidden_ref, *refs):
        *weights, mid_ref, vec_ref, out_ref = refs

        @pl.when(pl.program_id(0) == 0)
        def _():
            out_ref[...] = mid_ref[...] + vec_ref[7:8, :]

        contract_hidden(hidden_ref, weights, out_ref)

    return run(
        body,
        (hidden, *[weights for part in parts for weights in part], middle, vectors),
        [((rows, width), F32)],
        (steps,),
        [pl.BlockSpec((rows, TILE), lambda j: (0, j))]
        + [among(steps // len(parts), at // 2, (width // 2, TILE)) for at in range(2 * len(parts))]
        + [fixed((rows, width)), fixed(vectors.shape)],
        [fixed((rows, width))],
    )[0]


def finish_second(partial_sum, hidden, parts, to_relative, counts):
    rows, width = partial_sum.shape
    steps = hidden.shape[1] // TILE

    def body(count_ref, hidden_ref, *refs):
        *weights, sum_ref, turn_ref, out_ref, total = refs

        @pl.when(pl.program_id(0) == 0)
        def _():
            total[...] = sum_ref[...]

        contract_hidden(hidden_ref, weights, total)

        @pl.when(pl.program_id(0) == steps - 1)
        def _():
            kept = lax.broadcasted_iota(jnp.int32, (rows, 1), 0) < count_ref[0]
            low = jnp.where(kept, total[...], 0.0).astype(BF16)
            out_ref[...] = mm_turned(low, turn_ref[...]).astype(BF16)

    return run(
        body,
        (counts, hidden, *[weights for part in parts for weights in part], partial_sum, to_relative),
        [((rows, width), BF16)],
        (steps,),
        [pl.BlockSpec(memory_space=pltpu.SMEM), pl.BlockSpec((rows, TILE), lambda j: (0, j))]
        + [among(steps // len(parts), at // 2, (width // 2, TILE)) for at in range(2 * len(parts))]
        + [fixed((rows, width)), fixed(to_relative.shape)],
        [fixed((rows, width))],
        [pltpu.VMEM((rows, width), F32)],
    )[0]


def product(slowest, tiles, extra=()):
    count, rows = tiles[0][0].shape
    operands, specs = [], []
    for *both, width, place in tiles:
        operands += both
        specs += [fixed((count, rows))] * 2
        shape = (1,) * (len(place) - 2) + (rows, width)
        specs += [pl.BlockSpec(shape, lambda j, place=place: place)] * 2
    width = sum(tile[4] for tile in tiles)
    full = width + (extra[0].shape[1] if extra else 0)
    operands += extra
    specs += [fixed(operand.shape) for operand in extra]

    def body(*refs):
        *ins, sent_ref, kept_ref = refs
        first = 0
        for at, tile in enumerate(tiles):
            left, left_other, right, right_other = (
                ref[0] if len(ref.shape) == 3 else ref[...] for ref in ins[4 * at : 4 * at + 4]
            )
            value = (mm(left, right) + mm(left_other, right_other)).astype(BF16)
            columns = slice(first, first + tile[4])
            first += tile[4]
            cut_rows(value, slowest, sent_ref, kept_ref, columns)
        if extra:
            value = (ins[-2][...] + ins[-1][...]).astype(BF16)
            cut_rows(value, slowest, sent_ref, kept_ref, slice(width, full))

    out = (count // 2, full)
    return run(body, operands, [(out, BF16)] * 2, (1,), specs, [fixed(out)] * 2)


def cut_rows(value, slowest, sent_ref, kept_ref, columns):
    part = value.shape[0] // 2 // slowest
    for group in range(slowest):
        low = 2 * group * part
        rows = slice(group * part, (group + 1) * part)
        kept_ref[rows, columns] = value[low : low + part]
        sent_ref[rows, columns] = value[low + part : low + 2 * part]


def product_wide(slowest, first, width, left, left_other, right, right_other):
    rows = right.shape[0]
    count = left.shape[0]

    def body(left_ref, left_other_ref, right_ref, right_other_ref, sent_ref, kept_ref):
        value = mm(left_ref[...], right_ref[...]) + mm(left_other_ref[...], right_other_ref[...])
        cut_rows(value.astype(BF16), slowest, sent_ref, kept_ref, slice(None))

    columns = pl.BlockSpec((rows, TILE), lambda j: (0, first // TILE + j))
    out_columns = pl.BlockSpec((count // 2, TILE), lambda j: (0, j))
    return run(
        body,
        (left, left_other, right, right_other),
        [((count // 2, width), BF16)] * 2,
        (width // TILE,),
        [fixed(left.shape)] * 2 + [columns] * 2,
        [out_columns] * 2,
    )


def added(first, second, kind=BF16):
    return (first.astype(F32) + second.astype(F32)).astype(kind)


def halved(pairs, joined):
    half = pairs[0][0].shape[0] // 2
    widths = [mine.shape[1] for mine, _ in pairs]
    if half % 16:
        totals = [added(*pair) for pair in pairs]
        if joined:
            totals = [jnp.concatenate(totals, 1)]
        return [(total[half:], total[:half]) for total in totals]

    def body(*refs):
        ins, outs = refs[: 2 * len(pairs)], refs[2 * len(pairs) :]
        for at in range(len(pairs)):
            mine, got = ins[2 * at], ins[2 * at + 1]
            sent_ref, kept_ref = outs[:2] if joined else outs[2 * at : 2 * at + 2]
            first = sum(widths[:at]) if joined else 0
            columns = slice(first, first + widths[at])
            sent_ref[:, columns] = added(mine[half:, :], got[half:, :])
            kept_ref[:, columns] = added(mine[:half, :], got[:half, :])

    out_widths = [sum(widths)] if joined else widths
    outs = [((half, width), BF16) for width in out_widths for _ in range(2)]
    outs = run(body, [v for pair in pairs for v in pair], outs)
    return [tuple(outs[at : at + 2]) for at in range(0, len(outs), 2)]


def joined(places, middle, count, mine, got):
    wide = mine[0].shape[-1] if len(mine) == 1 else sum(value.shape[-1] for value in mine)
    parts = (slice(0, middle), slice(middle, wide))
    pairs = list(zip(places, mine, got))
    shapes = [(*value.shape[:at], 2, *value.shape[at:]) for at, value, _ in pairs]

    def widths(shape):
        if count == 1:
            return [(*shape[:-1], wide)]
        return [(*shape[:-1], part.stop - part.start) for part in parts]

    out_shapes = shapes if len(mine) == count else widths(shapes[0])
    if mine[0].shape[-2] % 16:
        both = [jnp.stack([value, come], at) for at, value, come in pairs]
        if len(mine) == count:
            return both
        if count == 1:
            rest = both[0].shape[:-1]
            return [jnp.concatenate([value.reshape(*rest, -1) for value in both], -1)]
        return [both[0][..., part] for part in parts]

    def body(*refs):
        outs = refs[2 * len(mine) :]
        for at, (place, value, _) in enumerate(pairs):
            for side in (0, 1):
                ref = refs[at + side * len(mine)]
                lead = (slice(None),) * place + (side,) + (slice(None),) * (value.ndim - 1 - place)
                if len(mine) == count:
                    outs[at][(*lead, slice(None))] = ref[...]
                elif count == 1:
                    outs[0][(*lead, parts[at])] = ref[...]
                else:
                    for out_ref, part in zip(outs, parts):
                        out_ref[(*lead, slice(None))] = ref[..., part]

    return run(body, [*mine, *got], [(shape, BF16) for shape in out_shapes])


class Sum:
    def __init__(self, links, firsts):
        self.links = links
        self.left, self.pairs = [], []
        self.z_left = links.z_bits
        for parts, order in zip(firsts, links.orders):
            self.add(parts, order)

    def add(self, parts, order):
        sent, kept = parts
        self.left.append(order[1:])
        self.pairs.append((kept, self.links.exchange(sent, order[0])))

    def step(self, order):
        inner = bool(self.left[0])
        joined = not inner and len(self.pairs) > 1
        parts = order(partial(halved, joined=joined), self.pairs)
        if inner:
            bits = [left[0] for left in self.left]
            self.left = [left[1:] for left in self.left]
        else:
            bits = [self.z_left[0]]
            self.z_left = self.z_left[1:]
        self.pairs = [
            (kept, self.links.exchange(sent, bit)) for (sent, kept), bit in zip(parts, bits)
        ]

    def settle(self, order):
        self.pairs = [(kept, order.settle(got)) for kept, got in self.pairs]

    def total(self):
        return added(*self.pairs[0], F32)


class Gather:
    def __init__(self, links, shards, middle):
        self.links, self.middle = links, middle
        steps = [tuple(reversed(order)) for order in links.orders]
        steps = list(zip(*steps))
        between = len(steps) // 2 if len(shards) == 2 else 0
        z_steps = [(bit,) for bit in reversed(links.z_bits)]
        self.steps = steps[:between] + z_steps + steps[between:] + [("c", "c")]
        self.blocks = list(shards)
        self.bits = [(), ()]
        self.send()

    def send(self):
        self.got = [
            self.links.exchange(block, bit) for block, bit in zip(self.blocks, self.steps[0])
        ]

    def join(self, order):
        done, *self.steps = self.steps
        bits = done * 2 if len(done) == 1 else done
        places = []
        for at, bit in enumerate(bits):
            held = sorted((*self.bits[at], bit), key=self.links.bits.index)
            self.bits[at] = tuple(held)
            places.append(held.index(bit))
        self.blocks = order(
            partial(joined, places, self.middle, len(self.steps[0])), self.blocks, self.got
        )
        if self.steps[0][0] == "c":
            self.blocks = [block.reshape(-1, block.shape[-1]) for block in self.blocks]

    def step(self, order):
        self.join(order)
        self.send()

    def settle(self, order):
        self.got = order.settle(self.got)

    def halves(self):
        return list(zip(self.blocks, self.got))


def last_update(late, last, spans, scale, moments, vector_scale, vector_moments):
    spans, vectors_at = spans
    rows, width = moments[0].shape
    count = vector_moments[0].shape[0]

    def body(*refs):
        late_kept, late_got, last_kept, last_got, scale_ref = refs[:5]
        weight_ref, mean_ref, square_ref, vscale_ref, vector_ref, vmean_ref, vsquare_ref = refs[5:12]
        outs = refs[12:]
        sums = [added(late_kept[...], late_got[...], F32), added(last_kept[...], last_got[...], F32)]
        for of_last, first, place, size in spans:
            columns = slice(place, place + size)
            mean, square, stepped = adam_step(
                weight_ref[:, columns],
                sums[of_last][:, first : first + size],
                mean_ref[:, columns],
                square_ref[:, columns],
                matrix_rate,
                weight_decay,
            )
            outs[0][:, columns] = mean
            outs[1][:, columns] = square
            outs[2][:, columns] = stepped * scale_ref[:, columns]
        grads = sums[1][:, vectors_at : vectors_at + PAIR].T[:count]
        mean, square, stepped = adam_step(
            vector_ref[...], grads, vmean_ref[...], vsquare_ref[...], vector_rate, 0.0
        )
        outs[3][...] = mean
        outs[4][...] = square
        row = lax.broadcasted_iota(jnp.int32, stepped.shape, 0)
        outs[5][...] = jnp.where(row == 4, stepped * vscale_ref[...], stepped)

    return run(
        body,
        (*late, *last, scale, *moments, vector_scale, *vector_moments),
        [((rows, width), F32)] * 3 + [(vector_moments[0].shape, F32)] * 3,
    )


def local(
    links,
    tokens,
    cotangent,
    counts,
    w_qkv,
    w_out,
    w_up,
    w_down,
    vectors,
    mean_qkv,
    mean_out,
    mean_up,
    mean_down,
    mean_vectors,
    square_qkv,
    square_out,
    square_up,
    square_down,
    square_vectors,
):
    seq_count, slot_count, model_width = tokens.shape
    rows = seq_count * slot_count
    head_width = model_width // H
    wide = w_down.shape[0]
    vector_count, shard_width = vectors.shape
    half = model_width // 2
    order = Order()

    low_qkv = w_qkv.astype(BF16)
    thirds = [low_qkv[:, at * half : (at + 1) * half] for at in range(6)]
    shard_vectors = jnp.pad(vectors.astype(BF16).T, ((0, 0), (0, PAIR - vector_count)))
    shard_qkv = jnp.concatenate([*thirds[0::2], shard_vectors, *thirds[1::2]], 1)
    low_out, low_up = w_out.astype(BF16).T, w_up.astype(BF16)
    shard_up = jnp.concatenate(
        [low_out[:, :half], low_up[:, : wide // 2], low_out[:, half:], low_up[:, wide // 2 :]], 1
    )
    shard_down = w_down.astype(BF16).T
    gather_qkv = Gather(links, [shard_qkv], 3 * half + PAIR)
    gather_down = Gather(
        links, [shard_down[:, : wide // 2], shard_down[:, wide // 2 :]], wide // 2
    )

    true_rows = (
        links.true_block()[:, None] * shard_width + jnp.arange(shard_width, dtype=jnp.int32)
    ).reshape(1, model_width)
    to_relative = (
        lax.broadcasted_iota(jnp.int32, (model_width, model_width), 0) == true_rows
    ).astype(BF16)
    keep_rows = lax.broadcasted_iota(jnp.int32, (rows, 1), 0) < counts[0]
    d_result = jnp.where(keep_rows, cotangent.reshape(rows, model_width), 0).astype(BF16)
    inputs = mm(tokens.reshape(rows, model_width), to_relative).astype(BF16)
    d_result_turned = mm(d_result, to_relative).astype(BF16)
    d_columns = lax.dot_general(
        to_relative, d_result, (((0,), (1,)), ((), ())), preferred_element_type=F32
    ).astype(BF16)

    def longer(gather, count):
        while len(gather.steps) > count:
            gather.step(order)

    inputs, d_result_turned, d_columns, to_relative = order.settle(
        (inputs, d_result_turned, d_columns, to_relative)
    )
    d_low, d_high = d_result_turned[:, :half], d_result_turned[:, half:]
    longer(gather_qkv, 5)
    gather_qkv.step(order)
    gather_down.settle(order)
    d_other = order.settle(links.exchange(d_columns[half:], "c"))
    d_mine = d_columns[:half]
    gather_qkv.step(order)
    gather_up = Gather(
        links, [order(lambda values: values + 0, shard_up)], half + wide // 2
    )
    gather_qkv.step(order)
    longer(gather_up, 5)
    gather_up.step(order)
    gather_qkv.step(order)
    gather_up.step(order)
    longer(gather_down, 5)
    gather_down.step(order)
    halves_qkv = gather_qkv.halves()
    normed_low, normed_high, normed_mine, normed_send, vector_rows, true_vectors = order(
        first_norm, inputs, *halves_qkv[0], to_relative
    )
    normed_other = links.exchange(normed_send, "c")
    projected = [
        order(partial(project, at), normed_low, normed_high, *halves_qkv[at], true_vectors)
        for at in (0, 1)
    ]
    normed_other = order.settle(normed_other)
    gather_up.step(order)
    shared, peak = order(attend, projected, counts)
    gather_down.step(order)
    shared_other = links.exchange(shared, "c")
    peak, peak_got = [peak], []

    def peak_send(bit):
        sent = order.settle(peak[0])
        peak_got.append(links.exchange(sent, bit))

    def peak_take():
        peak[0] = order(jnp.maximum, peak[0], peak_got.pop())

    first_bit, *more_bits = links.bits
    peak_send(first_bit)
    peak_take()
    for bit in more_bits[4:]:
        peak_send(bit)
        peak_take()
    peak_send(more_bits[0])
    gather_up.step(order)
    shared_other = order.settle(shared_other)
    peak_take()
    peak_send(more_bits[1])
    peak_take()
    peak_send(more_bits[2])
    gather_down.step(order)
    peak_take()
    peak_send(more_bits[3])
    halves_up = gather_up.halves()
    middle, normed_two_low, normed_two_high, normed_two_mine, normed_two_send = order(
        second_norm, inputs, shared, halves_up, vector_rows
    )
    peak_take()
    normed_two_other = links.exchange(normed_two_send, "c")
    hidden, slope, hidden_other = [], [], []
    for at in (0, 1):
        out, out_slope = order(
            partial(expand, at), normed_two_low, normed_two_high, *halves_up[at], true_vectors
        )
        hidden.append(out)
        slope.append(out_slope)
        hidden_other.append(links.exchange(out, "c"))
        if at == 0:
            normed_two_other = order.settle(normed_two_other)
    slowest = [1, 2 ** len(links.y_bits)]

    down_parts = [
        order(
            partial(product_wide, slowest[at], 0, wide // 2),
            d_mine,
            d_other,
            hidden[at],
            hidden_other[at],
        )
        for at in (0, 1)
    ]
    gather_down.step(order)
    sum_down = Sum(links, order.settle(down_parts))
    halves_down = gather_down.halves()
    d_pre, d_pre_sums = order(expand_back, d_low, d_high, halves_down, slope)
    d_pre_other = links.exchange(d_pre, "c")
    partial_sum = order(contract_first, d_pre, *halves_up[0])
    result = order(finish_first, middle, hidden[0], halves_down[:1], vector_rows)
    for _ in links.orders[0][1:]:
        sum_down.step(order)
    sum_up = Sum(
        links,
        [
            order(
                partial(product_wide, slowest[at], at * wide // 2, wide // 2),
                normed_two_mine,
                normed_two_other,
                d_pre,
                d_pre_other,
            )
            for at in (0, 1)
        ],
    )
    d_middle, d_branch_low, d_branch_high, d_out_one, d_out_two, grads = order(
        contract_second, d_pre, halves_up, partial_sum, middle, d_result_turned, vector_rows
    )
    d_branch_other = links.exchange(d_branch_high, "c")
    sum_down.step(order)
    d_branch_other = order.settle(d_branch_other)
    d_projected, d_projected_other, head_sums = [], [], []
    for at, d_out in enumerate((d_out_one, d_out_two)):
        out, sums = order(attend_back, projected[at], d_out, counts)
        d_projected.append(out)
        d_projected_other.append(links.exchange(out, "c"))
        head_sums.append(sums)


    def out_tile(at):
        return (d_branch_low, d_branch_other, shared, shared_other, half, (0, at))

    def qkv_tile(at, part, width, column):
        return (
            normed_mine,
            normed_other,
            d_projected[at],
            d_projected_other[at],
            width,
            (part, 0, column),
        )

    def late_product(at, tiles, extra=()):
        def call(operands, extra):
            return product(
                slowest[at],
                [(*operands[4 * i : 4 * i + 4], *tile[4:]) for i, tile in enumerate(tiles)],
                extra,
            )

        return order(call, [operand for tile in tiles for operand in tile[:4]], extra)

    partial_sum = order(input_back_first, d_projected[0], *halves_qkv[0])
    for _ in links.z_bits[1:]:
        sum_down.step(order)
    for _ in links.orders[0][1:]:
        sum_up.step(order)
    d_projected_other = order.settle(d_projected_other)
    quarter = half // 2
    sum_late = Sum(
        links,
        [
            late_product(at, [out_tile(at), qkv_tile(0, at, half, 0), qkv_tile(0, 2, quarter, at)])
            for at in (0, 1)
        ],
    )
    token_grad, vectors_low, vectors_high = order(
        input_back_second,
        d_projected[1],
        *halves_qkv[1],
        partial_sum,
        inputs,
        d_middle,
        grads,
        head_sums,
        d_pre_sums,
        vector_rows,
        to_relative,
    )
    token_grad = token_grad.reshape(seq_count, slot_count, model_width)
    sum_down.settle(order)
    vectors_other = links.exchange(vectors_high, "c")
    sum_up.step(order)
    last = [
        late_product(
            at,
            [qkv_tile(1, at, half, 0), qkv_tile(1, 2, quarter, at)],
            ((), (vectors_low, vectors_other))[at],
        )
        for at in (0, 1)
    ]
    sum_last = Sum(links, last)
    for _ in links.orders[0][1:]:
        sum_late.step(order)
    for _ in links.z_bits[1:]:
        sum_up.step(order)
    for _ in links.orders[0][1:]:
        sum_last.step(order)
    sum_late.step(order)
    result = order(finish_second, result, hidden[1], halves_down[1:], to_relative, counts)
    result_out = result.reshape(seq_count, slot_count, model_width)
    mean_down = order.settle(mean_down)
    sum_up.settle(order)
    sum_last.step(order)
    for _ in links.z_bits[1:]:
        sum_late.step(order)
    head_peak = order.settle(peak[0])[:, 0]
    vectors, mean_vectors, square_vectors, first_col = order.settle(
        (
            vectors,
            mean_vectors,
            square_vectors,
            lax.axis_index(("dp", "fsdp")) * shard_width,
        )
    )
    shrink = jnp.sqrt(clip_limit / jnp.maximum(head_peak, clip_limit))
    head_cols = jnp.repeat(shrink, head_width)
    qkv_scale = jnp.concatenate([head_cols, head_cols, jnp.ones((model_width,), F32)])[None]
    col_head = (first_col + jnp.arange(shard_width, dtype=jnp.int32)) // head_width
    col_shrink = jnp.sum(
        jnp.where(
            col_head[:, None] == jnp.arange(H, dtype=jnp.int32)[None, :], shrink[None, :], 0.0
        ),
        1,
    )[None]
    for _ in links.z_bits[1:]:
        sum_last.step(order)
    sum_late.settle(order)
    spans = (
        (0, half, 0, half),
        (1, 0, half, half),
        (0, half * 3 + quarter, 2 * half, half),
        (1, half + quarter, 3 * half, half),
        (0, 2 * half, 4 * half, quarter),
        (0, 4 * half + quarter, 4 * half + quarter, quarter),
        (1, half, 5 * half, quarter),
        (1, 2 * half + quarter, 5 * half + quarter, quarter),
    )
    vectors_at = 3 * half
    late = sum_late.total()
    reduced_out = jnp.concatenate([late[:, :half], late[:, 2 * half + quarter :][:, :half]], 1).T
    reduced_up = sum_up.total()
    reduced_down = sum_down.total().T
    mean_o, square_o, new_out = adam_step(
        w_out, reduced_out, mean_out, square_out, matrix_rate, weight_decay
    )
    mean_u, square_u, new_up = adam_step(
        w_up, reduced_up, mean_up, square_up, matrix_rate, weight_decay
    )
    mean_d, square_d, new_down = adam_step(
        w_down, reduced_down, mean_down, square_down, matrix_rate, weight_decay
    )
    if shard_width % 8 == 0:
        mean_q, square_q, new_qkv, mean_v, square_v, new_vectors = last_update(
            sum_late.pairs[0],
            sum_last.pairs[0],
            (spans, vectors_at),
            qkv_scale,
            (w_qkv, mean_qkv, square_qkv),
            col_shrink,
            (vectors, mean_vectors, square_vectors),
        )
    else:
        sums = (late, sum_last.total())
        reduced_qkv = jnp.concatenate(
            [sums[which][:, first : first + size] for which, first, _, size in spans], 1
        )
        mean_q, square_q, stepped_qkv = adam_step(
            w_qkv, reduced_qkv, mean_qkv, square_qkv, matrix_rate, weight_decay
        )
        new_qkv = stepped_qkv * qkv_scale
        reduced_vectors = sums[1][:, vectors_at : vectors_at + vector_count].T
        mean_v, square_v, stepped_vectors = adam_step(
            vectors, reduced_vectors, mean_vectors, square_vectors, vector_rate, 0.0
        )
        row_pick = (jnp.arange(vector_count, dtype=jnp.int32) == 4)[:, None]
        new_vectors = jnp.where(row_pick, stepped_vectors * col_shrink, stepped_vectors)
    return (
        result_out,
        token_grad,
        head_peak,
        mean_q,
        square_q,
        new_qkv,
        mean_o,
        square_o,
        new_out,
        mean_u,
        square_u,
        new_up,
        mean_d,
        square_d,
        new_down,
        mean_v,
        square_v,
        new_vectors,
    )


def solution(mesh):
    links = Links(mesh.shape["dp"], mesh.shape["fsdp"])
    return jax.shard_map(
        partial(local, links),
        mesh=mesh,
        in_specs=(
            P(("dp", "fsdp"), None, None),
            P(("dp", "fsdp"), None, None),
            P(("dp", "fsdp")),
            P(("dp", "fsdp"), None),
            P(None, ("dp", "fsdp")),
            P(("dp", "fsdp"), None),
            P(None, ("dp", "fsdp")),
            P(None, ("dp", "fsdp")),
            P(("dp", "fsdp"), None),
            P(None, ("dp", "fsdp")),
            P(("dp", "fsdp"), None),
            P(None, ("dp", "fsdp")),
            P(None, ("dp", "fsdp")),
            P(("dp", "fsdp"), None),
            P(None, ("dp", "fsdp")),
            P(("dp", "fsdp"), None),
            P(None, ("dp", "fsdp")),
            P(None, ("dp", "fsdp")),
        ),
        out_specs=(
            P(("dp", "fsdp"), None, None),
            P(("dp", "fsdp"), None, None),
            P(),
            P(("dp", "fsdp"), None),
            P(("dp", "fsdp"), None),
            P(("dp", "fsdp"), None),
            P(None, ("dp", "fsdp")),
            P(None, ("dp", "fsdp")),
            P(None, ("dp", "fsdp")),
            P(("dp", "fsdp"), None),
            P(("dp", "fsdp"), None),
            P(("dp", "fsdp"), None),
            P(None, ("dp", "fsdp")),
            P(None, ("dp", "fsdp")),
            P(None, ("dp", "fsdp")),
            P(None, ("dp", "fsdp")),
            P(None, ("dp", "fsdp")),
            P(None, ("dp", "fsdp")),
        ),
        check_vma=False,
    )
```

```python
from functools import partial

import jax
import jax.numpy as jnp
import numpy as np
from jax import lax
from jax.experimental import pallas as pl
from jax.experimental.pallas import tpu as pltpu
from jax.sharding import PartitionSpec as P

H = 16
STEP = 10


beta_one = 0.9
beta_two = 0.95
adam_epsilon = 1e-08
weight_decay = 0.1
matrix_rate = 0.1
vector_rate = 0.5
clip_limit = 8.0
norm_epsilon = 1e-06
masked_value = -1e30
TILE = 512
PAIR = 128
HALF_ROOT = 0.5**0.5
DENSITY = 0.3989422804014327
F32 = jnp.float32
BF16 = jnp.bfloat16


def adam_step(weight, gradient, mean_old, square_old, step_rate, decay_rate):
    mean_new = beta_one * mean_old + (1.0 - beta_one) * gradient
    square_new = beta_two * square_old + (1.0 - beta_two) * gradient * gradient
    fix_one = 1.0 - beta_one**STEP
    fix_two = 1.0 - beta_two**STEP
    stepped = weight - step_rate * (
        mean_new / fix_one / (jnp.sqrt(square_new / fix_two) + adam_epsilon) + decay_rate * weight
    )
    return (mean_new, square_new, stepped)


def bit_names(letter, count):
    return tuple(letter + str(at) for at in range(count))


class Links:
    def __init__(self, dp_count, inner_count):
        self.device_count = dp_count * inner_count
        inner_bits = inner_count.bit_length() - 1
        z_bits = bit_names("z", dp_count.bit_length() - 2)
        x_bits = bit_names("x", inner_bits // 2)
        y_bits = bit_names("y", inner_bits - inner_bits // 2)
        self.place = {"c": ("dp", dp_count, 0)}
        self.place.update({bit: ("dp", dp_count, at + 1) for at, bit in enumerate(z_bits)})
        self.place.update({bit: ("fsdp", inner_count, at) for at, bit in enumerate(x_bits)})
        self.place.update(
            {bit: ("fsdp", inner_count, at + len(x_bits)) for at, bit in enumerate(y_bits)}
        )
        self.bits = ("c",) + y_bits + x_bits + z_bits
        self.orders = (y_bits + x_bits, x_bits + y_bits)
        self.z_bits = z_bits
        self.y_bits = y_bits
        self.inner_bits = inner_bits

    def true_block(self):
        masks = []
        for block in range(self.device_count):
            mask = 0
            for at, bit in enumerate(reversed(self.bits)):
                if block >> at & 1:
                    axis, _, place = self.place[bit]
                    mask |= 1 << (place + (self.inner_bits if axis == "dp" else 0))
            masks.append(mask)
        return lax.axis_index(("dp", "fsdp")) ^ jnp.array(masks, jnp.int32)

    def exchange(self, values, *bits):
        axis, count, _ = self.place[bits[0]]
        mask = sum(1 << self.place[bit][2] for bit in bits)
        return lax.ppermute(values, axis, [(at, at ^ mask) for at in range(count)])


class Order:
    def __init__(self):
        self.ended = ()

    def __call__(self, call, *operands):
        operands, _ = lax.optimization_barrier((operands, self.ended))
        result = call(*operands)
        self.ended = result
        return result

    def settle(self, value):
        return self(lambda come: come, value)


def run(body, operands, outs, grid=(), in_specs=None, out_specs=None, scratch=()):
    whole = pl.BlockSpec(memory_space=pltpu.VMEM)
    return pl.pallas_call(
        body,
        out_shape=[
            pltpu.HBM(shape, kind) if hbm else jax.ShapeDtypeStruct(shape, kind)
            for shape, kind, *hbm in outs
        ],
        grid=grid,
        in_specs=in_specs or [whole] * len(operands),
        out_specs=out_specs or [whole] * len(outs),
        scratch_shapes=scratch,
        compiler_params=pltpu.CompilerParams(vmem_limit_bytes=12 * 2**20),
        cost_estimate=pl.CostEstimate(flops=30 * 10**9, bytes_accessed=1000, transcendentals=0),
    )(*operands)


def fixed(shape):
    return pl.BlockSpec(shape, lambda j: (0,) * len(shape))


def mm(first, second):
    return lax.dot_general(first, second, (((1,), (0,)), ((), ())), preferred_element_type=F32)


def mm_turned(first, second):
    return lax.dot_general(first, second, (((1,), (1,)), ((), ())), preferred_element_type=F32)


def mm_rows(first, second):
    return lax.dot_general(first, second, (((0,), (0,)), ((), ())), preferred_element_type=F32)


def pieces(values, count=3):
    out = []
    for _ in range(count):
        piece = values.astype(BF16)
        out.append(piece)
        values = values - piece.astype(F32)
    return out


def normalized(values):
    centered = values - jnp.mean(values, -1, keepdims=True)
    scale = lax.rsqrt(jnp.mean(centered * centered, -1, keepdims=True) + norm_epsilon)
    return centered * scale, scale


def norm_back(grad, values, gain):
    unit, scale = normalized(values)
    inner = grad * gain
    d_values = scale * (
        inner
        - jnp.mean(inner, -1, keepdims=True)
        - unit * jnp.mean(inner * unit, -1, keepdims=True)
    )
    return (
        d_values,
        jnp.sum(grad * unit, 0, keepdims=True),
        jnp.sum(grad, 0, keepdims=True),
    )


def first_norm(inputs, mine, other, to_relative):
    rows, width = inputs.shape
    half = width // 2

    def body(
        x_ref, mine_ref, other_ref, turn_ref, low_ref, high_ref, lowt_ref, hight_ref, rel_ref, true_ref
    ):
        turned = jnp.concatenate(
            [mine_ref[...].astype(F32).T, other_ref[...].astype(F32).T], 1
        )[:16]
        rel_ref[...] = turned
        true_ref[...] = mm_turned(turned.astype(BF16), turn_ref[...])
        unit, _ = normalized(x_ref[...].astype(F32))
        normed = (unit * turned[0:1] + turned[1:2]).astype(BF16)
        low_ref[...] = normed[:, :half]
        high_ref[...] = normed[:, half:]
        lowt_ref[...] = normed[:, :half].T
        hight_ref[...] = normed[:, half:].T

    vectors_at = mine.shape[1] // PAIR - 1
    weights = pl.BlockSpec((half, PAIR), lambda j: (0, vectors_at))
    return run(
        body,
        (inputs, mine, other, to_relative),
        [((rows, half), BF16)] * 2 + [((half, rows), BF16)] * 2 + [((16, width), F32)] * 2,
        (1,),
        [fixed(inputs.shape), weights, weights, fixed(to_relative.shape)],
        [fixed((rows, half))] * 2 + [fixed((half, rows))] * 2 + [fixed((16, width))] * 2,
    )


def project(at, low, high, mine, other, true_vectors):
    rows, half = low.shape

    def body(low_ref, high_ref, mine_ref, other_ref, vec_ref, out_ref):
        j = pl.program_id(0)
        bias = jnp.where(j == 0, vec_ref[4:5, :], jnp.where(j == 2, vec_ref[5:6, :], 0.0))
        value = mm(low_ref[...], mine_ref[...]) + mm(high_ref[...], other_ref[...])
        out_ref[0] = (value + bias).astype(BF16)

    weights = pl.BlockSpec((half, TILE), lambda j: (0, j))
    return run(
        body,
        (low, high, mine, other, true_vectors),
        [((3, rows, TILE), BF16)],
        (3,),
        [fixed(low.shape)] * 2 + [weights] * 2 + [pl.BlockSpec((16, TILE), lambda j: (0, at))],
        [pl.BlockSpec((1, rows, TILE), lambda j: (j, 0, 0))],
    )[0]


def head_mask(rows, side):
    lane = lax.broadcasted_iota(jnp.int32, (rows, PAIR), 1)
    return lane < PAIR // 2 if side == 0 else lane >= PAIR // 2


def attend(projected, counts):
    _, rows, width = projected[0].shape
    steps = width // PAIR

    def body(count_ref, *refs):
        *ins, out_ref, peak_ref = refs
        j = pl.program_id(0)

        def heads(q_ref, k_ref, v_ref):
            count = count_ref[0]
            key_ok = lax.broadcasted_iota(jnp.int32, (rows, rows), 1) < count
            row_ok = lax.broadcasted_iota(jnp.int32, (rows, 1), 0) < count
            queries = q_ref[0]
            out = None
            for side in (0, 1):
                chosen = head_mask(rows, side)
                scores = mm_turned(jnp.where(chosen, queries, 0), k_ref[0]) * (PAIR // 2) ** -0.5
                scores = jnp.where(key_ok, scores, masked_value)
                top = jnp.max(scores, -1, keepdims=True)
                peak = jnp.max(jnp.where(row_ok, top, masked_value))
                peak_ref[pl.ds(j * 2 + side, 1), :] = jnp.full((1, PAIR), peak)
                exponent = jnp.exp(scores - top)
                probs = exponent * (1.0 / jnp.sum(exponent, -1, keepdims=True))
                value = mm(probs.astype(BF16), v_ref[0])
                out = value if side == 0 else jnp.where(chosen, value, out)
            out_ref[...] = out.astype(BF16)

        @pl.when(j < steps)
        def _():
            heads(*ins[:3])

        @pl.when(j >= steps)
        def _():
            heads(*ins[3:])

    def part(index, at):
        return pl.BlockSpec(
            (1, rows, PAIR), lambda j: (index, 0, jnp.clip(j - at * steps, 0, steps - 1))
        )

    return run(
        body,
        (counts, *[projected[0]] * 3, *[projected[1]] * 3),
        [((rows, 2 * width), BF16), ((4 * steps, PAIR), F32)],
        (2 * steps,),
        [pl.BlockSpec(memory_space=pltpu.SMEM)]
        + [part(index, at) for at in (0, 1) for index in range(3)],
        [pl.BlockSpec((rows, PAIR), lambda j: (0, j)), fixed((4 * steps, PAIR))],
    )


def attend_back(projected, d_out, counts):
    _, rows, width = projected.shape
    steps = width // PAIR
    scale = (PAIR // 2) ** -0.5

    def body(count_ref, q_ref, k_ref, v_ref, d_ref, out_ref, sum_ref):
        key_ok = lax.broadcasted_iota(jnp.int32, (rows, rows), 0) < count_ref[0]
        queries, keys, values, grad = q_ref[0], k_ref[0], v_ref[0], d_ref[...]
        parts = [None] * 3
        for side in (0, 1):
            chosen = head_mask(rows, side)
            scores = mm_turned(jnp.where(chosen, keys, 0), queries) * scale
            scores = jnp.where(key_ok, scores, masked_value)
            exponent = jnp.exp(scores - jnp.max(scores, 0, keepdims=True))
            probs = exponent * (1.0 / jnp.sum(exponent, 0, keepdims=True))
            d_probs = mm_turned(jnp.where(chosen, values, 0), grad)
            inner = jnp.sum(probs * d_probs, 0, keepdims=True)
            d_scores = (probs * (d_probs - inner)).astype(BF16)
            new = [
                mm_rows(d_scores, keys) * scale,
                mm(d_scores, queries) * scale,
                mm(probs.astype(BF16), grad),
            ]
            parts = new if side == 0 else [jnp.where(chosen, n, p) for n, p in zip(new, parts)]
        low = [part.astype(BF16) for part in parts]
        for at in range(3):
            out_ref[at] = low[at]
        sum_ref[0:1, :] = jnp.sum(low[0].astype(F32), 0, keepdims=True)
        sum_ref[1:2, :] = jnp.sum(low[2].astype(F32), 0, keepdims=True)

    def part(index):
        return pl.BlockSpec((1, rows, PAIR), lambda j: (index, 0, j))

    columns = pl.BlockSpec((rows, PAIR), lambda j: (0, j))
    return run(
        body,
        (counts, projected, projected, projected, d_out),
        [((3, rows, width), BF16), ((8, width), F32)],
        (steps,),
        [pl.BlockSpec(memory_space=pltpu.SMEM), part(0), part(1), part(2), columns],
        [
            pl.BlockSpec((3, rows, PAIR), lambda j: (0, 0, j)),
            pl.BlockSpec((8, PAIR), lambda j: (0, j)),
        ],
    )


def second_norm(inputs, attended, weights, vectors):
    rows, width = inputs.shape
    half = width // 2

    def body(x_ref, a_ref, b_ref, wa_ref, wa2_ref, wb_ref, wb2_ref, vec_ref, mid_ref, low_ref, high_ref, lowt_ref, hight_ref):
        first, second = a_ref[...], b_ref[...]
        branch = jnp.concatenate(
            [
                mm_turned(first, wa_ref[...]) + mm_turned(second, wb_ref[...]),
                mm_turned(first, wa2_ref[...]) + mm_turned(second, wb2_ref[...]),
            ],
            1,
        )
        middle = x_ref[...].astype(F32) + branch + vec_ref[6:7, :]
        mid_ref[...] = middle
        unit, _ = normalized(middle)
        normed = (unit * vec_ref[2:3, :] + vec_ref[3:4, :]).astype(BF16)
        low_ref[...] = normed[:, :half]
        high_ref[...] = normed[:, half:]
        lowt_ref[...] = normed[:, :half].T
        hight_ref[...] = normed[:, half:].T

    block = pl.BlockSpec((half, TILE), lambda j: (0, 0))
    return run(
        body,
        (inputs, attended, attended, *weights[0], *weights[1], vectors),
        [((rows, width), F32)] + [((rows, half), BF16)] * 2 + [((half, rows), BF16)] * 2,
        (1,),
        [fixed(inputs.shape)]
        + [pl.BlockSpec((rows, TILE), lambda j, at=at: (0, at)) for at in (0, 1)]
        + [block] * 4
        + [fixed(vectors.shape)],
        [fixed((rows, width))] + [fixed((rows, half))] * 2 + [fixed((half, rows))] * 2,
    )


def expand(at, low, high, mine, other, true_vectors):
    rows, half = low.shape
    count = mine.shape[1] - TILE
    per_row = true_vectors.shape[1] // TILE
    first_row = 8 + at * count // true_vectors.shape[1]

    def body(low_ref, high_ref, mine_ref, other_ref, vec_ref, out_ref, slope_ref):
        row = first_row + pl.program_id(0) // per_row
        pre = mm(low_ref[...], mine_ref[...]) + mm(high_ref[...], other_ref[...])
        pre = pre + vec_ref[pl.ds(row, 1), :]
        below = 0.5 * (1.0 + lax.erf(pre * HALF_ROOT))
        out_ref[...] = (pre * below).astype(BF16)
        slope = below + pre * (DENSITY * jnp.exp(-0.5 * pre * pre))
        slope_ref[...] = slope.astype(BF16)

    weights = pl.BlockSpec((half, TILE), lambda j: (0, j + 1))
    columns = pl.BlockSpec((rows, TILE), lambda j: (0, j))
    return run(
        body,
        (low, high, mine, other, true_vectors),
        [((rows, count), BF16), ((rows, count), BF16, "hbm")],
        (count // TILE,),
        [fixed(low.shape)] * 2
        + [weights] * 2
        + [pl.BlockSpec((16, TILE), lambda j: (0, j % per_row))],
        [columns, columns],
    )


def among(count, at, shape):
    return pl.BlockSpec(shape, lambda j: (0, jnp.clip(j - at * count, 0, count - 1)))


def expand_back(low, high, parts, slopes):
    rows, half = low.shape
    steps = parts[0][0].shape[1] // TILE
    slope_steps = slopes[0].shape[1] // TILE

    def body(low_ref, high_ref, *refs):
        weights, slope_refs = refs[: 2 * len(parts)], refs[2 * len(parts) : -2]
        out_ref, sum_ref = refs[-2:]
        j = pl.program_id(0)
        for at in range(len(parts)):

            @pl.when(j // steps == at)
            def _(at=at):
                mine_ref, other_ref = weights[2 * at : 2 * at + 2]
                slope_ref = slope_refs[at * steps // slope_steps]
                value = mm(low_ref[...], mine_ref[...]) + mm(high_ref[...], other_ref[...])
                value = (value * slope_ref[...].astype(F32)).astype(BF16)
                out_ref[...] = value
                sum_ref[...] = jnp.sum(value.astype(F32), 0, keepdims=True)

    count = len(parts) * steps
    return run(
        body,
        (low, high, *[weights for part in parts for weights in part], *slopes),
        [((rows, count * TILE), BF16), ((1, count * TILE), F32)],
        (count,),
        [fixed(low.shape)] * 2
        + [among(steps, at // 2, (half, TILE)) for at in range(2 * len(parts))]
        + [among(slope_steps, at, (rows, TILE)) for at in range(len(slopes))],
        [pl.BlockSpec((rows, TILE), lambda j: (0, j)), pl.BlockSpec((1, TILE), lambda j: (0, j))],
    )


def contract_first(d_pre, mine, other):
    rows, count = d_pre.shape
    half = mine.shape[0]
    count = count // 2

    def body(d_ref, mine_ref, other_ref, out_ref):
        @pl.when(pl.program_id(0) == 0)
        def _():
            out_ref[...] = jnp.zeros_like(out_ref)

        out_ref[:, :half] += mm_turned(d_ref[...], mine_ref[...])
        out_ref[:, half:] += mm_turned(d_ref[...], other_ref[...])

    weights = pl.BlockSpec((half, TILE), lambda j: (0, j + 1))
    return run(
        body,
        (d_pre, mine, other),
        [((rows, 2 * half), F32)],
        (count // TILE,),
        [pl.BlockSpec((rows, TILE), lambda j: (0, j)), weights, weights],
        [fixed((rows, 2 * half))],
    )[0]


def contract_second(d_pre, weights, partial_sum, middle, d_result, vectors):
    rows, count = d_pre.shape
    half = weights[0][0].shape[0]
    width = 2 * half
    steps = count // 2 // TILE

    def body(
        d_ref, mine_ref, other_ref, wa_ref, wa2_ref, wb_ref, wb2_ref, sum_ref, mid_ref, res_ref,
        vec_ref, dm_ref, low_ref, high_ref, outa_ref, outb_ref, grads_ref, total,
    ):
        j = pl.program_id(0)

        @pl.when(j == 0)
        def _():
            total[...] = sum_ref[...]

        total[:, :half] += mm_turned(d_ref[...], mine_ref[...])
        total[:, half:] += mm_turned(d_ref[...], other_ref[...])

        @pl.when(j == steps - 1)
        def _():
            d_values, d_gain, d_shift = norm_back(total[...], mid_ref[...], vec_ref[2:3, :])
            result_grad = res_ref[...].astype(F32)
            d_middle = result_grad + d_values
            branch = d_middle.astype(BF16)
            dm_ref[...] = d_middle
            first, second = branch[:, :half], branch[:, half:]
            low_ref[...] = first.T
            high_ref[...] = second.T
            outa_ref[...] = (mm(first, wa_ref[...]) + mm(second, wa2_ref[...])).astype(BF16)
            outb_ref[...] = (mm(first, wb_ref[...]) + mm(second, wb2_ref[...])).astype(BF16)
            grads_ref[0:1, :] = d_gain
            grads_ref[1:2, :] = d_shift
            grads_ref[2:3, :] = jnp.sum(branch.astype(F32), 0, keepdims=True)
            grads_ref[3:4, :] = jnp.sum(result_grad, 0, keepdims=True)

    tile = pl.BlockSpec((half, TILE), lambda j: (0, j + 1))
    block = pl.BlockSpec((half, TILE), lambda j: (0, 0))
    return run(
        body,
        (d_pre, *weights[1], *weights[0], *weights[1], partial_sum, middle, d_result, vectors),
        [((rows, width), F32)]
        + [((half, rows), BF16)] * 2
        + [((rows, TILE), BF16)] * 2
        + [((8, width), F32)],
        (steps,),
        [pl.BlockSpec((rows, TILE), lambda j: (0, steps + j)), tile, tile]
        + [block] * 4
        + [fixed((rows, width))] * 3
        + [fixed(vectors.shape)],
        [fixed((rows, width))]
        + [fixed((half, rows))] * 2
        + [fixed((rows, TILE))] * 2
        + [fixed((8, width))],
        [pltpu.VMEM((rows, width), F32)],
    )


def input_back_first(d_projected, mine, other):
    rows = d_projected.shape[1]
    half = mine.shape[0]

    def body(d_ref, mine_ref, other_ref, out_ref):
        @pl.when(pl.program_id(0) == 0)
        def _():
            out_ref[...] = jnp.zeros_like(out_ref)

        out_ref[:, :half] += mm_turned(d_ref[0], mine_ref[...])
        out_ref[:, half:] += mm_turned(d_ref[0], other_ref[...])

    weights = pl.BlockSpec((half, TILE), lambda j: (0, j))
    return run(
        body,
        (d_projected, mine, other),
        [((rows, 2 * half), F32)],
        (3,),
        [pl.BlockSpec((1, rows, TILE), lambda j: (j, 0, 0)), weights, weights],
        [fixed((rows, 2 * half))],
    )[0]


def input_back_second(
    d_projected, mine, other, partial_sum, inputs, d_middle, grads, head_sums, d_pre_sums, vectors, to_relative
):
    rows = d_projected.shape[1]
    half = mine.shape[0]
    width = 2 * half

    def body(
        d_ref, mine_ref, other_ref, sum_ref, x_ref, dm_ref, grads_ref, heada_ref, headb_ref, pre_ref,
        vec_ref, turn_ref, out_ref, low_ref, high_ref, total, true_rows, all_rows,
    ):
        j = pl.program_id(0)

        @pl.when(j == 0)
        def _():
            total[...] = sum_ref[...]

        total[:, :half] += mm_turned(d_ref[0], mine_ref[...])
        total[:, half:] += mm_turned(d_ref[0], other_ref[...])

        @pl.when(j == 2)
        def _():
            d_values, d_gain, d_shift = norm_back(total[...], x_ref[...].astype(F32), vec_ref[0:1, :])
            low = (dm_ref[...] + d_values).astype(BF16)
            out_ref[...] = mm_turned(low, turn_ref[...]).astype(BF16)
            true_rows[...] = jnp.zeros_like(true_rows)
            for at, ref in enumerate((heada_ref, headb_ref)):
                true_rows[0:2, at * TILE : (at + 1) * TILE] = ref[0:2, :]
            for part in range(pre_ref.shape[1] // width):
                row = 2 + part
                true_rows[row : row + 1, :] = pre_ref[:, part * width : (part + 1) * width]
            turned = sum(mm(part, turn_ref[...]) for part in pieces(true_rows[...]))
            all_rows[...] = jnp.zeros_like(all_rows)
            all_rows[0:1, :] = d_gain
            all_rows[1:2, :] = d_shift
            all_rows[2:4, :] = grads_ref[0:2, :]
            all_rows[4:6, :] = turned[0:2]
            all_rows[6:8, :] = grads_ref[2:4, :]
            all_rows[8:14, :] = turned[2:8]
            columns = all_rows[...].T
            low_ref[...] = columns[:half]
            high_ref[...] = columns[half:]

    weights = pl.BlockSpec((half, TILE), lambda j: (0, j))
    operands = (
        d_projected,
        mine,
        other,
        partial_sum,
        inputs,
        d_middle,
        grads,
        *head_sums,
        d_pre_sums,
        vectors,
        to_relative,
    )
    return run(
        body,
        operands,
        [((rows, width), BF16)] + [((half, PAIR), F32)] * 2,
        (3,),
        [pl.BlockSpec((1, rows, TILE), lambda j: (j, 0, 0)), weights, weights]
        + [fixed(operand.shape) for operand in operands[3:]],
        [fixed((rows, width))] + [fixed((half, PAIR))] * 2,
        [pltpu.VMEM((rows, width), F32), pltpu.VMEM((8, width), F32), pltpu.VMEM((PAIR, width), F32)],
    )


def contract_hidden(hidden, parts, total):
    half = total.shape[1] // 2
    steps = len(parts) // 2
    per_part = pl.num_programs(0) // steps
    for at in range(steps):

        @pl.when(pl.program_id(0) // per_part == at)
        def _(at=at):
            total[:, :half] += mm_turned(hidden[...], parts[2 * at][...])
            total[:, half:] += mm_turned(hidden[...], parts[2 * at + 1][...])


def finish_first(middle, hidden, parts, vectors):
    rows, width = middle.shape
    steps = hidden.shape[1] // TILE

    def body(hidden_ref, *refs):
        *weights, mid_ref, vec_ref, out_ref = refs

        @pl.when(pl.program_id(0) == 0)
        def _():
            out_ref[...] = mid_ref[...] + vec_ref[7:8, :]

        contract_hidden(hidden_ref, weights, out_ref)

    return run(
        body,
        (hidden, *[weights for part in parts for weights in part], middle, vectors),
        [((rows, width), F32)],
        (steps,),
        [pl.BlockSpec((rows, TILE), lambda j: (0, j))]
        + [among(steps // len(parts), at // 2, (width // 2, TILE)) for at in range(2 * len(parts))]
        + [fixed((rows, width)), fixed(vectors.shape)],
        [fixed((rows, width))],
    )[0]


def finish_second(partial_sum, hidden, parts, to_relative, counts):
    rows, width = partial_sum.shape
    steps = hidden.shape[1] // TILE

    def body(count_ref, hidden_ref, *refs):
        *weights, sum_ref, turn_ref, out_ref, total = refs

        @pl.when(pl.program_id(0) == 0)
        def _():
            total[...] = sum_ref[...]

        contract_hidden(hidden_ref, weights, total)

        @pl.when(pl.program_id(0) == steps - 1)
        def _():
            kept = lax.broadcasted_iota(jnp.int32, (rows, 1), 0) < count_ref[0]
            low = jnp.where(kept, total[...], 0.0).astype(BF16)
            out_ref[...] = mm_turned(low, turn_ref[...]).astype(BF16)

    return run(
        body,
        (counts, hidden, *[weights for part in parts for weights in part], partial_sum, to_relative),
        [((rows, width), BF16)],
        (steps,),
        [pl.BlockSpec(memory_space=pltpu.SMEM), pl.BlockSpec((rows, TILE), lambda j: (0, j))]
        + [among(steps // len(parts), at // 2, (width // 2, TILE)) for at in range(2 * len(parts))]
        + [fixed((rows, width)), fixed(to_relative.shape)],
        [fixed((rows, width))],
        [pltpu.VMEM((rows, width), F32)],
    )[0]


def product(slowest, tiles, extra=()):
    count, rows = tiles[0][0].shape
    operands, specs = [], []
    for *both, width, place in tiles:
        operands += both
        specs += [fixed((count, rows))] * 2
        shape = (1,) * (len(place) - 2) + (rows, width)
        specs += [pl.BlockSpec(shape, lambda j, place=place: place)] * 2
    width = sum(tile[4] for tile in tiles)
    full = width + (extra[0].shape[1] if extra else 0)
    operands += extra
    specs += [fixed(operand.shape) for operand in extra]

    def body(*refs):
        *ins, sent_ref, kept_ref = refs
        first = 0
        for at, tile in enumerate(tiles):
            left, left_other, right, right_other = (
                ref[0] if len(ref.shape) == 3 else ref[...] for ref in ins[4 * at : 4 * at + 4]
            )
            value = (mm(left, right) + mm(left_other, right_other)).astype(BF16)
            columns = slice(first, first + tile[4])
            first += tile[4]
            cut_rows(value, slowest, sent_ref, kept_ref, columns)
        if extra:
            value = (ins[-2][...] + ins[-1][...]).astype(BF16)
            cut_rows(value, slowest, sent_ref, kept_ref, slice(width, full))

    out = (count // 2, full)
    return run(body, operands, [(out, BF16)] * 2, (1,), specs, [fixed(out)] * 2)


def cut_rows(value, slowest, sent_ref, kept_ref, columns):
    part = value.shape[0] // 2 // slowest
    for group in range(slowest):
        low = 2 * group * part
        rows = slice(group * part, (group + 1) * part)
        kept_ref[rows, columns] = value[low : low + part]
        sent_ref[rows, columns] = value[low + part : low + 2 * part]


def product_wide(slowest, first, width, left, left_other, right, right_other):
    rows = right.shape[0]
    count = left.shape[0]

    def body(left_ref, left_other_ref, right_ref, right_other_ref, sent_ref, kept_ref):
        value = mm(left_ref[...], right_ref[...]) + mm(left_other_ref[...], right_other_ref[...])
        cut_rows(value.astype(BF16), slowest, sent_ref, kept_ref, slice(None))

    columns = pl.BlockSpec((rows, TILE), lambda j: (0, first // TILE + j))
    out_columns = pl.BlockSpec((count // 2, TILE), lambda j: (0, j))
    return run(
        body,
        (left, left_other, right, right_other),
        [((count // 2, width), BF16, "hbm")] * 2,
        (width // TILE,),
        [fixed(left.shape)] * 2 + [columns] * 2,
        [out_columns] * 2,
    )


def added(first, second, kind=BF16):
    return (first.astype(F32) + second.astype(F32)).astype(kind)


def halved(pairs, joined):
    half = pairs[0][0].shape[0] // 2
    widths = [mine.shape[1] for mine, _ in pairs]
    if half % 16:
        totals = [added(*pair) for pair in pairs]
        if joined:
            totals = [jnp.concatenate(totals, 1)]
        return [(total[half:], total[:half]) for total in totals]

    def body(*refs):
        ins, outs = refs[: 2 * len(pairs)], refs[2 * len(pairs) :]
        for at in range(len(pairs)):
            mine, got = ins[2 * at], ins[2 * at + 1]
            sent_ref, kept_ref = outs[:2] if joined else outs[2 * at : 2 * at + 2]
            first = sum(widths[:at]) if joined else 0
            columns = slice(first, first + widths[at])
            sent_ref[:, columns] = added(mine[half:, :], got[half:, :])
            kept_ref[:, columns] = added(mine[:half, :], got[:half, :])

    out_widths = [sum(widths)] if joined else widths
    outs = [((half, width), BF16) for width in out_widths for _ in range(2)]
    outs = run(body, [v for pair in pairs for v in pair], outs)
    return [tuple(outs[at : at + 2]) for at in range(0, len(outs), 2)]


def joined(places, middle, count, mine, got):
    wide = mine[0].shape[-1] if len(mine) == 1 else sum(value.shape[-1] for value in mine)
    parts = (slice(0, middle), slice(middle, wide))
    pairs = list(zip(places, mine, got))
    shapes = [(*value.shape[:at], 2, *value.shape[at:]) for at, value, _ in pairs]

    def widths(shape):
        if count == 1:
            return [(*shape[:-1], wide)]
        return [(*shape[:-1], part.stop - part.start) for part in parts]

    out_shapes = shapes if len(mine) == count else widths(shapes[0])
    if mine[0].shape[-2] % 16:
        both = [jnp.stack([value, come], at) for at, value, come in pairs]
        if len(mine) == count:
            return both
        if count == 1:
            rest = both[0].shape[:-1]
            return [jnp.concatenate([value.reshape(*rest, -1) for value in both], -1)]
        return [both[0][..., part] for part in parts]

    def body(*refs):
        outs = refs[2 * len(mine) :]
        for at, (place, value, _) in enumerate(pairs):
            for side in (0, 1):
                ref = refs[at + side * len(mine)]
                lead = (slice(None),) * place + (side,) + (slice(None),) * (value.ndim - 1 - place)
                if len(mine) == count:
                    outs[at][(*lead, slice(None))] = ref[...]
                elif count == 1:
                    outs[0][(*lead, parts[at])] = ref[...]
                else:
                    for out_ref, part in zip(outs, parts):
                        out_ref[(*lead, slice(None))] = ref[..., part]

    return run(body, [*mine, *got], [(shape, BF16) for shape in out_shapes])


def joined_all(bits, middle, blocks):
    rows, wide = blocks[0].shape
    parts = (slice(0, middle), slice(middle, wide))
    shape = (2,) * bits
    if rows % 16:
        whole = jnp.stack(blocks).reshape(*shape, rows, wide)
        return [whole[..., part] for part in parts]

    def body(*refs):
        for at, ref in enumerate(refs[: len(blocks)]):
            lead = tuple(at >> (bits - 1 - bit) & 1 for bit in range(bits))
            for out_ref, part in zip(refs[len(blocks) :], parts):
                out_ref[(*lead, slice(None), slice(None))] = ref[:, part]

    return run(
        body, blocks, [((*shape, rows, part.stop - part.start), BF16) for part in parts]
    )


class Sum:
    def __init__(self, links, firsts):
        self.links = links
        self.left, self.pairs = [], []
        self.z_left = links.z_bits
        for parts, order in zip(firsts, links.orders):
            self.add(parts, order)

    def add(self, parts, order):
        sent, kept = parts
        self.left.append(order[1:])
        self.pairs.append((kept, self.links.exchange(sent, order[0])))

    def step(self, order):
        inner = bool(self.left[0])
        joined = not inner and len(self.pairs) > 1
        parts = order(partial(halved, joined=joined), self.pairs)
        if inner:
            bits = [left[0] for left in self.left]
            self.left = [left[1:] for left in self.left]
        else:
            bits = [self.z_left[0]]
            self.z_left = self.z_left[1:]
        self.pairs = [
            (kept, self.links.exchange(sent, bit)) for (sent, kept), bit in zip(parts, bits)
        ]

    def settle(self, order):
        self.pairs = [(kept, order.settle(got)) for kept, got in self.pairs]

    def total(self):
        return added(*self.pairs[0], F32)


class Gather:
    def __init__(self, links, shards, middle, at_once=False):
        self.links, self.middle = links, middle
        steps = [tuple(reversed(order)) for order in links.orders]
        steps = list(zip(*steps))
        between = len(steps) // 2 if len(shards) == 2 else 0
        z_steps = ["all z"] if at_once else [(bit,) for bit in reversed(links.z_bits)]
        self.steps = steps[:between] + z_steps + steps[between:] + [("c", "c")]
        self.blocks = list(shards)
        self.bits = [(), ()]
        self.send()

    def send(self):
        if self.steps[0] == "all z":
            z_bits = self.links.z_bits
            chosen = [
                [bit for at, bit in enumerate(z_bits) if block >> (len(z_bits) - 1 - at) & 1]
                for block in range(1, 2 ** len(z_bits))
            ]
            self.got = [self.links.exchange(self.blocks[0], *bits) for bits in chosen]
            return
        self.got = [
            self.links.exchange(block, bit) for block, bit in zip(self.blocks, self.steps[0])
        ]

    def join(self, order):
        done, *self.steps = self.steps
        if done == "all z":
            z_bits = self.links.z_bits
            self.bits = [z_bits, z_bits]
            self.blocks = order(
                partial(joined_all, len(z_bits), self.middle), [*self.blocks, *self.got]
            )
            return
        bits = done * 2 if len(done) == 1 else done
        places = []
        for at, bit in enumerate(bits):
            held = sorted((*self.bits[at], bit), key=self.links.bits.index)
            self.bits[at] = tuple(held)
            places.append(held.index(bit))
        self.blocks = order(
            partial(joined, places, self.middle, len(self.steps[0])), self.blocks, self.got
        )
        if self.steps[0][0] == "c":
            self.blocks = [block.reshape(-1, block.shape[-1]) for block in self.blocks]

    def step(self, order):
        self.join(order)
        self.send()

    def settle(self, order):
        self.got = order.settle(self.got)

    def halves(self):
        return list(zip(self.blocks, self.got))


def last_update(late, last, spans, scale, moments, vector_scale, vector_moments):
    spans, vectors_at = spans
    rows, width = moments[0].shape
    count = vector_moments[0].shape[0]

    def body(*refs):
        late_kept, late_got, last_kept, last_got, scale_ref = refs[:5]
        weight_ref, mean_ref, square_ref, vscale_ref, vector_ref, vmean_ref, vsquare_ref = refs[5:12]
        outs = refs[12:]
        sums = [added(late_kept[...], late_got[...], F32), added(last_kept[...], last_got[...], F32)]
        for of_last, first, place, size in spans:
            columns = slice(place, place + size)
            mean, square, stepped = adam_step(
                weight_ref[:, columns],
                sums[of_last][:, first : first + size],
                mean_ref[:, columns],
                square_ref[:, columns],
                matrix_rate,
                weight_decay,
            )
            outs[0][:, columns] = mean
            outs[1][:, columns] = square
            outs[2][:, columns] = stepped * scale_ref[:, columns]
        grads = sums[1][:, vectors_at : vectors_at + PAIR].T[:count]
        mean, square, stepped = adam_step(
            vector_ref[...], grads, vmean_ref[...], vsquare_ref[...], vector_rate, 0.0
        )
        outs[3][...] = mean
        outs[4][...] = square
        row = lax.broadcasted_iota(jnp.int32, stepped.shape, 0)
        outs[5][...] = jnp.where(row == 4, stepped * vscale_ref[...], stepped)

    return run(
        body,
        (*late, *last, scale, *moments, vector_scale, *vector_moments),
        [((rows, width), F32)] * 3 + [(vector_moments[0].shape, F32)] * 3,
    )


def local(
    links,
    tokens,
    cotangent,
    counts,
    w_qkv,
    w_out,
    w_up,
    w_down,
    vectors,
    mean_qkv,
    mean_out,
    mean_up,
    mean_down,
    mean_vectors,
    square_qkv,
    square_out,
    square_up,
    square_down,
    square_vectors,
):
    seq_count, slot_count, model_width = tokens.shape
    rows = seq_count * slot_count
    head_width = model_width // H
    wide = w_down.shape[0]
    vector_count, shard_width = vectors.shape
    half = model_width // 2
    order = Order()

    low_qkv = w_qkv.astype(BF16)
    thirds = [low_qkv[:, at * half : (at + 1) * half] for at in range(6)]
    shard_vectors = jnp.pad(vectors.astype(BF16).T, ((0, 0), (0, PAIR - vector_count)))
    shard_qkv = jnp.concatenate([*thirds[0::2], shard_vectors, *thirds[1::2]], 1)
    low_out, low_up = w_out.astype(BF16).T, w_up.astype(BF16)
    shard_up = jnp.concatenate(
        [low_out[:, :half], low_up[:, : wide // 2], low_out[:, half:], low_up[:, wide // 2 :]], 1
    )
    shard_down = w_down.astype(BF16).T
    gather_qkv = Gather(links, [shard_qkv], 3 * half + PAIR, True)
    gather_down = Gather(
        links, [shard_down[:, : wide // 2], shard_down[:, wide // 2 :]], wide // 2
    )

    true_rows = (
        links.true_block()[:, None] * shard_width + jnp.arange(shard_width, dtype=jnp.int32)
    ).reshape(1, model_width)
    to_relative = (
        lax.broadcasted_iota(jnp.int32, (model_width, model_width), 0) == true_rows
    ).astype(BF16)
    keep_rows = lax.broadcasted_iota(jnp.int32, (rows, 1), 0) < counts[0]
    d_result = jnp.where(keep_rows, cotangent.reshape(rows, model_width), 0).astype(BF16)
    inputs = mm(tokens.reshape(rows, model_width), to_relative).astype(BF16)
    d_result_turned = mm(d_result, to_relative).astype(BF16)
    d_columns = lax.dot_general(
        to_relative, d_result, (((0,), (1,)), ((), ())), preferred_element_type=F32
    ).astype(BF16)

    def longer(gather, count):
        while len(gather.steps) > count:
            gather.step(order)

    inputs, d_result_turned, d_columns, to_relative = order.settle(
        (inputs, d_result_turned, d_columns, to_relative)
    )
    d_low, d_high = d_result_turned[:, :half], d_result_turned[:, half:]
    longer(gather_qkv, 4)
    gather_down.settle(order)
    d_other = order.settle(links.exchange(d_columns[half:], "c"))
    d_mine = d_columns[:half]
    gather_qkv.step(order)
    gather_up = Gather(
        links, [order(lambda values: values + 0, shard_up)], half + wide // 2
    )
    gather_qkv.step(order)
    longer(gather_up, 5)
    gather_up.step(order)
    gather_qkv.step(order)
    gather_up.step(order)
    longer(gather_down, 5)
    gather_down.step(order)
    halves_qkv = gather_qkv.halves()
    normed_low, normed_high, normed_mine, normed_send, vector_rows, true_vectors = order(
        first_norm, inputs, *halves_qkv[0], to_relative
    )
    normed_other = links.exchange(normed_send, "c")
    projected = [
        order(partial(project, at), normed_low, normed_high, *halves_qkv[at], true_vectors)
        for at in (0, 1)
    ]
    normed_other = order.settle(normed_other)
    gather_up.step(order)
    shared, peak = order(attend, projected, counts)
    gather_down.step(order)
    shared_other = links.exchange(shared, "c")
    peak, peak_got = [peak], []

    def peak_send(bit):
        sent = order.settle(peak[0])
        peak_got.append(links.exchange(sent, bit))

    def peak_take():
        peak[0] = order(jnp.maximum, peak[0], peak_got.pop())

    first_bit, *more_bits = links.bits
    peak_send(first_bit)
    peak_take()
    for bit in more_bits[4:]:
        peak_send(bit)
        peak_take()
    peak_send(more_bits[0])
    gather_up.step(order)
    shared_other = order.settle(shared_other)
    peak_take()
    peak_send(more_bits[1])
    peak_take()
    peak_send(more_bits[2])
    gather_down.step(order)
    peak_take()
    peak_send(more_bits[3])
    halves_up = gather_up.halves()
    middle, normed_two_low, normed_two_high, normed_two_mine, normed_two_send = order(
        second_norm, inputs, shared, halves_up, vector_rows
    )
    peak_take()
    normed_two_other = links.exchange(normed_two_send, "c")
    hidden, slope, hidden_other = [], [], []
    for at in (0, 1):
        out, out_slope = order(
            partial(expand, at), normed_two_low, normed_two_high, *halves_up[at], true_vectors
        )
        hidden.append(out)
        slope.append(out_slope)
        hidden_other.append(links.exchange(out, "c"))
        if at == 0:
            normed_two_other = order.settle(normed_two_other)
    slowest = [1, 2 ** len(links.y_bits)]

    down_parts = [
        order(
            partial(product_wide, slowest[at], 0, wide // 2),
            d_mine,
            d_other,
            hidden[at],
            hidden_other[at],
        )
        for at in (0, 1)
    ]
    gather_down.step(order)
    sum_down = Sum(links, order.settle(down_parts))
    halves_down = gather_down.halves()
    d_pre, d_pre_sums = order(expand_back, d_low, d_high, halves_down, slope)
    d_pre_other = links.exchange(d_pre, "c")
    partial_sum = order(contract_first, d_pre, *halves_up[0])
    result = order(finish_first, middle, hidden[0], halves_down[:1], vector_rows)
    for _ in links.orders[0][1:]:
        sum_down.step(order)
    sum_up = Sum(
        links,
        [
            order(
                partial(product_wide, slowest[at], at * wide // 2, wide // 2),
                normed_two_mine,
                normed_two_other,
                d_pre,
                d_pre_other,
            )
            for at in (0, 1)
        ],
    )
    d_middle, d_branch_low, d_branch_high, d_out_one, d_out_two, grads = order(
        contract_second, d_pre, halves_up, partial_sum, middle, d_result_turned, vector_rows
    )
    d_branch_other = links.exchange(d_branch_high, "c")
    sum_down.step(order)
    d_branch_other = order.settle(d_branch_other)
    d_projected, d_projected_other, head_sums = [], [], []
    for at, d_out in enumerate((d_out_one, d_out_two)):
        out, sums = order(attend_back, projected[at], d_out, counts)
        d_projected.append(out)
        d_projected_other.append(links.exchange(out, "c"))
        head_sums.append(sums)


    def out_tile(at):
        return (d_branch_low, d_branch_other, shared, shared_other, half, (0, at))

    def qkv_tile(at, part, width, column):
        return (
            normed_mine,
            normed_other,
            d_projected[at],
            d_projected_other[at],
            width,
            (part, 0, column),
        )

    def late_product(at, tiles, extra=()):
        def call(operands, extra):
            return product(
                slowest[at],
                [(*operands[4 * i : 4 * i + 4], *tile[4:]) for i, tile in enumerate(tiles)],
                extra,
            )

        return order(call, [operand for tile in tiles for operand in tile[:4]], extra)

    partial_sum = order(input_back_first, d_projected[0], *halves_qkv[0])
    for _ in links.z_bits[1:]:
        sum_down.step(order)
    for _ in links.orders[0][1:]:
        sum_up.step(order)
    d_projected_other = order.settle(d_projected_other)
    quarter = half // 2
    sum_late = Sum(
        links,
        [
            late_product(at, [out_tile(at), qkv_tile(0, at, half, 0), qkv_tile(0, 2, quarter, at)])
            for at in (0, 1)
        ],
    )
    token_grad, vectors_low, vectors_high = order(
        input_back_second,
        d_projected[1],
        *halves_qkv[1],
        partial_sum,
        inputs,
        d_middle,
        grads,
        head_sums,
        d_pre_sums,
        vector_rows,
        to_relative,
    )
    token_grad = token_grad.reshape(seq_count, slot_count, model_width)
    sum_down.settle(order)
    vectors_other = links.exchange(vectors_high, "c")
    sum_up.step(order)
    last = [
        late_product(
            at,
            [qkv_tile(1, at, half, 0), qkv_tile(1, 2, quarter, at)],
            ((), (vectors_low, vectors_other))[at],
        )
        for at in (0, 1)
    ]
    sum_last = Sum(links, last)
    result = order(finish_second, result, hidden[1], halves_down[1:], to_relative, counts)
    result_out = result.reshape(seq_count, slot_count, model_width)
    for _ in links.orders[0][1:]:
        sum_late.step(order)
    for _ in links.z_bits[1:]:
        sum_up.step(order)
    for _ in links.orders[0][1:]:
        sum_last.step(order)
    sum_late.step(order)
    sum_last.step(order)
    mean_down, mean_up = order.settle((mean_down, mean_up))
    sum_up.settle(order)
    for _ in links.z_bits[1:]:
        sum_late.step(order)
    head_peak = order.settle(peak[0])[:, 0]
    vectors, mean_vectors, square_vectors, first_col = order.settle(
        (
            vectors,
            mean_vectors,
            square_vectors,
            lax.axis_index(("dp", "fsdp")) * shard_width,
        )
    )
    shrink = jnp.sqrt(clip_limit / jnp.maximum(head_peak, clip_limit))
    head_cols = jnp.repeat(shrink, head_width)
    qkv_scale = jnp.concatenate([head_cols, head_cols, jnp.ones((model_width,), F32)])[None]
    col_head = (first_col + jnp.arange(shard_width, dtype=jnp.int32)) // head_width
    col_shrink = jnp.sum(
        jnp.where(
            col_head[:, None] == jnp.arange(H, dtype=jnp.int32)[None, :], shrink[None, :], 0.0
        ),
        1,
    )[None]
    for _ in links.z_bits[1:]:
        sum_last.step(order)
    sum_late.settle(order)
    spans = (
        (0, half, 0, half),
        (1, 0, half, half),
        (0, half * 3 + quarter, 2 * half, half),
        (1, half + quarter, 3 * half, half),
        (0, 2 * half, 4 * half, quarter),
        (0, 4 * half + quarter, 4 * half + quarter, quarter),
        (1, half, 5 * half, quarter),
        (1, 2 * half + quarter, 5 * half + quarter, quarter),
    )
    vectors_at = 3 * half
    late = sum_late.total()
    reduced_out = jnp.concatenate([late[:, :half], late[:, 2 * half + quarter :][:, :half]], 1).T
    reduced_up = sum_up.total()
    reduced_down = sum_down.total().T
    mean_o, square_o, new_out = adam_step(
        w_out, reduced_out, mean_out, square_out, matrix_rate, weight_decay
    )
    mean_u, square_u, new_up = adam_step(
        w_up, reduced_up, mean_up, square_up, matrix_rate, weight_decay
    )
    mean_d, square_d, new_down = adam_step(
        w_down, reduced_down, mean_down, square_down, matrix_rate, weight_decay
    )
    if shard_width % 8 == 0:
        mean_q, square_q, new_qkv, mean_v, square_v, new_vectors = last_update(
            sum_late.pairs[0],
            sum_last.pairs[0],
            (spans, vectors_at),
            qkv_scale,
            (w_qkv, mean_qkv, square_qkv),
            col_shrink,
            (vectors, mean_vectors, square_vectors),
        )
    else:
        sums = (late, sum_last.total())
        reduced_qkv = jnp.concatenate(
            [sums[which][:, first : first + size] for which, first, _, size in spans], 1
        )
        mean_q, square_q, stepped_qkv = adam_step(
            w_qkv, reduced_qkv, mean_qkv, square_qkv, matrix_rate, weight_decay
        )
        new_qkv = stepped_qkv * qkv_scale
        reduced_vectors = sums[1][:, vectors_at : vectors_at + vector_count].T
        mean_v, square_v, stepped_vectors = adam_step(
            vectors, reduced_vectors, mean_vectors, square_vectors, vector_rate, 0.0
        )
        row_pick = (jnp.arange(vector_count, dtype=jnp.int32) == 4)[:, None]
        new_vectors = jnp.where(row_pick, stepped_vectors * col_shrink, stepped_vectors)
    return (
        result_out,
        token_grad,
        head_peak,
        mean_q,
        square_q,
        new_qkv,
        mean_o,
        square_o,
        new_out,
        mean_u,
        square_u,
        new_up,
        mean_d,
        square_d,
        new_down,
        mean_v,
        square_v,
        new_vectors,
    )


def solution(mesh):
    links = Links(mesh.shape["dp"], mesh.shape["fsdp"])
    return jax.shard_map(
        partial(local, links),
        mesh=mesh,
        in_specs=(
            P(("dp", "fsdp"), None, None),
            P(("dp", "fsdp"), None, None),
            P(("dp", "fsdp")),
            P(("dp", "fsdp"), None),
            P(None, ("dp", "fsdp")),
            P(("dp", "fsdp"), None),
            P(None, ("dp", "fsdp")),
            P(None, ("dp", "fsdp")),
            P(("dp", "fsdp"), None),
            P(None, ("dp", "fsdp")),
            P(("dp", "fsdp"), None),
            P(None, ("dp", "fsdp")),
            P(None, ("dp", "fsdp")),
            P(("dp", "fsdp"), None),
            P(None, ("dp", "fsdp")),
            P(("dp", "fsdp"), None),
            P(None, ("dp", "fsdp")),
            P(None, ("dp", "fsdp")),
        ),
        out_specs=(
            P(("dp", "fsdp"), None, None),
            P(("dp", "fsdp"), None, None),
            P(),
            P(("dp", "fsdp"), None),
            P(("dp", "fsdp"), None),
            P(("dp", "fsdp"), None),
            P(None, ("dp", "fsdp")),
            P(None, ("dp", "fsdp")),
            P(None, ("dp", "fsdp")),
            P(("dp", "fsdp"), None),
            P(("dp", "fsdp"), None),
            P(("dp", "fsdp"), None),
            P(None, ("dp", "fsdp")),
            P(None, ("dp", "fsdp")),
            P(None, ("dp", "fsdp")),
            P(None, ("dp", "fsdp")),
            P(None, ("dp", "fsdp")),
            P(None, ("dp", "fsdp")),
        ),
        check_vma=False,
    )
```

```python
from functools import partial

import jax
import jax.numpy as jnp
import numpy as np
from jax import lax
from jax.experimental import pallas as pl
from jax.experimental.pallas import tpu as pltpu
from jax.sharding import PartitionSpec as P

H = 16
STEP = 10


beta_one = 0.9
beta_two = 0.95
adam_epsilon = 1e-08
weight_decay = 0.1
matrix_rate = 0.1
vector_rate = 0.5
clip_limit = 8.0
norm_epsilon = 1e-06
masked_value = -1e30
TILE = 512
PAIR = 128
HALF_ROOT = 0.5**0.5
DENSITY = 0.3989422804014327
F32 = jnp.float32
BF16 = jnp.bfloat16


def adam_step(weight, gradient, mean_old, square_old, step_rate, decay_rate):
    mean_new = beta_one * mean_old + (1.0 - beta_one) * gradient
    square_new = beta_two * square_old + (1.0 - beta_two) * gradient * gradient
    fix_one = 1.0 - beta_one**STEP
    fix_two = 1.0 - beta_two**STEP
    stepped = weight - step_rate * (
        mean_new / fix_one / (jnp.sqrt(square_new / fix_two) + adam_epsilon) + decay_rate * weight
    )
    return (mean_new, square_new, stepped)


def bit_names(letter, count):
    return tuple(letter + str(at) for at in range(count))


class Links:
    def __init__(self, dp_count, inner_count):
        self.device_count = dp_count * inner_count
        inner_bits = inner_count.bit_length() - 1
        z_bits = bit_names("z", dp_count.bit_length() - 2)
        x_bits = bit_names("x", inner_bits // 2)
        y_bits = bit_names("y", inner_bits - inner_bits // 2)
        self.place = {"c": ("dp", dp_count, 0)}
        self.place.update({bit: ("dp", dp_count, at + 1) for at, bit in enumerate(z_bits)})
        self.place.update({bit: ("fsdp", inner_count, at) for at, bit in enumerate(x_bits)})
        self.place.update(
            {bit: ("fsdp", inner_count, at + len(x_bits)) for at, bit in enumerate(y_bits)}
        )
        self.bits = ("c",) + y_bits + x_bits + z_bits
        self.orders = (y_bits + x_bits, x_bits + y_bits)
        self.z_bits = z_bits
        self.y_bits = y_bits
        self.inner_bits = inner_bits

    def true_block(self):
        masks = []
        for block in range(self.device_count):
            mask = 0
            for at, bit in enumerate(reversed(self.bits)):
                if block >> at & 1:
                    axis, _, place = self.place[bit]
                    mask |= 1 << (place + (self.inner_bits if axis == "dp" else 0))
            masks.append(mask)
        return lax.axis_index(("dp", "fsdp")) ^ jnp.array(masks, jnp.int32)

    def exchange(self, values, *bits):
        axis, count, _ = self.place[bits[0]]
        mask = sum(1 << self.place[bit][2] for bit in bits)
        return lax.ppermute(values, axis, [(at, at ^ mask) for at in range(count)])


class Order:
    def __init__(self):
        self.ended = ()

    def __call__(self, call, *operands):
        operands, _ = lax.optimization_barrier((operands, self.ended))
        result = call(*operands)
        self.ended = result
        return result

    def settle(self, value):
        return self(lambda come: come, value)


def run(body, operands, outs, grid=(), in_specs=None, out_specs=None, scratch=()):
    whole = pl.BlockSpec(memory_space=pltpu.VMEM)
    return pl.pallas_call(
        body,
        out_shape=[
            pltpu.HBM(shape, kind) if hbm else jax.ShapeDtypeStruct(shape, kind)
            for shape, kind, *hbm in outs
        ],
        grid=grid,
        in_specs=in_specs or [whole] * len(operands),
        out_specs=out_specs or [whole] * len(outs),
        scratch_shapes=scratch,
        compiler_params=pltpu.CompilerParams(vmem_limit_bytes=12 * 2**20),
        cost_estimate=pl.CostEstimate(flops=30 * 10**9, bytes_accessed=1000, transcendentals=0),
    )(*operands)


def fixed(shape):
    return pl.BlockSpec(shape, lambda j: (0,) * len(shape))


def mm(first, second):
    return lax.dot_general(first, second, (((1,), (0,)), ((), ())), preferred_element_type=F32)


def mm_turned(first, second):
    return lax.dot_general(first, second, (((1,), (1,)), ((), ())), preferred_element_type=F32)


def mm_rows(first, second):
    return lax.dot_general(first, second, (((0,), (0,)), ((), ())), preferred_element_type=F32)


def pieces(values, count=3):
    out = []
    for _ in range(count):
        piece = values.astype(BF16)
        out.append(piece)
        values = values - piece.astype(F32)
    return out


def normalized(values):
    centered = values - jnp.mean(values, -1, keepdims=True)
    scale = lax.rsqrt(jnp.mean(centered * centered, -1, keepdims=True) + norm_epsilon)
    return centered * scale, scale


def norm_back(grad, values, gain):
    unit, scale = normalized(values)
    inner = grad * gain
    d_values = scale * (
        inner
        - jnp.mean(inner, -1, keepdims=True)
        - unit * jnp.mean(inner * unit, -1, keepdims=True)
    )
    return (
        d_values,
        jnp.sum(grad * unit, 0, keepdims=True),
        jnp.sum(grad, 0, keepdims=True),
    )


def first_norm(inputs, mine, other, to_relative):
    rows, width = inputs.shape
    half = width // 2

    def body(
        x_ref, mine_ref, other_ref, turn_ref, low_ref, high_ref, lowt_ref, hight_ref, rel_ref, true_ref
    ):
        turned = jnp.concatenate(
            [mine_ref[...].astype(F32).T, other_ref[...].astype(F32).T], 1
        )[:16]
        rel_ref[...] = turned
        true_ref[...] = mm_turned(turned.astype(BF16), turn_ref[...])
        unit, _ = normalized(x_ref[...].astype(F32))
        normed = (unit * turned[0:1] + turned[1:2]).astype(BF16)
        low_ref[...] = normed[:, :half]
        high_ref[...] = normed[:, half:]
        lowt_ref[...] = normed[:, :half].T
        hight_ref[...] = normed[:, half:].T

    vectors_at = mine.shape[1] // PAIR - 1
    weights = pl.BlockSpec((half, PAIR), lambda j: (0, vectors_at))
    return run(
        body,
        (inputs, mine, other, to_relative),
        [((rows, half), BF16)] * 2 + [((half, rows), BF16)] * 2 + [((16, width), F32)] * 2,
        (1,),
        [fixed(inputs.shape), weights, weights, fixed(to_relative.shape)],
        [fixed((rows, half))] * 2 + [fixed((half, rows))] * 2 + [fixed((16, width))] * 2,
    )


def project(at, low, high, mine, other, true_vectors):
    rows, half = low.shape

    def body(low_ref, high_ref, mine_ref, other_ref, vec_ref, out_ref):
        j = pl.program_id(0)
        bias = jnp.where(j == 0, vec_ref[4:5, :], jnp.where(j == 2, vec_ref[5:6, :], 0.0))
        value = mm(low_ref[...], mine_ref[...]) + mm(high_ref[...], other_ref[...])
        out_ref[0] = (value + bias).astype(BF16)

    weights = pl.BlockSpec((half, TILE), lambda j: (0, j))
    return run(
        body,
        (low, high, mine, other, true_vectors),
        [((3, rows, TILE), BF16)],
        (3,),
        [fixed(low.shape)] * 2 + [weights] * 2 + [pl.BlockSpec((16, TILE), lambda j: (0, at))],
        [pl.BlockSpec((1, rows, TILE), lambda j: (j, 0, 0))],
    )[0]


def head_mask(rows, side):
    lane = lax.broadcasted_iota(jnp.int32, (rows, PAIR), 1)
    return lane < PAIR // 2 if side == 0 else lane >= PAIR // 2


def attend(projected, counts):
    _, rows, width = projected[0].shape
    steps = width // PAIR

    def body(count_ref, *refs):
        *ins, out_ref, peak_ref = refs
        j = pl.program_id(0)

        def heads(q_ref, k_ref, v_ref):
            count = count_ref[0]
            key_ok = lax.broadcasted_iota(jnp.int32, (rows, rows), 1) < count
            row_ok = lax.broadcasted_iota(jnp.int32, (rows, 1), 0) < count
            queries = q_ref[0]
            out = None
            for side in (0, 1):
                chosen = head_mask(rows, side)
                scores = mm_turned(jnp.where(chosen, queries, 0), k_ref[0]) * (PAIR // 2) ** -0.5
                scores = jnp.where(key_ok, scores, masked_value)
                top = jnp.max(scores, -1, keepdims=True)
                peak = jnp.max(jnp.where(row_ok, top, masked_value))
                peak_ref[pl.ds(j * 2 + side, 1), :] = jnp.full((1, PAIR), peak)
                exponent = jnp.exp(scores - top)
                probs = exponent * (1.0 / jnp.sum(exponent, -1, keepdims=True))
                value = mm(probs.astype(BF16), v_ref[0])
                out = value if side == 0 else jnp.where(chosen, value, out)
            out_ref[...] = out.astype(BF16)

        @pl.when(j < steps)
        def _():
            heads(*ins[:3])

        @pl.when(j >= steps)
        def _():
            heads(*ins[3:])

    def part(index, at):
        return pl.BlockSpec(
            (1, rows, PAIR), lambda j: (index, 0, jnp.clip(j - at * steps, 0, steps - 1))
        )

    return run(
        body,
        (counts, *[projected[0]] * 3, *[projected[1]] * 3),
        [((rows, 2 * width), BF16), ((4 * steps, PAIR), F32)],
        (2 * steps,),
        [pl.BlockSpec(memory_space=pltpu.SMEM)]
        + [part(index, at) for at in (0, 1) for index in range(3)],
        [pl.BlockSpec((rows, PAIR), lambda j: (0, j)), fixed((4 * steps, PAIR))],
    )


def attend_back(projected, d_out, counts):
    _, rows, width = projected.shape
    steps = width // PAIR
    scale = (PAIR // 2) ** -0.5

    def body(count_ref, q_ref, k_ref, v_ref, d_ref, out_ref, sum_ref):
        key_ok = lax.broadcasted_iota(jnp.int32, (rows, rows), 0) < count_ref[0]
        queries, keys, values, grad = q_ref[0], k_ref[0], v_ref[0], d_ref[...]
        parts = [None] * 3
        for side in (0, 1):
            chosen = head_mask(rows, side)
            scores = mm_turned(jnp.where(chosen, keys, 0), queries) * scale
            scores = jnp.where(key_ok, scores, masked_value)
            exponent = jnp.exp(scores - jnp.max(scores, 0, keepdims=True))
            probs = exponent * (1.0 / jnp.sum(exponent, 0, keepdims=True))
            d_probs = mm_turned(jnp.where(chosen, values, 0), grad)
            inner = jnp.sum(probs * d_probs, 0, keepdims=True)
            d_scores = (probs * (d_probs - inner)).astype(BF16)
            new = [
                mm_rows(d_scores, keys) * scale,
                mm(d_scores, queries) * scale,
                mm(probs.astype(BF16), grad),
            ]
            parts = new if side == 0 else [jnp.where(chosen, n, p) for n, p in zip(new, parts)]
        low = [part.astype(BF16) for part in parts]
        for at in range(3):
            out_ref[at] = low[at]
        sum_ref[0:1, :] = jnp.sum(low[0].astype(F32), 0, keepdims=True)
        sum_ref[1:2, :] = jnp.sum(low[2].astype(F32), 0, keepdims=True)

    def part(index):
        return pl.BlockSpec((1, rows, PAIR), lambda j: (index, 0, j))

    columns = pl.BlockSpec((rows, PAIR), lambda j: (0, j))
    return run(
        body,
        (counts, projected, projected, projected, d_out),
        [((3, rows, width), BF16), ((8, width), F32)],
        (steps,),
        [pl.BlockSpec(memory_space=pltpu.SMEM), part(0), part(1), part(2), columns],
        [
            pl.BlockSpec((3, rows, PAIR), lambda j: (0, 0, j)),
            pl.BlockSpec((8, PAIR), lambda j: (0, j)),
        ],
    )


def second_norm(inputs, attended, weights, vectors):
    rows, width = inputs.shape
    half = width // 2

    def body(x_ref, a_ref, b_ref, wa_ref, wa2_ref, wb_ref, wb2_ref, vec_ref, mid_ref, low_ref, high_ref, lowt_ref, hight_ref):
        first, second = a_ref[...], b_ref[...]
        branch = jnp.concatenate(
            [
                mm_turned(first, wa_ref[...]) + mm_turned(second, wb_ref[...]),
                mm_turned(first, wa2_ref[...]) + mm_turned(second, wb2_ref[...]),
            ],
            1,
        )
        middle = x_ref[...].astype(F32) + branch + vec_ref[6:7, :]
        mid_ref[...] = middle
        unit, _ = normalized(middle)
        normed = (unit * vec_ref[2:3, :] + vec_ref[3:4, :]).astype(BF16)
        low_ref[...] = normed[:, :half]
        high_ref[...] = normed[:, half:]
        lowt_ref[...] = normed[:, :half].T
        hight_ref[...] = normed[:, half:].T

    block = pl.BlockSpec((half, TILE), lambda j: (0, 0))
    return run(
        body,
        (inputs, attended, attended, *weights[0], *weights[1], vectors),
        [((rows, width), F32)] + [((rows, half), BF16)] * 2 + [((half, rows), BF16)] * 2,
        (1,),
        [fixed(inputs.shape)]
        + [pl.BlockSpec((rows, TILE), lambda j, at=at: (0, at)) for at in (0, 1)]
        + [block] * 4
        + [fixed(vectors.shape)],
        [fixed((rows, width))] + [fixed((rows, half))] * 2 + [fixed((half, rows))] * 2,
    )


def expand(at, low, high, mine, other, true_vectors):
    rows, half = low.shape
    count = mine.shape[1] - TILE
    per_row = true_vectors.shape[1] // TILE
    first_row = 8 + at * count // true_vectors.shape[1]

    def body(low_ref, high_ref, mine_ref, other_ref, vec_ref, out_ref, slope_ref):
        row = first_row + pl.program_id(0) // per_row
        pre = mm(low_ref[...], mine_ref[...]) + mm(high_ref[...], other_ref[...])
        pre = pre + vec_ref[pl.ds(row, 1), :]
        below = 0.5 * (1.0 + lax.erf(pre * HALF_ROOT))
        out_ref[...] = (pre * below).astype(BF16)
        slope = below + pre * (DENSITY * jnp.exp(-0.5 * pre * pre))
        slope_ref[...] = slope.astype(BF16)

    weights = pl.BlockSpec((half, TILE), lambda j: (0, j + 1))
    columns = pl.BlockSpec((rows, TILE), lambda j: (0, j))
    return run(
        body,
        (low, high, mine, other, true_vectors),
        [((rows, count), BF16), ((rows, count), BF16, "hbm")],
        (count // TILE,),
        [fixed(low.shape)] * 2
        + [weights] * 2
        + [pl.BlockSpec((16, TILE), lambda j: (0, j % per_row))],
        [columns, columns],
    )


def among(count, at, shape):
    return pl.BlockSpec(shape, lambda j: (0, jnp.clip(j - at * count, 0, count - 1)))


def expand_back(grads, weights, slopes):
    rows = slopes[0].shape[0]
    steps = slopes[0].shape[1] // TILE
    counts = [len(pieces) for pieces in weights]
    operands, specs = [], []
    for at, (lefts, rights) in enumerate(zip(grads, weights)):
        operands += [*lefts, *rights]
        specs += [fixed(left.shape) for left in lefts]
        specs += [among(steps, at, (right.shape[0], TILE)) for right in rights]

    def body(*refs):
        *ins, first_slope, second_slope, out_ref, sum_ref = refs
        j = pl.program_id(0)
        for at, slope_ref in enumerate((first_slope, second_slope)):
            first = 2 * sum(counts[:at])
            lefts, rights = ins[first : first + counts[at]], ins[first + counts[at] :][: counts[at]]

            @pl.when(j // steps == at)
            def _(lefts=lefts, rights=rights, slope_ref=slope_ref):
                value = sum(mm(left[...], right[...]) for left, right in zip(lefts, rights))
                value = (value * slope_ref[...].astype(F32)).astype(BF16)
                out_ref[...] = value
                sum_ref[...] = jnp.sum(value.astype(F32), 0, keepdims=True)

    count = 2 * steps
    return run(
        body,
        (*operands, *slopes),
        [((rows, count * TILE), BF16), ((1, count * TILE), F32)],
        (count,),
        specs + [among(steps, at, (rows, TILE)) for at in range(2)],
        [pl.BlockSpec((rows, TILE), lambda j: (0, j)), pl.BlockSpec((1, TILE), lambda j: (0, j))],
    )


def contract_first(d_pre, mine, other):
    rows, count = d_pre.shape
    half = mine.shape[0]
    count = count // 2

    def body(d_ref, mine_ref, other_ref, out_ref):
        @pl.when(pl.program_id(0) == 0)
        def _():
            out_ref[...] = jnp.zeros_like(out_ref)

        out_ref[:, :half] += mm_turned(d_ref[...], mine_ref[...])
        out_ref[:, half:] += mm_turned(d_ref[...], other_ref[...])

    weights = pl.BlockSpec((half, TILE), lambda j: (0, j + 1))
    return run(
        body,
        (d_pre, mine, other),
        [((rows, 2 * half), F32)],
        (count // TILE,),
        [pl.BlockSpec((rows, TILE), lambda j: (0, j)), weights, weights],
        [fixed((rows, 2 * half))],
    )[0]


def contract_second(d_pre, weights, partial_sum, middle, d_result, vectors):
    rows, count = d_pre.shape
    half = weights[0][0].shape[0]
    width = 2 * half
    steps = count // 2 // TILE

    def body(
        d_ref, mine_ref, other_ref, wa_ref, wa2_ref, wb_ref, wb2_ref, sum_ref, mid_ref, res_ref,
        vec_ref, dm_ref, low_ref, high_ref, outa_ref, outb_ref, grads_ref, total,
    ):
        j = pl.program_id(0)

        @pl.when(j == 0)
        def _():
            total[...] = sum_ref[...]

        total[:, :half] += mm_turned(d_ref[...], mine_ref[...])
        total[:, half:] += mm_turned(d_ref[...], other_ref[...])

        @pl.when(j == steps - 1)
        def _():
            d_values, d_gain, d_shift = norm_back(total[...], mid_ref[...], vec_ref[2:3, :])
            result_grad = res_ref[...].astype(F32)
            d_middle = result_grad + d_values
            branch = d_middle.astype(BF16)
            dm_ref[...] = d_middle
            first, second = branch[:, :half], branch[:, half:]
            low_ref[...] = first.T
            high_ref[...] = second.T
            outa_ref[...] = (mm(first, wa_ref[...]) + mm(second, wa2_ref[...])).astype(BF16)
            outb_ref[...] = (mm(first, wb_ref[...]) + mm(second, wb2_ref[...])).astype(BF16)
            grads_ref[0:1, :] = d_gain
            grads_ref[1:2, :] = d_shift
            grads_ref[2:3, :] = jnp.sum(branch.astype(F32), 0, keepdims=True)
            grads_ref[3:4, :] = jnp.sum(result_grad, 0, keepdims=True)

    tile = pl.BlockSpec((half, TILE), lambda j: (0, j + 1))
    block = pl.BlockSpec((half, TILE), lambda j: (0, 0))
    return run(
        body,
        (d_pre, *weights[1], *weights[0], *weights[1], partial_sum, middle, d_result, vectors),
        [((rows, width), F32)]
        + [((half, rows), BF16)] * 2
        + [((rows, TILE), BF16)] * 2
        + [((8, width), F32)],
        (steps,),
        [pl.BlockSpec((rows, TILE), lambda j: (0, steps + j)), tile, tile]
        + [block] * 4
        + [fixed((rows, width))] * 3
        + [fixed(vectors.shape)],
        [fixed((rows, width))]
        + [fixed((half, rows))] * 2
        + [fixed((rows, TILE))] * 2
        + [fixed((8, width))],
        [pltpu.VMEM((rows, width), F32)],
    )


def input_back_first(d_projected, mine, other):
    rows = d_projected.shape[1]
    half = mine.shape[0]

    def body(d_ref, mine_ref, other_ref, out_ref):
        @pl.when(pl.program_id(0) == 0)
        def _():
            out_ref[...] = jnp.zeros_like(out_ref)

        out_ref[:, :half] += mm_turned(d_ref[0], mine_ref[...])
        out_ref[:, half:] += mm_turned(d_ref[0], other_ref[...])

    weights = pl.BlockSpec((half, TILE), lambda j: (0, j))
    return run(
        body,
        (d_projected, mine, other),
        [((rows, 2 * half), F32)],
        (3,),
        [pl.BlockSpec((1, rows, TILE), lambda j: (j, 0, 0)), weights, weights],
        [fixed((rows, 2 * half))],
    )[0]


def input_back_second(
    d_projected, mine, other, partial_sum, inputs, d_middle, grads, head_sums, d_pre_sums, vectors, to_relative
):
    rows = d_projected.shape[1]
    half = mine.shape[0]
    width = 2 * half

    def body(
        d_ref, mine_ref, other_ref, sum_ref, x_ref, dm_ref, grads_ref, heada_ref, headb_ref, pre_ref,
        vec_ref, turn_ref, out_ref, low_ref, high_ref, total, true_rows, all_rows,
    ):
        j = pl.program_id(0)

        @pl.when(j == 0)
        def _():
            total[...] = sum_ref[...]

        total[:, :half] += mm_turned(d_ref[0], mine_ref[...])
        total[:, half:] += mm_turned(d_ref[0], other_ref[...])

        @pl.when(j == 2)
        def _():
            d_values, d_gain, d_shift = norm_back(total[...], x_ref[...].astype(F32), vec_ref[0:1, :])
            low = (dm_ref[...] + d_values).astype(BF16)
            out_ref[...] = mm_turned(low, turn_ref[...]).astype(BF16)
            true_rows[...] = jnp.zeros_like(true_rows)
            for at, ref in enumerate((heada_ref, headb_ref)):
                true_rows[0:2, at * TILE : (at + 1) * TILE] = ref[0:2, :]
            for part in range(pre_ref.shape[1] // width):
                row = 2 + part
                true_rows[row : row + 1, :] = pre_ref[:, part * width : (part + 1) * width]
            turned = sum(mm(part, turn_ref[...]) for part in pieces(true_rows[...]))
            all_rows[...] = jnp.zeros_like(all_rows)
            all_rows[0:1, :] = d_gain
            all_rows[1:2, :] = d_shift
            all_rows[2:4, :] = grads_ref[0:2, :]
            all_rows[4:6, :] = turned[0:2]
            all_rows[6:8, :] = grads_ref[2:4, :]
            all_rows[8:14, :] = turned[2:8]
            columns = all_rows[...].T
            low_ref[...] = columns[:half]
            high_ref[...] = columns[half:]

    weights = pl.BlockSpec((half, TILE), lambda j: (0, j))
    operands = (
        d_projected,
        mine,
        other,
        partial_sum,
        inputs,
        d_middle,
        grads,
        *head_sums,
        d_pre_sums,
        vectors,
        to_relative,
    )
    return run(
        body,
        operands,
        [((rows, width), BF16)] + [((half, PAIR), F32)] * 2,
        (3,),
        [pl.BlockSpec((1, rows, TILE), lambda j: (j, 0, 0)), weights, weights]
        + [fixed(operand.shape) for operand in operands[3:]],
        [fixed((rows, width))] + [fixed((half, PAIR))] * 2,
        [pltpu.VMEM((rows, width), F32), pltpu.VMEM((8, width), F32), pltpu.VMEM((PAIR, width), F32)],
    )


def contract_hidden(hidden, weights, ranges, total):
    for ref, places in zip(weights, ranges):
        value = mm_turned(hidden[...], ref[...])
        first = 0
        for low, high in places:
            total[:, low:high] += value[:, first : first + high - low]
            first += high - low


def finish_first(middle, hidden, weights, vectors, ranges):
    rows, width = middle.shape
    steps = hidden.shape[1] // TILE

    def body(hidden_ref, *refs):
        *weight_refs, mid_ref, vec_ref, out_ref = refs

        @pl.when(pl.program_id(0) == 0)
        def _():
            out_ref[...] = mid_ref[...] + vec_ref[7:8, :]

        contract_hidden(hidden_ref, weight_refs, ranges, out_ref)

    columns = pl.BlockSpec((rows, TILE), lambda j: (0, j))
    return run(
        body,
        (hidden, *weights, middle, vectors),
        [((rows, width), F32)],
        (steps,),
        [columns]
        + [pl.BlockSpec((right.shape[0], TILE), lambda j: (0, j)) for right in weights]
        + [fixed((rows, width)), fixed(vectors.shape)],
        [fixed((rows, width))],
    )[0]


def finish_second(partial_sum, hidden, weights, to_relative, counts, ranges):
    rows, width = partial_sum.shape
    steps = hidden.shape[1] // TILE

    def body(count_ref, hidden_ref, *refs):
        *weight_refs, sum_ref, turn_ref, out_ref, total = refs

        @pl.when(pl.program_id(0) == 0)
        def _():
            total[...] = sum_ref[...]

        contract_hidden(hidden_ref, weight_refs, ranges, total)

        @pl.when(pl.program_id(0) == steps - 1)
        def _():
            kept = lax.broadcasted_iota(jnp.int32, (rows, 1), 0) < count_ref[0]
            low = jnp.where(kept, total[...], 0.0).astype(BF16)
            out_ref[...] = mm_turned(low, turn_ref[...]).astype(BF16)

    columns = pl.BlockSpec((rows, TILE), lambda j: (0, j))
    return run(
        body,
        (counts, hidden, *weights, partial_sum, to_relative),
        [((rows, width), BF16)],
        (steps,),
        [pl.BlockSpec(memory_space=pltpu.SMEM), columns]
        + [pl.BlockSpec((right.shape[0], TILE), lambda j: (0, j)) for right in weights]
        + [fixed((rows, width)), fixed(to_relative.shape)],
        [fixed((rows, width))],
        [pltpu.VMEM((rows, width), F32)],
    )[0]


def product(slowest, tiles, extra=()):
    count, rows = tiles[0][0].shape
    operands, specs = [], []
    for *both, width, place in tiles:
        operands += both
        specs += [fixed((count, rows))] * 2
        shape = (1,) * (len(place) - 2) + (rows, width)
        specs += [pl.BlockSpec(shape, lambda j, place=place: place)] * 2
    width = sum(tile[4] for tile in tiles)
    full = width + (extra[0].shape[1] if extra else 0)
    operands += extra
    specs += [fixed(operand.shape) for operand in extra]

    def body(*refs):
        *ins, sent_ref, kept_ref = refs
        first = 0
        for at, tile in enumerate(tiles):
            left, left_other, right, right_other = (
                ref[0] if len(ref.shape) == 3 else ref[...] for ref in ins[4 * at : 4 * at + 4]
            )
            value = (mm(left, right) + mm(left_other, right_other)).astype(BF16)
            columns = slice(first, first + tile[4])
            first += tile[4]
            cut_rows(value, slowest, sent_ref, kept_ref, columns)
        if extra:
            value = (ins[-2][...] + ins[-1][...]).astype(BF16)
            cut_rows(value, slowest, sent_ref, kept_ref, slice(width, full))

    out = (count // 2, full)
    return run(body, operands, [(out, BF16)] * 2, (1,), specs, [fixed(out)] * 2)


def cut_rows(value, slowest, sent_ref, kept_ref, columns):
    part = value.shape[0] // 2 // slowest
    for group in range(slowest):
        low = 2 * group * part
        rows = slice(group * part, (group + 1) * part)
        kept_ref[rows, columns] = value[low : low + part]
        sent_ref[rows, columns] = value[low + part : low + 2 * part]


def product_wide(slowest, first, width, left, left_other, right, right_other):
    rows = right.shape[0]
    count = left.shape[0]

    def body(left_ref, left_other_ref, right_ref, right_other_ref, sent_ref, kept_ref):
        value = mm(left_ref[...], right_ref[...]) + mm(left_other_ref[...], right_other_ref[...])
        cut_rows(value.astype(BF16), slowest, sent_ref, kept_ref, slice(None))

    columns = pl.BlockSpec((rows, TILE), lambda j: (0, first // TILE + j))
    out_columns = pl.BlockSpec((count // 2, TILE), lambda j: (0, j))
    return run(
        body,
        (left, left_other, right, right_other),
        [((count // 2, width), BF16, "hbm")] * 2,
        (width // TILE,),
        [fixed(left.shape)] * 2 + [columns] * 2,
        [out_columns] * 2,
    )


def added(first, second, kind=BF16):
    return (first.astype(F32) + second.astype(F32)).astype(kind)


def halved(pairs, joined):
    half = pairs[0][0].shape[0] // 2
    widths = [mine.shape[1] for mine, _ in pairs]
    if half % 16:
        totals = [added(*pair) for pair in pairs]
        if joined:
            totals = [jnp.concatenate(totals, 1)]
        return [(total[half:], total[:half]) for total in totals]

    def body(*refs):
        ins, outs = refs[: 2 * len(pairs)], refs[2 * len(pairs) :]
        for at in range(len(pairs)):
            mine, got = ins[2 * at], ins[2 * at + 1]
            sent_ref, kept_ref = outs[:2] if joined else outs[2 * at : 2 * at + 2]
            first = sum(widths[:at]) if joined else 0
            columns = slice(first, first + widths[at])
            sent_ref[:, columns] = added(mine[half:, :], got[half:, :])
            kept_ref[:, columns] = added(mine[:half, :], got[:half, :])

    out_widths = [sum(widths)] if joined else widths
    outs = [((half, width), BF16) for width in out_widths for _ in range(2)]
    outs = run(body, [v for pair in pairs for v in pair], outs)
    return [tuple(outs[at : at + 2]) for at in range(0, len(outs), 2)]


def joined(places, middle, count, mine, got):
    wide = mine[0].shape[-1] if len(mine) == 1 else sum(value.shape[-1] for value in mine)
    parts = (slice(0, middle), slice(middle, wide))
    pairs = list(zip(places, mine, got))
    shapes = [(*value.shape[:at], 2, *value.shape[at:]) for at, value, _ in pairs]

    def widths(shape):
        if count == 1:
            return [(*shape[:-1], wide)]
        return [(*shape[:-1], part.stop - part.start) for part in parts]

    out_shapes = shapes if len(mine) == count else widths(shapes[0])
    if mine[0].shape[-2] % 16:
        both = [jnp.stack([value, come], at) for at, value, come in pairs]
        if len(mine) == count:
            return both
        if count == 1:
            rest = both[0].shape[:-1]
            return [jnp.concatenate([value.reshape(*rest, -1) for value in both], -1)]
        return [both[0][..., part] for part in parts]

    def body(*refs):
        outs = refs[2 * len(mine) :]
        for at, (place, value, _) in enumerate(pairs):
            for side in (0, 1):
                ref = refs[at + side * len(mine)]
                lead = (slice(None),) * place + (side,) + (slice(None),) * (value.ndim - 1 - place)
                if len(mine) == count:
                    outs[at][(*lead, slice(None))] = ref[...]
                elif count == 1:
                    outs[0][(*lead, parts[at])] = ref[...]
                else:
                    for out_ref, part in zip(outs, parts):
                        out_ref[(*lead, slice(None))] = ref[..., part]

    return run(body, [*mine, *got], [(shape, BF16) for shape in out_shapes])


def joined_all(bits, middle, blocks):
    rows, wide = blocks[0].shape
    parts = (slice(0, middle), slice(middle, wide))
    shape = (2,) * bits
    if rows % 16:
        whole = jnp.stack(blocks).reshape(*shape, rows, wide)
        return [whole[..., part] for part in parts]

    def body(*refs):
        for at, ref in enumerate(refs[: len(blocks)]):
            lead = tuple(at >> (bits - 1 - bit) & 1 for bit in range(bits))
            for out_ref, part in zip(refs[len(blocks) :], parts):
                out_ref[(*lead, slice(None), slice(None))] = ref[:, part]

    return run(
        body, blocks, [((*shape, rows, part.stop - part.start), BF16) for part in parts]
    )


class Sum:
    def __init__(self, links, firsts):
        self.links = links
        self.left, self.pairs = [], []
        self.z_left = links.z_bits
        for parts, order in zip(firsts, links.orders):
            self.add(parts, order)

    def add(self, parts, order):
        sent, kept = parts
        self.left.append(order[1:])
        self.pairs.append((kept, self.links.exchange(sent, order[0])))

    def step(self, order):
        inner = bool(self.left[0])
        joined = not inner and len(self.pairs) > 1
        parts = order(partial(halved, joined=joined), self.pairs)
        if inner:
            bits = [left[0] for left in self.left]
            self.left = [left[1:] for left in self.left]
        else:
            bits = [self.z_left[0]]
            self.z_left = self.z_left[1:]
        self.pairs = [
            (kept, self.links.exchange(sent, bit)) for (sent, kept), bit in zip(parts, bits)
        ]

    def settle(self, order):
        self.pairs = [(kept, order.settle(got)) for kept, got in self.pairs]

    def total(self):
        return added(*self.pairs[0], F32)


class Gather:
    def __init__(self, links, shards, middle, at_once=False):
        self.links, self.middle = links, middle
        steps = [tuple(reversed(order)) for order in links.orders]
        steps = list(zip(*steps))
        between = len(steps) // 2 if len(shards) == 2 else 0
        z_steps = ["all z"] if at_once else [(bit,) for bit in reversed(links.z_bits)]
        self.steps = steps[:between] + z_steps + steps[between:] + [("c", "c")]
        self.blocks = list(shards)
        self.bits = [(), ()]
        self.send()

    def send(self):
        if self.steps[0] == "all z":
            z_bits = self.links.z_bits
            chosen = [
                [bit for at, bit in enumerate(z_bits) if block >> (len(z_bits) - 1 - at) & 1]
                for block in range(1, 2 ** len(z_bits))
            ]
            self.got = [self.links.exchange(self.blocks[0], *bits) for bits in chosen]
            return
        self.got = [
            self.links.exchange(block, bit) for block, bit in zip(self.blocks, self.steps[0])
        ]

    def join(self, order):
        done, *self.steps = self.steps
        if done == "all z":
            z_bits = self.links.z_bits
            self.bits = [z_bits, z_bits]
            self.blocks = order(
                partial(joined_all, len(z_bits), self.middle), [*self.blocks, *self.got]
            )
            return
        bits = done * 2 if len(done) == 1 else done
        places = []
        for at, bit in enumerate(bits):
            held = sorted((*self.bits[at], bit), key=self.links.bits.index)
            self.bits[at] = tuple(held)
            places.append(held.index(bit))
        self.blocks = order(
            partial(joined, places, self.middle, len(self.steps[0])), self.blocks, self.got
        )
        if self.steps[0][0] == "c":
            self.blocks = [block.reshape(-1, block.shape[-1]) for block in self.blocks]

    def step(self, order):
        self.join(order)
        self.send()

    def settle(self, order):
        self.got = order.settle(self.got)

    def core_early(self, order):
        self.blocks = order.settle(self.blocks)
        self.early = [self.links.exchange(block, "c") for block in self.blocks]

    def core_late(self, order):
        self.got = order.settle(self.got)
        self.late = [self.links.exchange(got, "c") for got in self.got]

    def pieces(self):
        return [
            [values.reshape(-1, values.shape[-1]) for values in four]
            for four in zip(self.blocks, self.got, self.early, self.late)
        ]

    def halves(self):
        return list(zip(self.blocks, self.got))


def last_update(late, last, spans, scale, moments, vector_scale, vector_moments):
    spans, vectors_at = spans
    rows, width = moments[0].shape
    count = vector_moments[0].shape[0]

    def body(*refs):
        late_kept, late_got, last_kept, last_got, scale_ref = refs[:5]
        weight_ref, mean_ref, square_ref, vscale_ref, vector_ref, vmean_ref, vsquare_ref = refs[5:12]
        outs = refs[12:]
        sums = [added(late_kept[...], late_got[...], F32), added(last_kept[...], last_got[...], F32)]
        for of_last, first, place, size in spans:
            columns = slice(place, place + size)
            mean, square, stepped = adam_step(
                weight_ref[:, columns],
                sums[of_last][:, first : first + size],
                mean_ref[:, columns],
                square_ref[:, columns],
                matrix_rate,
                weight_decay,
            )
            outs[0][:, columns] = mean
            outs[1][:, columns] = square
            outs[2][:, columns] = stepped * scale_ref[:, columns]
        grads = sums[1][:, vectors_at : vectors_at + PAIR].T[:count]
        mean, square, stepped = adam_step(
            vector_ref[...], grads, vmean_ref[...], vsquare_ref[...], vector_rate, 0.0
        )
        outs[3][...] = mean
        outs[4][...] = square
        row = lax.broadcasted_iota(jnp.int32, stepped.shape, 0)
        outs[5][...] = jnp.where(row == 4, stepped * vscale_ref[...], stepped)

    return run(
        body,
        (*late, *last, scale, *moments, vector_scale, *vector_moments),
        [((rows, width), F32)] * 3 + [(vector_moments[0].shape, F32)] * 3,
    )


def local(
    links,
    tokens,
    cotangent,
    counts,
    w_qkv,
    w_out,
    w_up,
    w_down,
    vectors,
    mean_qkv,
    mean_out,
    mean_up,
    mean_down,
    mean_vectors,
    square_qkv,
    square_out,
    square_up,
    square_down,
    square_vectors,
):
    seq_count, slot_count, model_width = tokens.shape
    rows = seq_count * slot_count
    head_width = model_width // H
    wide = w_down.shape[0]
    vector_count, shard_width = vectors.shape
    half = model_width // 2
    order = Order()

    low_qkv = w_qkv.astype(BF16)
    thirds = [low_qkv[:, at * half : (at + 1) * half] for at in range(6)]
    shard_vectors = jnp.pad(vectors.astype(BF16).T, ((0, 0), (0, PAIR - vector_count)))
    shard_qkv = jnp.concatenate([*thirds[0::2], shard_vectors, *thirds[1::2]], 1)
    low_out, low_up = w_out.astype(BF16).T, w_up.astype(BF16)
    shard_up = jnp.concatenate(
        [low_out[:, :half], low_up[:, : wide // 2], low_out[:, half:], low_up[:, wide // 2 :]], 1
    )
    shard_down = w_down.astype(BF16).T
    gather_qkv = Gather(links, [shard_qkv], 3 * half + PAIR, True)
    gather_down = Gather(
        links, [shard_down[:, : wide // 2], shard_down[:, wide // 2 :]], wide // 2
    )

    true_rows = (
        links.true_block()[:, None] * shard_width + jnp.arange(shard_width, dtype=jnp.int32)
    ).reshape(1, model_width)
    to_relative = (
        lax.broadcasted_iota(jnp.int32, (model_width, model_width), 0) == true_rows
    ).astype(BF16)
    keep_rows = lax.broadcasted_iota(jnp.int32, (rows, 1), 0) < counts[0]
    d_result = jnp.where(keep_rows, cotangent.reshape(rows, model_width), 0).astype(BF16)
    inputs = mm(tokens.reshape(rows, model_width), to_relative).astype(BF16)
    d_result_turned = mm(d_result, to_relative).astype(BF16)
    d_columns = lax.dot_general(
        to_relative, d_result, (((0,), (1,)), ((), ())), preferred_element_type=F32
    ).astype(BF16)

    def longer(gather, count):
        while len(gather.steps) > count:
            gather.step(order)

    inputs, d_result_turned, d_columns, to_relative = order.settle(
        (inputs, d_result_turned, d_columns, to_relative)
    )
    longer(gather_qkv, 4)
    gather_down.settle(order)
    d_other = order.settle(links.exchange(d_columns[half:], "c"))
    d_mine = d_columns[:half]
    gather_qkv.step(order)
    gather_up = Gather(
        links, [order(lambda values: values + 0, shard_up)], half + wide // 2
    )
    gather_qkv.step(order)
    longer(gather_up, 5)
    gather_up.step(order)
    slowest = [1, 2 ** len(links.y_bits)]
    in_pieces = half // 2 // slowest[1] % PAIR == 0
    ranges_down = []
    for slow in slowest:
        group = half // slow
        cuts = ((0, group // 2), (group // 2, group)) if in_pieces else ((0, group),)
        ranges_down.append(
            [
                [(core + at * group + low, core + at * group + high) for at in range(slow)]
                for core in (0, half)
                for low, high in cuts
            ]
        )
    grads_down = order.settle(
        [
            [
                jnp.concatenate([d_result_turned[:, low:high] for low, high in places], 1)
                for places in ranges
            ]
            for ranges in ranges_down
        ]
    )
    gather_qkv.step(order)
    gather_up.step(order)
    longer(gather_down, 5)
    gather_down.step(order)
    halves_qkv = gather_qkv.halves()
    normed_low, normed_high, normed_mine, normed_send, vector_rows, true_vectors = order(
        first_norm, inputs, *halves_qkv[0], to_relative
    )
    normed_other = links.exchange(normed_send, "c")
    projected = [
        order(partial(project, at), normed_low, normed_high, *halves_qkv[at], true_vectors)
        for at in (0, 1)
    ]
    normed_other = order.settle(normed_other)
    gather_up.step(order)
    shared, peak = order(attend, projected, counts)
    gather_down.step(order)
    shared_other = links.exchange(shared, "c")
    peak, peak_got = [peak], []

    def peak_send(bit):
        sent = order.settle(peak[0])
        peak_got.append(links.exchange(sent, bit))

    def peak_take():
        peak[0] = order(jnp.maximum, peak[0], peak_got.pop())

    first_bit, *more_bits = links.bits
    peak_send(first_bit)
    peak_take()
    for bit in more_bits[4:]:
        peak_send(bit)
        peak_take()
    peak_send(more_bits[0])
    gather_up.step(order)
    shared_other = order.settle(shared_other)
    peak_take()
    peak_send(more_bits[1])
    peak_take()
    peak_send(more_bits[2])
    gather_down.step(order)
    peak_take()
    peak_send(more_bits[3])
    halves_up = gather_up.halves()
    middle, normed_two_low, normed_two_high, normed_two_mine, normed_two_send = order(
        second_norm, inputs, shared, halves_up, vector_rows
    )
    peak_take()
    normed_two_other = links.exchange(normed_two_send, "c")
    if in_pieces:
        gather_down.core_early(order)
    hidden, slope, hidden_other = [], [], []
    for at in (0, 1):
        out, out_slope = order(
            partial(expand, at), normed_two_low, normed_two_high, *halves_up[at], true_vectors
        )
        hidden.append(out)
        slope.append(out_slope)
        hidden_other.append(links.exchange(out, "c"))
        if at == 0:
            normed_two_other = order.settle(normed_two_other)
            if in_pieces:
                gather_down.early = order.settle(gather_down.early)

    down_parts = [
        order(
            partial(product_wide, slowest[at], 0, wide // 2),
            d_mine,
            d_other,
            hidden[at],
            hidden_other[at],
        )
        for at in (0, 1)
    ]
    if in_pieces:
        gather_down.core_late(order)
    else:
        gather_down.step(order)
    sum_down = Sum(links, order.settle(down_parts))
    weights_down = gather_down.pieces() if in_pieces else gather_down.halves()
    d_pre, d_pre_sums = order(expand_back, grads_down, weights_down, slope)
    d_pre_other = links.exchange(d_pre, "c")
    partial_sum = order(contract_first, d_pre, *halves_up[0])
    result = order(
        partial(finish_first, ranges=ranges_down[0]), middle, hidden[0], weights_down[0], vector_rows
    )
    for _ in links.orders[0][1:]:
        sum_down.step(order)
    sum_up = Sum(
        links,
        [
            order(
                partial(product_wide, slowest[at], at * wide // 2, wide // 2),
                normed_two_mine,
                normed_two_other,
                d_pre,
                d_pre_other,
            )
            for at in (0, 1)
        ],
    )
    d_middle, d_branch_low, d_branch_high, d_out_one, d_out_two, grads = order(
        contract_second, d_pre, halves_up, partial_sum, middle, d_result_turned, vector_rows
    )
    d_branch_other = links.exchange(d_branch_high, "c")
    sum_down.step(order)
    d_branch_other = order.settle(d_branch_other)
    d_projected, d_projected_other, head_sums = [], [], []
    for at, d_out in enumerate((d_out_one, d_out_two)):
        out, sums = order(attend_back, projected[at], d_out, counts)
        d_projected.append(out)
        d_projected_other.append(links.exchange(out, "c"))
        head_sums.append(sums)


    def out_tile(at):
        return (d_branch_low, d_branch_other, shared, shared_other, half, (0, at))

    def qkv_tile(at, part, width, column):
        return (
            normed_mine,
            normed_other,
            d_projected[at],
            d_projected_other[at],
            width,
            (part, 0, column),
        )

    def late_product(at, tiles, extra=()):
        def call(operands, extra):
            return product(
                slowest[at],
                [(*operands[4 * i : 4 * i + 4], *tile[4:]) for i, tile in enumerate(tiles)],
                extra,
            )

        return order(call, [operand for tile in tiles for operand in tile[:4]], extra)

    partial_sum = order(input_back_first, d_projected[0], *halves_qkv[0])
    for _ in links.z_bits[1:]:
        sum_down.step(order)
    for _ in links.orders[0][1:]:
        sum_up.step(order)
    d_projected_other = order.settle(d_projected_other)
    quarter = half // 2
    sum_late = Sum(
        links,
        [
            late_product(at, [out_tile(at), qkv_tile(0, at, half, 0), qkv_tile(0, 2, quarter, at)])
            for at in (0, 1)
        ],
    )
    token_grad, vectors_low, vectors_high = order(
        input_back_second,
        d_projected[1],
        *halves_qkv[1],
        partial_sum,
        inputs,
        d_middle,
        grads,
        head_sums,
        d_pre_sums,
        vector_rows,
        to_relative,
    )
    token_grad = token_grad.reshape(seq_count, slot_count, model_width)
    sum_down.settle(order)
    vectors_other = links.exchange(vectors_high, "c")
    sum_up.step(order)
    last = [
        late_product(
            at,
            [qkv_tile(1, at, half, 0), qkv_tile(1, 2, quarter, at)],
            ((), (vectors_low, vectors_other))[at],
        )
        for at in (0, 1)
    ]
    sum_last = Sum(links, last)
    result = order(
        partial(finish_second, ranges=ranges_down[1]),
        result,
        hidden[1],
        weights_down[1],
        to_relative,
        counts,
    )
    result_out = result.reshape(seq_count, slot_count, model_width)
    for _ in links.orders[0][1:]:
        sum_late.step(order)
    for _ in links.z_bits[1:]:
        sum_up.step(order)
    for _ in links.orders[0][1:]:
        sum_last.step(order)
    sum_late.step(order)
    sum_last.step(order)
    mean_down, mean_up = order.settle((mean_down, mean_up))
    sum_up.settle(order)
    for _ in links.z_bits[1:]:
        sum_late.step(order)
    head_peak = order.settle(peak[0])[:, 0]
    vectors, mean_vectors, square_vectors, first_col = order.settle(
        (
            vectors,
            mean_vectors,
            square_vectors,
            lax.axis_index(("dp", "fsdp")) * shard_width,
        )
    )
    shrink = jnp.sqrt(clip_limit / jnp.maximum(head_peak, clip_limit))
    head_cols = jnp.repeat(shrink, head_width)
    qkv_scale = jnp.concatenate([head_cols, head_cols, jnp.ones((model_width,), F32)])[None]
    col_head = (first_col + jnp.arange(shard_width, dtype=jnp.int32)) // head_width
    col_shrink = jnp.sum(
        jnp.where(
            col_head[:, None] == jnp.arange(H, dtype=jnp.int32)[None, :], shrink[None, :], 0.0
        ),
        1,
    )[None]
    for _ in links.z_bits[1:]:
        sum_last.step(order)
    sum_late.settle(order)
    spans = (
        (0, half, 0, half),
        (1, 0, half, half),
        (0, half * 3 + quarter, 2 * half, half),
        (1, half + quarter, 3 * half, half),
        (0, 2 * half, 4 * half, quarter),
        (0, 4 * half + quarter, 4 * half + quarter, quarter),
        (1, half, 5 * half, quarter),
        (1, 2 * half + quarter, 5 * half + quarter, quarter),
    )
    vectors_at = 3 * half
    late = sum_late.total()
    reduced_out = jnp.concatenate([late[:, :half], late[:, 2 * half + quarter :][:, :half]], 1).T
    reduced_up = sum_up.total()
    reduced_down = sum_down.total().T
    mean_o, square_o, new_out = adam_step(
        w_out, reduced_out, mean_out, square_out, matrix_rate, weight_decay
    )
    mean_u, square_u, new_up = adam_step(
        w_up, reduced_up, mean_up, square_up, matrix_rate, weight_decay
    )
    mean_d, square_d, new_down = adam_step(
        w_down, reduced_down, mean_down, square_down, matrix_rate, weight_decay
    )
    if shard_width % 8 == 0:
        mean_q, square_q, new_qkv, mean_v, square_v, new_vectors = last_update(
            sum_late.pairs[0],
            sum_last.pairs[0],
            (spans, vectors_at),
            qkv_scale,
            (w_qkv, mean_qkv, square_qkv),
            col_shrink,
            (vectors, mean_vectors, square_vectors),
        )
    else:
        sums = (late, sum_last.total())
        reduced_qkv = jnp.concatenate(
            [sums[which][:, first : first + size] for which, first, _, size in spans], 1
        )
        mean_q, square_q, stepped_qkv = adam_step(
            w_qkv, reduced_qkv, mean_qkv, square_qkv, matrix_rate, weight_decay
        )
        new_qkv = stepped_qkv * qkv_scale
        reduced_vectors = sums[1][:, vectors_at : vectors_at + vector_count].T
        mean_v, square_v, stepped_vectors = adam_step(
            vectors, reduced_vectors, mean_vectors, square_vectors, vector_rate, 0.0
        )
        row_pick = (jnp.arange(vector_count, dtype=jnp.int32) == 4)[:, None]
        new_vectors = jnp.where(row_pick, stepped_vectors * col_shrink, stepped_vectors)
    return (
        result_out,
        token_grad,
        head_peak,
        mean_q,
        square_q,
        new_qkv,
        mean_o,
        square_o,
        new_out,
        mean_u,
        square_u,
        new_up,
        mean_d,
        square_d,
        new_down,
        mean_v,
        square_v,
        new_vectors,
    )


def solution(mesh):
    links = Links(mesh.shape["dp"], mesh.shape["fsdp"])
    return jax.shard_map(
        partial(local, links),
        mesh=mesh,
        in_specs=(
            P(("dp", "fsdp"), None, None),
            P(("dp", "fsdp"), None, None),
            P(("dp", "fsdp")),
            P(("dp", "fsdp"), None),
            P(None, ("dp", "fsdp")),
            P(("dp", "fsdp"), None),
            P(None, ("dp", "fsdp")),
            P(None, ("dp", "fsdp")),
            P(("dp", "fsdp"), None),
            P(None, ("dp", "fsdp")),
            P(("dp", "fsdp"), None),
            P(None, ("dp", "fsdp")),
            P(None, ("dp", "fsdp")),
            P(("dp", "fsdp"), None),
            P(None, ("dp", "fsdp")),
            P(("dp", "fsdp"), None),
            P(None, ("dp", "fsdp")),
            P(None, ("dp", "fsdp")),
        ),
        out_specs=(
            P(("dp", "fsdp"), None, None),
            P(("dp", "fsdp"), None, None),
            P(),
            P(("dp", "fsdp"), None),
            P(("dp", "fsdp"), None),
            P(("dp", "fsdp"), None),
            P(None, ("dp", "fsdp")),
            P(None, ("dp", "fsdp")),
            P(None, ("dp", "fsdp")),
            P(("dp", "fsdp"), None),
            P(("dp", "fsdp"), None),
            P(("dp", "fsdp"), None),
            P(None, ("dp", "fsdp")),
            P(None, ("dp", "fsdp")),
            P(None, ("dp", "fsdp")),
            P(None, ("dp", "fsdp")),
            P(None, ("dp", "fsdp")),
            P(None, ("dp", "fsdp")),
        ),
        check_vma=False,
    )
```

```python
from functools import partial

import jax
import jax.numpy as jnp
import numpy as np
from jax import lax
from jax.experimental import pallas as pl
from jax.experimental.pallas import tpu as pltpu
from jax.sharding import PartitionSpec as P

H = 16
STEP = 10


beta_one = 0.9
beta_two = 0.95
adam_epsilon = 1e-08
weight_decay = 0.1
matrix_rate = 0.1
vector_rate = 0.5
clip_limit = 8.0
norm_epsilon = 1e-06
masked_value = -1e30
TILE = 512
PAIR = 128
HALF_ROOT = 0.5**0.5
DENSITY = 0.3989422804014327
F32 = jnp.float32
BF16 = jnp.bfloat16


def adam_step(weight, gradient, mean_old, square_old, step_rate, decay_rate):
    mean_new = beta_one * mean_old + (1.0 - beta_one) * gradient
    square_new = beta_two * square_old + (1.0 - beta_two) * gradient * gradient
    fix_one = 1.0 - beta_one**STEP
    fix_two = 1.0 - beta_two**STEP
    stepped = weight - step_rate * (
        mean_new / fix_one / (jnp.sqrt(square_new / fix_two) + adam_epsilon) + decay_rate * weight
    )
    return (mean_new, square_new, stepped)


def bit_names(letter, count):
    return tuple(letter + str(at) for at in range(count))


class Links:
    def __init__(self, dp_count, inner_count):
        self.device_count = dp_count * inner_count
        inner_bits = inner_count.bit_length() - 1
        z_bits = bit_names("z", dp_count.bit_length() - 2)
        x_bits = bit_names("x", inner_bits // 2)
        y_bits = bit_names("y", inner_bits - inner_bits // 2)
        self.place = {"c": ("dp", dp_count, 0)}
        self.place.update({bit: ("dp", dp_count, at + 1) for at, bit in enumerate(z_bits)})
        self.place.update({bit: ("fsdp", inner_count, at) for at, bit in enumerate(x_bits)})
        self.place.update(
            {bit: ("fsdp", inner_count, at + len(x_bits)) for at, bit in enumerate(y_bits)}
        )
        self.bits = ("c",) + y_bits + x_bits + z_bits
        self.orders = (y_bits + x_bits, x_bits + y_bits)
        self.z_bits = z_bits
        self.y_bits = y_bits
        self.inner_bits = inner_bits

    def true_block(self):
        masks = []
        for block in range(self.device_count):
            mask = 0
            for at, bit in enumerate(reversed(self.bits)):
                if block >> at & 1:
                    axis, _, place = self.place[bit]
                    mask |= 1 << (place + (self.inner_bits if axis == "dp" else 0))
            masks.append(mask)
        return lax.axis_index(("dp", "fsdp")) ^ jnp.array(masks, jnp.int32)

    def line(self, values, moves):
        _, count, place = self.place[self.z_bits[0]]
        inner = 1 << place
        pairs = [
            (first * inner + at, last * inner + at) for first, last in moves for at in range(inner)
        ]
        return lax.ppermute(values, "dp", pairs)

    def exchange(self, values, *bits):
        axis, count, _ = self.place[bits[0]]
        mask = sum(1 << self.place[bit][2] for bit in bits)
        return lax.ppermute(values, axis, [(at, at ^ mask) for at in range(count)])


class Order:
    def __init__(self):
        self.ended = ()

    def __call__(self, call, *operands):
        operands, _ = lax.optimization_barrier((operands, self.ended))
        result = call(*operands)
        self.ended = result
        return result

    def settle(self, value):
        return self(lambda come: come, value)


def run(body, operands, outs, grid=(), in_specs=None, out_specs=None, scratch=()):
    whole = pl.BlockSpec(memory_space=pltpu.VMEM)
    return pl.pallas_call(
        body,
        out_shape=[
            pltpu.HBM(shape, kind) if hbm else jax.ShapeDtypeStruct(shape, kind)
            for shape, kind, *hbm in outs
        ],
        grid=grid,
        in_specs=in_specs or [whole] * len(operands),
        out_specs=out_specs or [whole] * len(outs),
        scratch_shapes=scratch,
        compiler_params=pltpu.CompilerParams(vmem_limit_bytes=12 * 2**20),
        cost_estimate=pl.CostEstimate(flops=30 * 10**9, bytes_accessed=1000, transcendentals=0),
    )(*operands)


def fixed(shape):
    return pl.BlockSpec(shape, lambda j: (0,) * len(shape))


def mm(first, second):
    return lax.dot_general(first, second, (((1,), (0,)), ((), ())), preferred_element_type=F32)


def mm_turned(first, second):
    return lax.dot_general(first, second, (((1,), (1,)), ((), ())), preferred_element_type=F32)


def mm_rows(first, second):
    return lax.dot_general(first, second, (((0,), (0,)), ((), ())), preferred_element_type=F32)


def pieces(values, count=3):
    out = []
    for _ in range(count):
        piece = values.astype(BF16)
        out.append(piece)
        values = values - piece.astype(F32)
    return out


def normalized(values):
    centered = values - jnp.mean(values, -1, keepdims=True)
    scale = lax.rsqrt(jnp.mean(centered * centered, -1, keepdims=True) + norm_epsilon)
    return centered * scale, scale


def norm_back(grad, values, gain):
    unit, scale = normalized(values)
    inner = grad * gain
    d_values = scale * (
        inner
        - jnp.mean(inner, -1, keepdims=True)
        - unit * jnp.mean(inner * unit, -1, keepdims=True)
    )
    return (
        d_values,
        jnp.sum(grad * unit, 0, keepdims=True),
        jnp.sum(grad, 0, keepdims=True),
    )


def packed_qkv(weights, vectors):
    rows, width = weights.shape
    part = width // 6
    first = 3 * part

    def body(weight_ref, vector_ref, out_ref):
        for at in range(6):
            start = at // 2 * part + at % 2 * (first + PAIR)
            out_ref[:, start : start + part] = weight_ref[:, at * part : (at + 1) * part].astype(BF16)
        vector = vector_ref[...]
        empty = jnp.zeros((PAIR - vector.shape[0], rows), F32)
        out_ref[:, first : first + PAIR] = jnp.concatenate([vector, empty], 0).T.astype(BF16)

    return run(body, (weights, vectors), [((rows, width + PAIR), BF16)])[0]


def first_norm(inputs, mine, other, to_relative):
    rows, width = inputs.shape
    half = width // 2

    def body(
        x_ref, mine_ref, other_ref, turn_ref, low_ref, high_ref, lowt_ref, hight_ref, rel_ref, true_ref
    ):
        turned = jnp.concatenate(
            [mine_ref[...].astype(F32).T, other_ref[...].astype(F32).T], 1
        )[:16]
        rel_ref[...] = turned
        true_ref[...] = mm_turned(turned.astype(BF16), turn_ref[...])
        unit, _ = normalized(x_ref[...].astype(F32))
        normed = (unit * turned[0:1] + turned[1:2]).astype(BF16)
        low_ref[...] = normed[:, :half]
        high_ref[...] = normed[:, half:]
        lowt_ref[...] = normed[:, :half].T
        hight_ref[...] = normed[:, half:].T

    vectors_at = mine.shape[1] // PAIR - 1
    weights = pl.BlockSpec((half, PAIR), lambda j: (0, vectors_at))
    return run(
        body,
        (inputs, mine, other, to_relative),
        [((rows, half), BF16)] * 2 + [((half, rows), BF16)] * 2 + [((16, width), F32)] * 2,
        (1,),
        [fixed(inputs.shape), weights, weights, fixed(to_relative.shape)],
        [fixed((rows, half))] * 2 + [fixed((half, rows))] * 2 + [fixed((16, width))] * 2,
    )


def project(at, low, high, mine, other, true_vectors):
    rows, half = low.shape

    def body(low_ref, high_ref, mine_ref, other_ref, vec_ref, out_ref):
        j = pl.program_id(0)
        bias = jnp.where(j == 0, vec_ref[4:5, :], jnp.where(j == 2, vec_ref[5:6, :], 0.0))
        value = mm(low_ref[...], mine_ref[...]) + mm(high_ref[...], other_ref[...])
        out_ref[0] = (value + bias).astype(BF16)

    weights = pl.BlockSpec((half, TILE), lambda j: (0, j))
    return run(
        body,
        (low, high, mine, other, true_vectors),
        [((3, rows, TILE), BF16)],
        (3,),
        [fixed(low.shape)] * 2 + [weights] * 2 + [pl.BlockSpec((16, TILE), lambda j: (0, at))],
        [pl.BlockSpec((1, rows, TILE), lambda j: (j, 0, 0))],
    )[0]


def head_mask(rows, side):
    lane = lax.broadcasted_iota(jnp.int32, (rows, PAIR), 1)
    return lane < PAIR // 2 if side == 0 else lane >= PAIR // 2


def attend(projected, counts):
    _, rows, width = projected[0].shape
    steps = width // PAIR

    def body(count_ref, *refs):
        *ins, out_ref, peak_ref = refs
        j = pl.program_id(0)

        def heads(q_ref, k_ref, v_ref):
            count = count_ref[0]
            key_ok = lax.broadcasted_iota(jnp.int32, (rows, rows), 1) < count
            row_ok = lax.broadcasted_iota(jnp.int32, (rows, 1), 0) < count
            queries = q_ref[0]
            out = None
            for side in (0, 1):
                chosen = head_mask(rows, side)
                scores = mm_turned(jnp.where(chosen, queries, 0), k_ref[0]) * (PAIR // 2) ** -0.5
                scores = jnp.where(key_ok, scores, masked_value)
                top = jnp.max(scores, -1, keepdims=True)
                peak = jnp.max(jnp.where(row_ok, top, masked_value))
                peak_ref[pl.ds(j * 2 + side, 1), :] = jnp.full((1, PAIR), peak)
                exponent = jnp.exp(scores - top)
                probs = exponent * (1.0 / jnp.sum(exponent, -1, keepdims=True))
                value = mm(probs.astype(BF16), v_ref[0])
                out = value if side == 0 else jnp.where(chosen, value, out)
            out_ref[...] = out.astype(BF16)

        @pl.when(j < steps)
        def _():
            heads(*ins[:3])

        @pl.when(j >= steps)
        def _():
            heads(*ins[3:])

    def part(index, at):
        return pl.BlockSpec(
            (1, rows, PAIR), lambda j: (index, 0, jnp.clip(j - at * steps, 0, steps - 1))
        )

    return run(
        body,
        (counts, *[projected[0]] * 3, *[projected[1]] * 3),
        [((rows, 2 * width), BF16), ((4 * steps, PAIR), F32)],
        (2 * steps,),
        [pl.BlockSpec(memory_space=pltpu.SMEM)]
        + [part(index, at) for at in (0, 1) for index in range(3)],
        [pl.BlockSpec((rows, PAIR), lambda j: (0, j)), fixed((4 * steps, PAIR))],
    )


def attend_back(projected, d_out, counts):
    _, rows, width = projected.shape
    steps = width // PAIR
    scale = (PAIR // 2) ** -0.5

    def body(count_ref, q_ref, k_ref, v_ref, d_ref, out_ref, sum_ref):
        key_ok = lax.broadcasted_iota(jnp.int32, (rows, rows), 0) < count_ref[0]
        queries, keys, values, grad = q_ref[0], k_ref[0], v_ref[0], d_ref[...]
        parts = [None] * 3
        for side in (0, 1):
            chosen = head_mask(rows, side)
            scores = mm_turned(jnp.where(chosen, keys, 0), queries) * scale
            scores = jnp.where(key_ok, scores, masked_value)
            exponent = jnp.exp(scores - jnp.max(scores, 0, keepdims=True))
            probs = exponent * (1.0 / jnp.sum(exponent, 0, keepdims=True))
            d_probs = mm_turned(jnp.where(chosen, values, 0), grad)
            inner = jnp.sum(probs * d_probs, 0, keepdims=True)
            d_scores = (probs * (d_probs - inner)).astype(BF16)
            new = [
                mm_rows(d_scores, keys) * scale,
                mm(d_scores, queries) * scale,
                mm(probs.astype(BF16), grad),
            ]
            parts = new if side == 0 else [jnp.where(chosen, n, p) for n, p in zip(new, parts)]
        low = [part.astype(BF16) for part in parts]
        for at in range(3):
            out_ref[at] = low[at]
        sum_ref[0:1, :] = jnp.sum(low[0].astype(F32), 0, keepdims=True)
        sum_ref[1:2, :] = jnp.sum(low[2].astype(F32), 0, keepdims=True)

    def part(index):
        return pl.BlockSpec((1, rows, PAIR), lambda j: (index, 0, j))

    columns = pl.BlockSpec((rows, PAIR), lambda j: (0, j))
    return run(
        body,
        (counts, projected, projected, projected, d_out),
        [((3, rows, width), BF16), ((8, width), F32)],
        (steps,),
        [pl.BlockSpec(memory_space=pltpu.SMEM), part(0), part(1), part(2), columns],
        [
            pl.BlockSpec((3, rows, PAIR), lambda j: (0, 0, j)),
            pl.BlockSpec((8, PAIR), lambda j: (0, j)),
        ],
    )


def second_norm(inputs, attended, weights, vectors):
    rows, width = inputs.shape
    half = width // 2

    def body(x_ref, a_ref, b_ref, wa_ref, wa2_ref, wb_ref, wb2_ref, vec_ref, mid_ref, low_ref, high_ref, lowt_ref, hight_ref):
        first, second = a_ref[...], b_ref[...]
        branch = jnp.concatenate(
            [
                mm_turned(first, wa_ref[...]) + mm_turned(second, wb_ref[...]),
                mm_turned(first, wa2_ref[...]) + mm_turned(second, wb2_ref[...]),
            ],
            1,
        )
        middle = x_ref[...].astype(F32) + branch + vec_ref[6:7, :]
        mid_ref[...] = middle
        unit, _ = normalized(middle)
        normed = (unit * vec_ref[2:3, :] + vec_ref[3:4, :]).astype(BF16)
        low_ref[...] = normed[:, :half]
        high_ref[...] = normed[:, half:]
        lowt_ref[...] = normed[:, :half].T
        hight_ref[...] = normed[:, half:].T

    block = pl.BlockSpec((half, TILE), lambda j: (0, 0))
    return run(
        body,
        (inputs, attended, attended, *weights[0], *weights[1], vectors),
        [((rows, width), F32)] + [((rows, half), BF16)] * 2 + [((half, rows), BF16)] * 2,
        (1,),
        [fixed(inputs.shape)]
        + [pl.BlockSpec((rows, TILE), lambda j, at=at: (0, at)) for at in (0, 1)]
        + [block] * 4
        + [fixed(vectors.shape)],
        [fixed((rows, width))] + [fixed((rows, half))] * 2 + [fixed((half, rows))] * 2,
    )


def expand(at, low, high, mine, other, true_vectors):
    rows, half = low.shape
    count = mine.shape[1] - TILE
    per_row = true_vectors.shape[1] // TILE
    first_row = 8 + at * count // true_vectors.shape[1]

    def body(low_ref, high_ref, mine_ref, other_ref, vec_ref, out_ref, slope_ref):
        row = first_row + pl.program_id(0) // per_row
        pre = mm(low_ref[...], mine_ref[...]) + mm(high_ref[...], other_ref[...])
        pre = pre + vec_ref[pl.ds(row, 1), :]
        below = 0.5 * (1.0 + lax.erf(pre * HALF_ROOT))
        out_ref[...] = (pre * below).astype(BF16)
        slope = below + pre * (DENSITY * jnp.exp(-0.5 * pre * pre))
        slope_ref[...] = slope.astype(BF16)

    weights = pl.BlockSpec((half, TILE), lambda j: (0, j + 1))
    columns = pl.BlockSpec((rows, TILE), lambda j: (0, j))
    return run(
        body,
        (low, high, mine, other, true_vectors),
        [((rows, count), BF16), ((rows, count), BF16, "hbm")],
        (count // TILE,),
        [fixed(low.shape)] * 2
        + [weights] * 2
        + [pl.BlockSpec((16, TILE), lambda j: (0, j % per_row))],
        [columns, columns],
    )


def among(count, at, shape):
    return pl.BlockSpec(shape, lambda j: (0, jnp.clip(j - at * count, 0, count - 1)))


def expand_back(grads, weights, slopes):
    rows = slopes[0].shape[0]
    steps = slopes[0].shape[1] // TILE
    counts = [len(pieces) for pieces in weights]
    operands, specs = [], []
    for at, (left, rights) in enumerate(zip(grads, weights)):
        operands += [left] * len(rights) + [*rights]
        specs += [
            pl.BlockSpec((rows, right.shape[0]), lambda j, piece=piece: (0, piece))
            for piece, right in enumerate(rights)
        ]
        specs += [among(steps, at, (right.shape[0], TILE)) for right in rights]

    def body(*refs):
        *ins, first_slope, second_slope, out_ref, sum_ref = refs
        j = pl.program_id(0)
        for at, slope_ref in enumerate((first_slope, second_slope)):
            first = 2 * sum(counts[:at])
            lefts, rights = ins[first : first + counts[at]], ins[first + counts[at] :][: counts[at]]

            @pl.when(j // steps == at)
            def _(lefts=lefts, rights=rights, slope_ref=slope_ref):
                value = sum(mm(left[...], right[...]) for left, right in zip(lefts, rights))
                value = (value * slope_ref[...].astype(F32)).astype(BF16)
                out_ref[...] = value
                sum_ref[...] = jnp.sum(value.astype(F32), 0, keepdims=True)

    count = 2 * steps
    return run(
        body,
        (*operands, *slopes),
        [((rows, count * TILE), BF16), ((1, count * TILE), F32)],
        (count,),
        specs + [among(steps, at, (rows, TILE)) for at in range(2)],
        [pl.BlockSpec((rows, TILE), lambda j: (0, j)), pl.BlockSpec((1, TILE), lambda j: (0, j))],
    )


def contract_first(d_pre, mine, other):
    rows, count = d_pre.shape
    half = mine.shape[0]
    count = count // 2

    def body(d_ref, mine_ref, other_ref, out_ref):
        @pl.when(pl.program_id(0) == 0)
        def _():
            out_ref[...] = jnp.zeros_like(out_ref)

        out_ref[:, :half] += mm_turned(d_ref[...], mine_ref[...])
        out_ref[:, half:] += mm_turned(d_ref[...], other_ref[...])

    weights = pl.BlockSpec((half, TILE), lambda j: (0, j + 1))
    return run(
        body,
        (d_pre, mine, other),
        [((rows, 2 * half), F32)],
        (count // TILE,),
        [pl.BlockSpec((rows, TILE), lambda j: (0, j)), weights, weights],
        [fixed((rows, 2 * half))],
    )[0]


def contract_second(d_pre, weights, partial_sum, middle, d_result, vectors):
    rows, count = d_pre.shape
    half = weights[0][0].shape[0]
    width = 2 * half
    steps = count // 2 // TILE

    def body(
        d_ref, mine_ref, other_ref, wa_ref, wa2_ref, wb_ref, wb2_ref, sum_ref, mid_ref, res_ref,
        vec_ref, dm_ref, low_ref, high_ref, outa_ref, outb_ref, grads_ref, total,
    ):
        j = pl.program_id(0)

        @pl.when(j == 0)
        def _():
            total[...] = sum_ref[...]

        total[:, :half] += mm_turned(d_ref[...], mine_ref[...])
        total[:, half:] += mm_turned(d_ref[...], other_ref[...])

        @pl.when(j == steps - 1)
        def _():
            d_values, d_gain, d_shift = norm_back(total[...], mid_ref[...], vec_ref[2:3, :])
            result_grad = res_ref[...].astype(F32)
            d_middle = result_grad + d_values
            branch = d_middle.astype(BF16)
            dm_ref[...] = d_middle
            first, second = branch[:, :half], branch[:, half:]
            low_ref[...] = first.T
            high_ref[...] = second.T
            outa_ref[...] = (mm(first, wa_ref[...]) + mm(second, wa2_ref[...])).astype(BF16)
            outb_ref[...] = (mm(first, wb_ref[...]) + mm(second, wb2_ref[...])).astype(BF16)
            grads_ref[0:1, :] = d_gain
            grads_ref[1:2, :] = d_shift
            grads_ref[2:3, :] = jnp.sum(branch.astype(F32), 0, keepdims=True)
            grads_ref[3:4, :] = jnp.sum(result_grad, 0, keepdims=True)

    tile = pl.BlockSpec((half, TILE), lambda j: (0, j + 1))
    block = pl.BlockSpec((half, TILE), lambda j: (0, 0))
    return run(
        body,
        (d_pre, *weights[1], *weights[0], *weights[1], partial_sum, middle, d_result, vectors),
        [((rows, width), F32)]
        + [((half, rows), BF16)] * 2
        + [((rows, TILE), BF16)] * 2
        + [((8, width), F32)],
        (steps,),
        [pl.BlockSpec((rows, TILE), lambda j: (0, steps + j)), tile, tile]
        + [block] * 4
        + [fixed((rows, width))] * 3
        + [fixed(vectors.shape)],
        [fixed((rows, width))]
        + [fixed((half, rows))] * 2
        + [fixed((rows, TILE))] * 2
        + [fixed((8, width))],
        [pltpu.VMEM((rows, width), F32)],
    )


def input_back_first(d_projected, mine, other):
    rows = d_projected.shape[1]
    half = mine.shape[0]

    def body(d_ref, mine_ref, other_ref, out_ref):
        @pl.when(pl.program_id(0) == 0)
        def _():
            out_ref[...] = jnp.zeros_like(out_ref)

        out_ref[:, :half] += mm_turned(d_ref[0], mine_ref[...])
        out_ref[:, half:] += mm_turned(d_ref[0], other_ref[...])

    weights = pl.BlockSpec((half, TILE), lambda j: (0, j))
    return run(
        body,
        (d_projected, mine, other),
        [((rows, 2 * half), F32)],
        (3,),
        [pl.BlockSpec((1, rows, TILE), lambda j: (j, 0, 0)), weights, weights],
        [fixed((rows, 2 * half))],
    )[0]


def input_back_second(
    d_projected, mine, other, partial_sum, inputs, d_middle, grads, head_sums, d_pre_sums, vectors, to_relative
):
    rows = d_projected.shape[1]
    half = mine.shape[0]
    width = 2 * half

    def body(
        d_ref, mine_ref, other_ref, sum_ref, x_ref, dm_ref, grads_ref, heada_ref, headb_ref, pre_ref,
        vec_ref, turn_ref, out_ref, low_ref, high_ref, total, true_rows, all_rows,
    ):
        j = pl.program_id(0)

        @pl.when(j == 0)
        def _():
            total[...] = sum_ref[...]

        total[:, :half] += mm_turned(d_ref[0], mine_ref[...])
        total[:, half:] += mm_turned(d_ref[0], other_ref[...])

        @pl.when(j == 2)
        def _():
            d_values, d_gain, d_shift = norm_back(total[...], x_ref[...].astype(F32), vec_ref[0:1, :])
            low = (dm_ref[...] + d_values).astype(BF16)
            out_ref[...] = mm_turned(low, turn_ref[...]).astype(BF16)
            true_rows[...] = jnp.zeros_like(true_rows)
            for at, ref in enumerate((heada_ref, headb_ref)):
                true_rows[0:2, at * TILE : (at + 1) * TILE] = ref[0:2, :]
            for part in range(pre_ref.shape[1] // width):
                row = 2 + part
                true_rows[row : row + 1, :] = pre_ref[:, part * width : (part + 1) * width]
            turned = sum(mm(part, turn_ref[...]) for part in pieces(true_rows[...]))
            all_rows[...] = jnp.zeros_like(all_rows)
            all_rows[0:1, :] = d_gain
            all_rows[1:2, :] = d_shift
            all_rows[2:4, :] = grads_ref[0:2, :]
            all_rows[4:6, :] = turned[0:2]
            all_rows[6:8, :] = grads_ref[2:4, :]
            all_rows[8:14, :] = turned[2:8]
            columns = all_rows[...].T
            low_ref[...] = columns[:half]
            high_ref[...] = columns[half:]

    weights = pl.BlockSpec((half, TILE), lambda j: (0, j))
    operands = (
        d_projected,
        mine,
        other,
        partial_sum,
        inputs,
        d_middle,
        grads,
        *head_sums,
        d_pre_sums,
        vectors,
        to_relative,
    )
    return run(
        body,
        operands,
        [((rows, width), BF16)] + [((half, PAIR), F32)] * 2,
        (3,),
        [pl.BlockSpec((1, rows, TILE), lambda j: (j, 0, 0)), weights, weights]
        + [fixed(operand.shape) for operand in operands[3:]],
        [fixed((rows, width))] + [fixed((half, PAIR))] * 2,
        [pltpu.VMEM((rows, width), F32), pltpu.VMEM((8, width), F32), pltpu.VMEM((PAIR, width), F32)],
    )


def contract_hidden(hidden, weights, ranges, total):
    for ref, places in zip(weights, ranges):
        value = mm_turned(hidden[...], ref[...])
        first = 0
        for low, high in places:
            total[:, low:high] += value[:, first : first + high - low]
            first += high - low


def finish_first(middle, hidden, weights, vectors, ranges):
    rows, width = middle.shape
    steps = hidden.shape[1] // TILE

    def body(hidden_ref, *refs):
        *weight_refs, mid_ref, vec_ref, out_ref = refs

        @pl.when(pl.program_id(0) == 0)
        def _():
            out_ref[...] = mid_ref[...] + vec_ref[7:8, :]

        contract_hidden(hidden_ref, weight_refs, ranges, out_ref)

    columns = pl.BlockSpec((rows, TILE), lambda j: (0, j))
    return run(
        body,
        (hidden, *weights, middle, vectors),
        [((rows, width), F32)],
        (steps,),
        [columns]
        + [pl.BlockSpec((right.shape[0], TILE), lambda j: (0, j)) for right in weights]
        + [fixed((rows, width)), fixed(vectors.shape)],
        [fixed((rows, width))],
    )[0]


def finish_second(partial_sum, hidden, weights, to_relative, counts, ranges):
    rows, width = partial_sum.shape
    steps = hidden.shape[1] // TILE

    def body(count_ref, hidden_ref, *refs):
        *weight_refs, sum_ref, turn_ref, out_ref, total = refs

        @pl.when(pl.program_id(0) == 0)
        def _():
            total[...] = sum_ref[...]

        contract_hidden(hidden_ref, weight_refs, ranges, total)

        @pl.when(pl.program_id(0) == steps - 1)
        def _():
            kept = lax.broadcasted_iota(jnp.int32, (rows, 1), 0) < count_ref[0]
            low = jnp.where(kept, total[...], 0.0).astype(BF16)
            out_ref[...] = mm_turned(low, turn_ref[...]).astype(BF16)

    columns = pl.BlockSpec((rows, TILE), lambda j: (0, j))
    return run(
        body,
        (counts, hidden, *weights, partial_sum, to_relative),
        [((rows, width), BF16)],
        (steps,),
        [pl.BlockSpec(memory_space=pltpu.SMEM), columns]
        + [pl.BlockSpec((right.shape[0], TILE), lambda j: (0, j)) for right in weights]
        + [fixed((rows, width)), fixed(to_relative.shape)],
        [fixed((rows, width))],
        [pltpu.VMEM((rows, width), F32)],
    )[0]


def product(slowest, tiles, extra=()):
    count, rows = tiles[0][0].shape
    operands, specs = [], []
    for *both, width, place in tiles:
        operands += both
        specs += [fixed((count, rows))] * 2
        shape = (1,) * (len(place) - 2) + (rows, width)
        specs += [pl.BlockSpec(shape, lambda j, place=place: place)] * 2
    width = sum(tile[4] for tile in tiles)
    full = width + (extra[0].shape[1] if extra else 0)
    operands += extra
    specs += [fixed(operand.shape) for operand in extra]

    def body(*refs):
        *ins, sent_ref, kept_ref = refs
        first = 0
        for at, tile in enumerate(tiles):
            left, left_other, right, right_other = (
                ref[0] if len(ref.shape) == 3 else ref[...] for ref in ins[4 * at : 4 * at + 4]
            )
            value = (mm(left, right) + mm(left_other, right_other)).astype(BF16)
            columns = slice(first, first + tile[4])
            first += tile[4]
            cut_rows(value, slowest, sent_ref, kept_ref, columns)
        if extra:
            value = (ins[-2][...] + ins[-1][...]).astype(BF16)
            cut_rows(value, slowest, sent_ref, kept_ref, slice(width, full))

    out = (count // 2, full)
    return run(body, operands, [(out, BF16)] * 2, (1,), specs, [fixed(out)] * 2)


def cut_rows(value, slowest, sent_ref, kept_ref, columns):
    part = value.shape[0] // 2 // slowest
    for group in range(slowest):
        low = 2 * group * part
        rows = slice(group * part, (group + 1) * part)
        kept_ref[rows, columns] = value[low : low + part]
        sent_ref[rows, columns] = value[low + part : low + 2 * part]


def product_wide(slowest, first, width, left, left_other, right, right_other):
    rows = right.shape[0]
    count = left.shape[0]

    def body(left_ref, left_other_ref, right_ref, right_other_ref, sent_ref, kept_ref):
        value = mm(left_ref[...], right_ref[...]) + mm(left_other_ref[...], right_other_ref[...])
        cut_rows(value.astype(BF16), slowest, sent_ref, kept_ref, slice(None))

    columns = pl.BlockSpec((rows, TILE), lambda j: (0, first // TILE + j))
    out_columns = pl.BlockSpec((count // 2, TILE), lambda j: (0, j))
    return run(
        body,
        (left, left_other, right, right_other),
        [((count // 2, width), BF16, "hbm")] * 2,
        (width // TILE,),
        [fixed(left.shape)] * 2 + [columns] * 2,
        [out_columns] * 2,
    )


def added(first, second, kind=BF16):
    return (first.astype(F32) + second.astype(F32)).astype(kind)


def halved(pairs, joined):
    half = pairs[0][0].shape[0] // 2
    widths = [mine.shape[1] for mine, _ in pairs]
    if half % 16:
        totals = [added(*pair) for pair in pairs]
        if joined:
            totals = [jnp.concatenate(totals, 1)]
        return [(total[half:], total[:half]) for total in totals]

    def body(*refs):
        ins, outs = refs[: 2 * len(pairs)], refs[2 * len(pairs) :]
        for at in range(len(pairs)):
            mine, got = ins[2 * at], ins[2 * at + 1]
            sent_ref, kept_ref = outs[:2] if joined else outs[2 * at : 2 * at + 2]
            first = sum(widths[:at]) if joined else 0
            columns = slice(first, first + widths[at])
            sent_ref[:, columns] = added(mine[half:, :], got[half:, :])
            kept_ref[:, columns] = added(mine[:half, :], got[:half, :])

    out_widths = [sum(widths)] if joined else widths
    outs = [((half, width), BF16) for width in out_widths for _ in range(2)]
    outs = run(body, [v for pair in pairs for v in pair], outs)
    return [tuple(outs[at : at + 2]) for at in range(0, len(outs), 2)]


def joined(places, middle, count, mine, got):
    wide = mine[0].shape[-1] if len(mine) == 1 else sum(value.shape[-1] for value in mine)
    parts = (slice(0, middle), slice(middle, wide))
    pairs = list(zip(places, mine, got))
    shapes = [(*value.shape[:at], 2, *value.shape[at:]) for at, value, _ in pairs]

    def widths(shape):
        if count == 1:
            return [(*shape[:-1], wide)]
        return [(*shape[:-1], part.stop - part.start) for part in parts]

    out_shapes = shapes if len(mine) == count else widths(shapes[0])
    if mine[0].shape[-2] % 16:
        both = [jnp.stack([value, come], at) for at, value, come in pairs]
        if len(mine) == count:
            return both
        if count == 1:
            rest = both[0].shape[:-1]
            return [jnp.concatenate([value.reshape(*rest, -1) for value in both], -1)]
        return [both[0][..., part] for part in parts]

    def body(*refs):
        outs = refs[2 * len(mine) :]
        for at, (place, value, _) in enumerate(pairs):
            for side in (0, 1):
                ref = refs[at + side * len(mine)]
                lead = (slice(None),) * place + (side,) + (slice(None),) * (value.ndim - 1 - place)
                if len(mine) == count:
                    outs[at][(*lead, slice(None))] = ref[...]
                elif count == 1:
                    outs[0][(*lead, parts[at])] = ref[...]
                else:
                    for out_ref, part in zip(outs, parts):
                        out_ref[(*lead, slice(None))] = ref[..., part]

    return run(body, [*mine, *got], [(shape, BF16) for shape in out_shapes])


def joined_all(bits, middle, blocks):
    rows, wide = blocks[0].shape
    parts = (slice(0, middle), slice(middle, wide))
    shape = (2,) * bits
    if rows % 16:
        whole = jnp.stack(blocks).reshape(*shape, rows, wide)
        return [whole[..., part] for part in parts]

    def body(*refs):
        for at, ref in enumerate(refs[: len(blocks)]):
            lead = tuple(at >> (bits - 1 - bit) & 1 for bit in range(bits))
            for out_ref, part in zip(refs[len(blocks) :], parts):
                out_ref[(*lead, slice(None), slice(None))] = ref[:, part]

    return run(
        body, blocks, [((*shape, rows, part.stop - part.start), BF16) for part in parts]
    )


def joined_line(middle, blocks, count, in_middle):
    *lead, rows, wide = blocks[0].shape
    parts = (slice(0, middle), slice(middle, wide)) if count == 2 else (slice(0, wide),)
    front = (slice(None),) * len(lead)

    def body(flag_ref, mine, near, across, over, past, back, *outs):
        def put(place, ref):
            for out_ref, part in zip(outs, parts):
                out_ref[(*front, *place, slice(None), slice(None))] = ref[..., part]

        put((0, 0), mine)
        put((1, 0), near)

        @pl.when(flag_ref[0] == 1)
        def _():
            put((0, 1), over)
            put((1, 1), across)

        @pl.when(flag_ref[0] == 0)
        def _():
            put((0, 1), back)
            put((1, 1), past)

    whole = pl.BlockSpec(memory_space=pltpu.VMEM)
    return run(
        body,
        (in_middle, *blocks),
        [((*lead, 2, 2, rows, part.stop - part.start), BF16) for part in parts],
        in_specs=[pl.BlockSpec(memory_space=pltpu.SMEM)] + [whole] * len(blocks),
    )


class Sum:
    def __init__(self, links, firsts):
        self.links = links
        self.left, self.pairs = [], []
        self.z_left = links.z_bits
        for parts, order in zip(firsts, links.orders):
            self.add(parts, order)

    def add(self, parts, order):
        sent, kept = parts
        self.left.append(order[1:])
        self.pairs.append((kept, self.links.exchange(sent, order[0])))

    def step(self, order):
        inner = bool(self.left[0])
        joined = not inner and len(self.pairs) > 1
        parts = order(partial(halved, joined=joined), self.pairs)
        if inner:
            bits = [left[0] for left in self.left]
            self.left = [left[1:] for left in self.left]
        else:
            bits = [self.z_left[0]]
            self.z_left = self.z_left[1:]
        self.pairs = [
            (kept, self.links.exchange(sent, bit)) for (sent, kept), bit in zip(parts, bits)
        ]

    def settle(self, order):
        self.pairs = [(kept, order.settle(got)) for kept, got in self.pairs]

    def total(self):
        return added(*self.pairs[0], F32)


class Gather:
    def __init__(self, links, shards, middle, at_once=False):
        self.links, self.middle = links, middle
        steps = [tuple(reversed(order)) for order in links.orders]
        steps = list(zip(*steps))
        between = len(steps) // 2 if len(shards) == 2 else 0
        z_steps = [(bit,) for bit in reversed(links.z_bits)]
        if at_once:
            z_steps = ["all z"]
        elif len(z_steps) == 2 and between and shards[0].shape[0] % 16 == 0:
            z_steps = ["line", "line on"]
        self.steps = steps[:between] + z_steps + steps[between:] + [("c", "c")]
        self.blocks = list(shards)
        self.bits = [(), ()]
        self.send()

    def parts(self):
        return 1 if isinstance(self.steps[0], str) else len(self.steps[0])

    def send(self):
        if self.steps[0] == "line":
            own = self.blocks[0]
            self.got = [
                self.links.exchange(own, self.links.z_bits[0]),
                self.links.line(own, ((1, 2), (2, 1))),
            ]
            return
        if self.steps[0] == "line on":
            near, across = self.got
            self.got = [
                near,
                across,
                self.links.line(near, ((1, 2), (2, 1))),
                self.links.line(near, ((1, 3), (2, 0))),
                self.links.line(across, ((1, 0), (2, 3))),
            ]
            return
        if self.steps[0] == "all z":
            z_bits = self.links.z_bits
            chosen = [
                [bit for at, bit in enumerate(z_bits) if block >> (len(z_bits) - 1 - at) & 1]
                for block in range(1, 2 ** len(z_bits))
            ]
            self.got = [self.links.exchange(self.blocks[0], *bits) for bits in chosen]
            return
        self.got = [
            self.links.exchange(block, bit) for block, bit in zip(self.blocks, self.steps[0])
        ]

    def join(self, order):
        done, *self.steps = self.steps
        if done == "line":
            self.got = order.settle(self.got)
            return
        if done == "line on":
            self.bits = [bits + self.links.z_bits for bits in self.bits]
            z = lax.axis_index("dp") // 2
            in_middle = ((z == 1) | (z == 2)).astype(jnp.int32)[None]
            self.blocks = order(
                lambda blocks, flag: joined_line(self.middle, blocks, self.parts(), flag),
                [*self.blocks, *self.got],
                in_middle,
            )
            return
        if done == "all z":
            z_bits = self.links.z_bits
            self.bits = [z_bits, z_bits]
            self.blocks = order(
                partial(joined_all, len(z_bits), self.middle), [*self.blocks, *self.got]
            )
            return
        bits = done * 2 if len(done) == 1 else done
        places = []
        for at, bit in enumerate(bits):
            held = sorted((*self.bits[at], bit), key=self.links.bits.index)
            self.bits[at] = tuple(held)
            places.append(held.index(bit))
        self.blocks = order(
            partial(joined, places, self.middle, self.parts()), self.blocks, self.got
        )
        if self.steps[0][0] == "c":
            self.blocks = [block.reshape(-1, block.shape[-1]) for block in self.blocks]

    def step(self, order):
        self.join(order)
        self.send()

    def settle(self, order):
        self.got = order.settle(self.got)

    def core_early(self, order):
        self.blocks = order.settle(self.blocks)
        self.early = [self.links.exchange(block, "c") for block in self.blocks]

    def core_late(self, order):
        self.got = order.settle(self.got)
        self.late = [self.links.exchange(got, "c") for got in self.got]

    def pieces(self):
        return [
            [values.reshape(-1, values.shape[-1]) for values in four]
            for four in zip(self.blocks, self.got, self.early, self.late)
        ]

    def halves(self):
        return list(zip(self.blocks, self.got))


def last_update(late, last, spans, scale, moments, vector_scale, vector_moments):
    spans, vectors_at = spans
    rows, width = moments[0].shape
    count = vector_moments[0].shape[0]

    def body(*refs):
        late_kept, late_got, last_kept, last_got, scale_ref = refs[:5]
        weight_ref, mean_ref, square_ref, vscale_ref, vector_ref, vmean_ref, vsquare_ref = refs[5:12]
        outs = refs[12:]
        sums = [added(late_kept[...], late_got[...], F32), added(last_kept[...], last_got[...], F32)]
        for of_last, first, place, size in spans:
            columns = slice(place, place + size)
            mean, square, stepped = adam_step(
                weight_ref[:, columns],
                sums[of_last][:, first : first + size],
                mean_ref[:, columns],
                square_ref[:, columns],
                matrix_rate,
                weight_decay,
            )
            outs[0][:, columns] = mean
            outs[1][:, columns] = square
            outs[2][:, columns] = stepped * scale_ref[:, columns]
        grads = sums[1][:, vectors_at : vectors_at + PAIR].T[:count]
        mean, square, stepped = adam_step(
            vector_ref[...], grads, vmean_ref[...], vsquare_ref[...], vector_rate, 0.0
        )
        outs[3][...] = mean
        outs[4][...] = square
        row = lax.broadcasted_iota(jnp.int32, stepped.shape, 0)
        outs[5][...] = jnp.where(row == 4, stepped * vscale_ref[...], stepped)

    return run(
        body,
        (*late, *last, scale, *moments, vector_scale, *vector_moments),
        [((rows, width), F32)] * 3 + [(vector_moments[0].shape, F32)] * 3,
    )


def local(
    links,
    tokens,
    cotangent,
    counts,
    w_qkv,
    w_out,
    w_up,
    w_down,
    vectors,
    mean_qkv,
    mean_out,
    mean_up,
    mean_down,
    mean_vectors,
    square_qkv,
    square_out,
    square_up,
    square_down,
    square_vectors,
):
    seq_count, slot_count, model_width = tokens.shape
    rows = seq_count * slot_count
    head_width = model_width // H
    wide = w_down.shape[0]
    vector_count, shard_width = vectors.shape
    half = model_width // 2
    order = Order()

    if shard_width % 16 == 0:
        shard_qkv = packed_qkv(w_qkv, vectors)
    else:
        low_qkv = w_qkv.astype(BF16)
        thirds = [low_qkv[:, at * half : (at + 1) * half] for at in range(6)]
        shard_vectors = jnp.pad(vectors.astype(BF16).T, ((0, 0), (0, PAIR - vector_count)))
        shard_qkv = jnp.concatenate([*thirds[0::2], shard_vectors, *thirds[1::2]], 1)
    low_out, low_up = w_out.astype(BF16).T, w_up.astype(BF16)
    shard_up = jnp.concatenate(
        [low_out[:, :half], low_up[:, : wide // 2], low_out[:, half:], low_up[:, wide // 2 :]], 1
    )
    shard_down = w_down.astype(BF16).T
    gather_qkv = Gather(links, [shard_qkv], 3 * half + PAIR, True)
    gather_down = Gather(
        links, [shard_down[:, : wide // 2], shard_down[:, wide // 2 :]], wide // 2
    )

    true_rows = (
        links.true_block()[:, None] * shard_width + jnp.arange(shard_width, dtype=jnp.int32)
    ).reshape(1, model_width)
    to_relative = (
        lax.broadcasted_iota(jnp.int32, (model_width, model_width), 0) == true_rows
    ).astype(BF16)
    keep_rows = lax.broadcasted_iota(jnp.int32, (rows, 1), 0) < counts[0]
    d_result = jnp.where(keep_rows, cotangent.reshape(rows, model_width), 0).astype(BF16)
    inputs = mm(tokens.reshape(rows, model_width), to_relative).astype(BF16)
    d_result_turned = mm(d_result, to_relative).astype(BF16)
    d_columns = lax.dot_general(
        to_relative, d_result, (((0,), (1,)), ((), ())), preferred_element_type=F32
    ).astype(BF16)

    def longer(gather, count):
        while len(gather.steps) > count:
            gather.step(order)

    inputs, d_result_turned, d_columns, to_relative = order.settle(
        (inputs, d_result_turned, d_columns, to_relative)
    )
    longer(gather_qkv, 4)
    gather_down.settle(order)
    d_other = order.settle(links.exchange(d_columns[half:], "c"))
    d_mine = d_columns[:half]
    gather_qkv.step(order)
    gather_up = Gather(
        links, [order(lambda values: values + 0, shard_up)], half + wide // 2
    )
    gather_qkv.step(order)
    longer(gather_up, 5)
    gather_up.step(order)
    slowest = [1, 2 ** len(links.y_bits)]
    in_pieces = half // 2 // slowest[1] % PAIR == 0
    ranges_down = []
    for slow in slowest:
        group = half // slow
        cuts = ((0, group // 2), (group // 2, group)) if in_pieces else ((0, group),)
        ranges_down.append(
            [
                [(core + at * group + low, core + at * group + high) for at in range(slow)]
                for core in (0, half)
                for low, high in cuts
            ]
        )
    d_late = order.settle(d_result_turned)
    grads_down = [
        d_result_turned,
        order.settle(
            jnp.concatenate(
                [d_late[:, low:high] for places in ranges_down[1] for low, high in places], 1
            )
        ),
    ]
    gather_qkv.step(order)
    gather_up.step(order)
    longer(gather_down, 5)
    gather_down.step(order)
    halves_qkv = gather_qkv.halves()
    normed_low, normed_high, normed_mine, normed_send, vector_rows, true_vectors = order(
        first_norm, inputs, *halves_qkv[0], to_relative
    )
    projected = [
        order(partial(project, at), normed_low, normed_high, *halves_qkv[at], true_vectors)
        for at in (0, 1)
    ]
    gather_up.step(order)
    gather_down.step(order)
    shared, peak = order(attend, projected, counts)
    peak, peak_got = [peak], []

    def peak_send(bit):
        sent = order.settle(peak[0])
        peak_got.append(links.exchange(sent, bit))

    def peak_take():
        peak[0] = order(jnp.maximum, peak[0], peak_got.pop())

    peak_bits = [links.bits[0], *links.z_bits[:2], links.orders[0][0], links.orders[1][0]]
    more_bits = [bit for bit in links.bits if bit not in peak_bits]
    gather_up.step(order)
    gather_down.step(order)
    halves_up = gather_up.halves()
    middle, normed_two_low, normed_two_high, normed_two_mine, normed_two_send = order(
        second_norm, inputs, shared, halves_up, vector_rows
    )
    normed_two_other = links.exchange(normed_two_send, "c")
    if in_pieces:
        gather_down.core_early(order)
    hidden, slope, hidden_other = [], [], []
    for at in (0, 1):
        out, out_slope = order(
            partial(expand, at), normed_two_low, normed_two_high, *halves_up[at], true_vectors
        )
        hidden.append(out)
        slope.append(out_slope)
        hidden_other.append(links.exchange(out, "c"))
        if at == 0:
            normed_two_other = order.settle(normed_two_other)
            if in_pieces:
                gather_down.early = order.settle(gather_down.early)

    down_parts = [
        order(
            partial(product_wide, slowest[at], 0, wide // 2),
            d_mine,
            d_other,
            hidden[at],
            hidden_other[at],
        )
        for at in (0, 1)
    ]
    if in_pieces:
        gather_down.core_late(order)
    else:
        gather_down.step(order)
    sum_down = Sum(links, order.settle(down_parts))
    shared_other = links.exchange(order.settle(shared), "c")
    normed_other = links.exchange(order.settle(normed_send), "c")
    weights_down = gather_down.pieces() if in_pieces else gather_down.halves()
    d_pre, d_pre_sums = order(expand_back, grads_down, weights_down, slope)
    d_pre_other = links.exchange(d_pre, "c")
    shared_other, normed_other = order.settle((shared_other, normed_other))
    peak_send(peak_bits[0])
    partial_sum = order(contract_first, d_pre, *halves_up[0])
    peak_take()
    peak_send(peak_bits[1])
    result = order(
        partial(finish_first, ranges=ranges_down[0]), middle, hidden[0], weights_down[0], vector_rows
    )
    peak_take()
    peak_send(peak_bits[2])
    for _ in links.orders[0][1:]:
        sum_down.step(order)
    peak_take()
    sum_up = Sum(
        links,
        [
            order(
                partial(product_wide, slowest[at], at * wide // 2, wide // 2),
                normed_two_mine,
                normed_two_other,
                d_pre,
                d_pre_other,
            )
            for at in (0, 1)
        ],
    )
    d_middle, d_branch_low, d_branch_high, d_out_one, d_out_two, grads = order(
        contract_second, d_pre, halves_up, partial_sum, middle, d_result_turned, vector_rows
    )
    d_branch_other = links.exchange(d_branch_high, "c")
    sum_down.step(order)
    d_branch_other = order.settle(d_branch_other)
    d_projected, d_projected_other, head_sums = [], [], []
    for at, d_out in enumerate((d_out_one, d_out_two)):
        out, sums = order(attend_back, projected[at], d_out, counts)
        d_projected.append(out)
        d_projected_other.append(links.exchange(out, "c"))
        head_sums.append(sums)


    def out_tile(at):
        return (d_branch_low, d_branch_other, shared, shared_other, half, (0, at))

    def qkv_tile(at, part, width, column):
        return (
            normed_mine,
            normed_other,
            d_projected[at],
            d_projected_other[at],
            width,
            (part, 0, column),
        )

    def late_product(at, tiles, extra=()):
        def call(operands, extra):
            return product(
                slowest[at],
                [(*operands[4 * i : 4 * i + 4], *tile[4:]) for i, tile in enumerate(tiles)],
                extra,
            )

        return order(call, [operand for tile in tiles for operand in tile[:4]], extra)

    partial_sum = order(input_back_first, d_projected[0], *halves_qkv[0])
    for _ in links.z_bits[1:]:
        sum_down.step(order)
    for _ in links.orders[0][1:]:
        sum_up.step(order)
    d_projected_other = order.settle(d_projected_other)
    quarter = half // 2
    sum_late = Sum(
        links,
        [
            late_product(at, [out_tile(at), qkv_tile(0, at, half, 0), qkv_tile(0, 2, quarter, at)])
            for at in (0, 1)
        ],
    )
    token_grad, vectors_low, vectors_high = order(
        input_back_second,
        d_projected[1],
        *halves_qkv[1],
        partial_sum,
        inputs,
        d_middle,
        grads,
        head_sums,
        d_pre_sums,
        vector_rows,
        to_relative,
    )
    token_grad = token_grad.reshape(seq_count, slot_count, model_width)
    sum_down.settle(order)
    vectors_other = links.exchange(vectors_high, "c")
    sum_up.step(order)
    last = [
        late_product(
            at,
            [qkv_tile(1, at, half, 0), qkv_tile(1, 2, quarter, at)],
            ((), (vectors_low, vectors_other))[at],
        )
        for at in (0, 1)
    ]
    sum_last = Sum(links, last)
    result = order(
        partial(finish_second, ranges=ranges_down[1]),
        result,
        hidden[1],
        weights_down[1],
        to_relative,
        counts,
    )
    result_out = result.reshape(seq_count, slot_count, model_width)
    for _ in links.orders[0][1:]:
        sum_late.step(order)
    for _ in links.z_bits[1:]:
        sum_up.step(order)
    for _ in links.orders[0][1:]:
        sum_last.step(order)
    sum_late.step(order)
    sum_last.step(order)
    peak_send(peak_bits[3])
    mean_down, mean_up = order.settle((mean_down, mean_up))
    sum_up.settle(order)
    peak_take()
    for bit in more_bits:
        peak_send(bit)
        peak_take()
    peak_send(peak_bits[4])
    for _ in links.z_bits[1:]:
        sum_late.step(order)
    peak_take()
    head_peak = order.settle(peak[0])[:, 0]
    vectors, mean_vectors, square_vectors, first_col = order.settle(
        (
            vectors,
            mean_vectors,
            square_vectors,
            lax.axis_index(("dp", "fsdp")) * shard_width,
        )
    )
    shrink = jnp.sqrt(clip_limit / jnp.maximum(head_peak, clip_limit))
    head_cols = jnp.repeat(shrink, head_width)
    qkv_scale = jnp.concatenate([head_cols, head_cols, jnp.ones((model_width,), F32)])[None]
    col_head = (first_col + jnp.arange(shard_width, dtype=jnp.int32)) // head_width
    col_shrink = jnp.sum(
        jnp.where(
            col_head[:, None] == jnp.arange(H, dtype=jnp.int32)[None, :], shrink[None, :], 0.0
        ),
        1,
    )[None]
    for _ in links.z_bits[1:]:
        sum_last.step(order)
    sum_late.settle(order)
    spans = (
        (0, half, 0, half),
        (1, 0, half, half),
        (0, half * 3 + quarter, 2 * half, half),
        (1, half + quarter, 3 * half, half),
        (0, 2 * half, 4 * half, quarter),
        (0, 4 * half + quarter, 4 * half + quarter, quarter),
        (1, half, 5 * half, quarter),
        (1, 2 * half + quarter, 5 * half + quarter, quarter),
    )
    vectors_at = 3 * half
    late = sum_late.total()
    reduced_out = jnp.concatenate([late[:, :half], late[:, 2 * half + quarter :][:, :half]], 1).T
    reduced_up = sum_up.total()
    reduced_down = sum_down.total().T
    mean_o, square_o, new_out = adam_step(
        w_out, reduced_out, mean_out, square_out, matrix_rate, weight_decay
    )
    mean_u, square_u, new_up = adam_step(
        w_up, reduced_up, mean_up, square_up, matrix_rate, weight_decay
    )
    mean_d, square_d, new_down = adam_step(
        w_down, reduced_down, mean_down, square_down, matrix_rate, weight_decay
    )
    if shard_width % 8 == 0:
        mean_q, square_q, new_qkv, mean_v, square_v, new_vectors = last_update(
            sum_late.pairs[0],
            sum_last.pairs[0],
            (spans, vectors_at),
            qkv_scale,
            (w_qkv, mean_qkv, square_qkv),
            col_shrink,
            (vectors, mean_vectors, square_vectors),
        )
    else:
        sums = (late, sum_last.total())
        reduced_qkv = jnp.concatenate(
            [sums[which][:, first : first + size] for which, first, _, size in spans], 1
        )
        mean_q, square_q, stepped_qkv = adam_step(
            w_qkv, reduced_qkv, mean_qkv, square_qkv, matrix_rate, weight_decay
        )
        new_qkv = stepped_qkv * qkv_scale
        reduced_vectors = sums[1][:, vectors_at : vectors_at + vector_count].T
        mean_v, square_v, stepped_vectors = adam_step(
            vectors, reduced_vectors, mean_vectors, square_vectors, vector_rate, 0.0
        )
        row_pick = (jnp.arange(vector_count, dtype=jnp.int32) == 4)[:, None]
        new_vectors = jnp.where(row_pick, stepped_vectors * col_shrink, stepped_vectors)
    return (
        result_out,
        token_grad,
        head_peak,
        mean_q,
        square_q,
        new_qkv,
        mean_o,
        square_o,
        new_out,
        mean_u,
        square_u,
        new_up,
        mean_d,
        square_d,
        new_down,
        mean_v,
        square_v,
        new_vectors,
    )


def solution(mesh):
    links = Links(mesh.shape["dp"], mesh.shape["fsdp"])
    return jax.shard_map(
        partial(local, links),
        mesh=mesh,
        in_specs=(
            P(("dp", "fsdp"), None, None),
            P(("dp", "fsdp"), None, None),
            P(("dp", "fsdp")),
            P(("dp", "fsdp"), None),
            P(None, ("dp", "fsdp")),
            P(("dp", "fsdp"), None),
            P(None, ("dp", "fsdp")),
            P(None, ("dp", "fsdp")),
            P(("dp", "fsdp"), None),
            P(None, ("dp", "fsdp")),
            P(("dp", "fsdp"), None),
            P(None, ("dp", "fsdp")),
            P(None, ("dp", "fsdp")),
            P(("dp", "fsdp"), None),
            P(None, ("dp", "fsdp")),
            P(("dp", "fsdp"), None),
            P(None, ("dp", "fsdp")),
            P(None, ("dp", "fsdp")),
        ),
        out_specs=(
            P(("dp", "fsdp"), None, None),
            P(("dp", "fsdp"), None, None),
            P(),
            P(("dp", "fsdp"), None),
            P(("dp", "fsdp"), None),
            P(("dp", "fsdp"), None),
            P(None, ("dp", "fsdp")),
            P(None, ("dp", "fsdp")),
            P(None, ("dp", "fsdp")),
            P(("dp", "fsdp"), None),
            P(("dp", "fsdp"), None),
            P(("dp", "fsdp"), None),
            P(None, ("dp", "fsdp")),
            P(None, ("dp", "fsdp")),
            P(None, ("dp", "fsdp")),
            P(None, ("dp", "fsdp")),
            P(None, ("dp", "fsdp")),
            P(None, ("dp", "fsdp")),
        ),
        check_vma=False,
    )
```

```python
from functools import partial

import jax
import jax.numpy as jnp
import numpy as np
from jax import lax
from jax.experimental import pallas as pl
from jax.experimental.pallas import tpu as pltpu
from jax.sharding import PartitionSpec as P

H = 16
STEP = 10


beta_one = 0.9
beta_two = 0.95
adam_epsilon = 1e-08
weight_decay = 0.1
matrix_rate = 0.1
vector_rate = 0.5
clip_limit = 8.0
norm_epsilon = 1e-06
masked_value = -1e30
TILE = 512
PAIR = 128
HALF_ROOT = 0.5**0.5
DENSITY = 0.3989422804014327
F32 = jnp.float32
BF16 = jnp.bfloat16


def adam_step(weight, gradient, mean_old, square_old, step_rate, decay_rate):
    mean_new = beta_one * mean_old + (1.0 - beta_one) * gradient
    square_new = beta_two * square_old + (1.0 - beta_two) * gradient * gradient
    fix_one = 1.0 - beta_one**STEP
    fix_two = 1.0 - beta_two**STEP
    stepped = weight - step_rate * (
        mean_new / fix_one / (jnp.sqrt(square_new / fix_two) + adam_epsilon) + decay_rate * weight
    )
    return (mean_new, square_new, stepped)


def bit_names(letter, count):
    return tuple(letter + str(at) for at in range(count))


class Links:
    def __init__(self, dp_count, inner_count):
        self.device_count = dp_count * inner_count
        inner_bits = inner_count.bit_length() - 1
        z_bits = bit_names("z", dp_count.bit_length() - 2)
        x_bits = bit_names("x", inner_bits // 2)
        y_bits = bit_names("y", inner_bits - inner_bits // 2)
        self.place = {"c": ("dp", dp_count, 0)}
        self.place.update({bit: ("dp", dp_count, at + 1) for at, bit in enumerate(z_bits)})
        self.place.update({bit: ("fsdp", inner_count, at) for at, bit in enumerate(x_bits)})
        self.place.update(
            {bit: ("fsdp", inner_count, at + len(x_bits)) for at, bit in enumerate(y_bits)}
        )
        self.bits = ("c",) + y_bits + x_bits + z_bits
        self.orders = (y_bits + x_bits, x_bits + y_bits)
        self.z_bits = z_bits
        self.y_bits = y_bits
        self.inner_bits = inner_bits

    def true_block(self):
        masks = []
        for block in range(self.device_count):
            mask = 0
            for at, bit in enumerate(reversed(self.bits)):
                if block >> at & 1:
                    axis, _, place = self.place[bit]
                    mask |= 1 << (place + (self.inner_bits if axis == "dp" else 0))
            masks.append(mask)
        return lax.axis_index(("dp", "fsdp")) ^ jnp.array(masks, jnp.int32)

    def exchange(self, values, *bits):
        axis, count, _ = self.place[bits[0]]
        mask = sum(1 << self.place[bit][2] for bit in bits)
        return lax.ppermute(values, axis, [(at, at ^ mask) for at in range(count)])


class Order:
    def __init__(self):
        self.ended = ()

    def __call__(self, call, *operands):
        operands, _ = lax.optimization_barrier((operands, self.ended))
        result = call(*operands)
        self.ended = result
        return result

    def settle(self, value):
        return self(lambda come: come, value)


def run(body, operands, outs, grid=(), in_specs=None, out_specs=None, scratch=()):
    whole = pl.BlockSpec(memory_space=pltpu.VMEM)
    return pl.pallas_call(
        body,
        out_shape=[
            pltpu.HBM(shape, kind) if hbm else jax.ShapeDtypeStruct(shape, kind)
            for shape, kind, *hbm in outs
        ],
        grid=grid,
        in_specs=in_specs or [whole] * len(operands),
        out_specs=out_specs or [whole] * len(outs),
        scratch_shapes=scratch,
        compiler_params=pltpu.CompilerParams(vmem_limit_bytes=12 * 2**20),
        cost_estimate=pl.CostEstimate(flops=24 * 10**9, bytes_accessed=1000, transcendentals=0),
    )(*operands)


def fixed(shape):
    return pl.BlockSpec(shape, lambda j: (0,) * len(shape))


def mm(first, second):
    return lax.dot_general(first, second, (((1,), (0,)), ((), ())), preferred_element_type=F32)


def mm_turned(first, second):
    return lax.dot_general(first, second, (((1,), (1,)), ((), ())), preferred_element_type=F32)


def mm_rows(first, second):
    return lax.dot_general(first, second, (((0,), (0,)), ((), ())), preferred_element_type=F32)


def pieces(values, count=3):
    out = []
    for _ in range(count):
        piece = values.astype(BF16)
        out.append(piece)
        values = values - piece.astype(F32)
    return out


def normalized(values):
    centered = values - jnp.mean(values, -1, keepdims=True)
    scale = lax.rsqrt(jnp.mean(centered * centered, -1, keepdims=True) + norm_epsilon)
    return centered * scale, scale


def norm_back(grad, values, gain):
    unit, scale = normalized(values)
    inner = grad * gain
    d_values = scale * (
        inner
        - jnp.mean(inner, -1, keepdims=True)
        - unit * jnp.mean(inner * unit, -1, keepdims=True)
    )
    return (
        d_values,
        jnp.sum(grad * unit, 0, keepdims=True),
        jnp.sum(grad, 0, keepdims=True),
    )


def first_norm(inputs, mine, other, to_relative):
    rows, width = inputs.shape
    half = width // 2

    def body(
        x_ref, mine_ref, other_ref, turn_ref, low_ref, high_ref, lowt_ref, hight_ref, rel_ref, true_ref
    ):
        turned = jnp.concatenate(
            [mine_ref[...].astype(F32).T, other_ref[...].astype(F32).T], 1
        )[:16]
        rel_ref[...] = turned
        true_ref[...] = mm_turned(turned.astype(BF16), turn_ref[...])
        unit, _ = normalized(x_ref[...].astype(F32))
        normed = (unit * turned[0:1] + turned[1:2]).astype(BF16)
        low_ref[...] = normed[:, :half]
        high_ref[...] = normed[:, half:]
        lowt_ref[...] = normed[:, :half].T
        hight_ref[...] = normed[:, half:].T

    vectors_at = mine.shape[1] // PAIR - 1
    weights = pl.BlockSpec((half, PAIR), lambda j: (0, vectors_at))
    return run(
        body,
        (inputs, mine, other, to_relative),
        [((rows, half), BF16)] * 2 + [((half, rows), BF16)] * 2 + [((16, width), F32)] * 2,
        (1,),
        [fixed(inputs.shape), weights, weights, fixed(to_relative.shape)],
        [fixed((rows, half))] * 2 + [fixed((half, rows))] * 2 + [fixed((16, width))] * 2,
    )


def project(at, low, high, mine, other, true_vectors):
    rows, half = low.shape

    def body(low_ref, high_ref, mine_ref, other_ref, vec_ref, out_ref):
        j = pl.program_id(0)
        bias = jnp.where(j == 0, vec_ref[4:5, :], jnp.where(j == 2, vec_ref[5:6, :], 0.0))
        value = mm(low_ref[...], mine_ref[...]) + mm(high_ref[...], other_ref[...])
        out_ref[0] = (value + bias).astype(BF16)

    weights = pl.BlockSpec((half, TILE), lambda j: (0, j))
    return run(
        body,
        (low, high, mine, other, true_vectors),
        [((3, rows, TILE), BF16)],
        (3,),
        [fixed(low.shape)] * 2 + [weights] * 2 + [pl.BlockSpec((16, TILE), lambda j: (0, at))],
        [pl.BlockSpec((1, rows, TILE), lambda j: (j, 0, 0))],
    )[0]


def head_mask(rows, side):
    lane = lax.broadcasted_iota(jnp.int32, (rows, PAIR), 1)
    return lane < PAIR // 2 if side == 0 else lane >= PAIR // 2


def attend(projected, counts):
    _, rows, width = projected[0].shape
    steps = width // PAIR

    def body(count_ref, *refs):
        *ins, out_ref, peak_ref = refs
        j = pl.program_id(0)

        def heads(q_ref, k_ref, v_ref):
            count = count_ref[0]
            key_ok = lax.broadcasted_iota(jnp.int32, (rows, rows), 1) < count
            row_ok = lax.broadcasted_iota(jnp.int32, (rows, 1), 0) < count
            queries = q_ref[0]
            out = None
            for side in (0, 1):
                chosen = head_mask(rows, side)
                scores = mm_turned(jnp.where(chosen, queries, 0), k_ref[0]) * (PAIR // 2) ** -0.5
                scores = jnp.where(key_ok, scores, masked_value)
                top = jnp.max(scores, -1, keepdims=True)
                peak = jnp.max(jnp.where(row_ok, top, masked_value))
                peak_ref[pl.ds(j * 2 + side, 1), :] = jnp.full((1, PAIR), peak)
                exponent = jnp.exp(scores - top)
                probs = exponent * (1.0 / jnp.sum(exponent, -1, keepdims=True))
                value = mm(probs.astype(BF16), v_ref[0])
                out = value if side == 0 else jnp.where(chosen, value, out)
            out_ref[...] = out.astype(BF16)

        @pl.when(j < steps)
        def _():
            heads(*ins[:3])

        @pl.when(j >= steps)
        def _():
            heads(*ins[3:])

    def part(index, at):
        return pl.BlockSpec(
            (1, rows, PAIR), lambda j: (index, 0, jnp.clip(j - at * steps, 0, steps - 1))
        )

    return run(
        body,
        (counts, *[projected[0]] * 3, *[projected[1]] * 3),
        [((rows, 2 * width), BF16), ((4 * steps, PAIR), F32)],
        (2 * steps,),
        [pl.BlockSpec(memory_space=pltpu.SMEM)]
        + [part(index, at) for at in (0, 1) for index in range(3)],
        [pl.BlockSpec((rows, PAIR), lambda j: (0, j)), fixed((4 * steps, PAIR))],
    )


def attend_back(projected, d_out, counts):
    _, rows, width = projected.shape
    steps = width // PAIR
    scale = (PAIR // 2) ** -0.5

    def body(count_ref, q_ref, k_ref, v_ref, d_ref, out_ref, sum_ref):
        key_ok = lax.broadcasted_iota(jnp.int32, (rows, rows), 0) < count_ref[0]
        queries, keys, values, grad = q_ref[0], k_ref[0], v_ref[0], d_ref[...]
        parts = [None] * 3
        for side in (0, 1):
            chosen = head_mask(rows, side)
            scores = mm_turned(jnp.where(chosen, keys, 0), queries) * scale
            scores = jnp.where(key_ok, scores, masked_value)
            exponent = jnp.exp(scores - jnp.max(scores, 0, keepdims=True))
            probs = exponent * (1.0 / jnp.sum(exponent, 0, keepdims=True))
            d_probs = mm_turned(jnp.where(chosen, values, 0), grad)
            inner = jnp.sum(probs * d_probs, 0, keepdims=True)
            d_scores = (probs * (d_probs - inner)).astype(BF16)
            new = [
                mm_rows(d_scores, keys) * scale,
                mm(d_scores, queries) * scale,
                mm(probs.astype(BF16), grad),
            ]
            parts = new if side == 0 else [jnp.where(chosen, n, p) for n, p in zip(new, parts)]
        low = [part.astype(BF16) for part in parts]
        for at in range(3):
            out_ref[at] = low[at]
        sum_ref[0:1, :] = jnp.sum(low[0].astype(F32), 0, keepdims=True)
        sum_ref[1:2, :] = jnp.sum(low[2].astype(F32), 0, keepdims=True)

    def part(index):
        return pl.BlockSpec((1, rows, PAIR), lambda j: (index, 0, j))

    columns = pl.BlockSpec((rows, PAIR), lambda j: (0, j))
    return run(
        body,
        (counts, projected, projected, projected, d_out),
        [((3, rows, width), BF16), ((8, width), F32)],
        (steps,),
        [pl.BlockSpec(memory_space=pltpu.SMEM), part(0), part(1), part(2), columns],
        [
            pl.BlockSpec((3, rows, PAIR), lambda j: (0, 0, j)),
            pl.BlockSpec((8, PAIR), lambda j: (0, j)),
        ],
    )


def second_norm(inputs, attended, weights, vectors):
    rows, width = inputs.shape
    half = width // 2

    def body(x_ref, a_ref, b_ref, wa_ref, wa2_ref, wb_ref, wb2_ref, vec_ref, mid_ref, low_ref, high_ref, lowt_ref, hight_ref):
        first, second = a_ref[...], b_ref[...]
        branch = jnp.concatenate(
            [
                mm_turned(first, wa_ref[...]) + mm_turned(second, wb_ref[...]),
                mm_turned(first, wa2_ref[...]) + mm_turned(second, wb2_ref[...]),
            ],
            1,
        )
        middle = x_ref[...].astype(F32) + branch + vec_ref[6:7, :]
        mid_ref[...] = middle
        unit, _ = normalized(middle)
        normed = (unit * vec_ref[2:3, :] + vec_ref[3:4, :]).astype(BF16)
        low_ref[...] = normed[:, :half]
        high_ref[...] = normed[:, half:]
        lowt_ref[...] = normed[:, :half].T
        hight_ref[...] = normed[:, half:].T

    block = pl.BlockSpec((half, TILE), lambda j: (0, 0))
    return run(
        body,
        (inputs, attended, attended, *weights[0], *weights[1], vectors),
        [((rows, width), F32)] + [((rows, half), BF16)] * 2 + [((half, rows), BF16)] * 2,
        (1,),
        [fixed(inputs.shape)]
        + [pl.BlockSpec((rows, TILE), lambda j, at=at: (0, at)) for at in (0, 1)]
        + [block] * 4
        + [fixed(vectors.shape)],
        [fixed((rows, width))] + [fixed((rows, half))] * 2 + [fixed((half, rows))] * 2,
    )


def expand(at, low, high, mine, other, true_vectors):
    rows, half = low.shape
    count = mine.shape[1] - TILE
    per_row = true_vectors.shape[1] // TILE
    first_row = 8 + at * count // true_vectors.shape[1]

    def body(low_ref, high_ref, mine_ref, other_ref, vec_ref, out_ref, slope_ref):
        row = first_row + pl.program_id(0) // per_row
        pre = mm(low_ref[...], mine_ref[...]) + mm(high_ref[...], other_ref[...])
        pre = pre + vec_ref[pl.ds(row, 1), :]
        below = 0.5 * (1.0 + lax.erf(pre * HALF_ROOT))
        out_ref[...] = (pre * below).astype(BF16)
        slope = below + pre * (DENSITY * jnp.exp(-0.5 * pre * pre))
        slope_ref[...] = slope.astype(BF16)

    weights = pl.BlockSpec((half, TILE), lambda j: (0, j + 1))
    columns = pl.BlockSpec((rows, TILE), lambda j: (0, j))
    return run(
        body,
        (low, high, mine, other, true_vectors),
        [((rows, count), BF16), ((rows, count), BF16, "hbm")],
        (count // TILE,),
        [fixed(low.shape)] * 2
        + [weights] * 2
        + [pl.BlockSpec((16, TILE), lambda j: (0, j % per_row))],
        [columns, columns],
    )


def among(count, at, shape):
    return pl.BlockSpec(shape, lambda j: (0, jnp.clip(j - at * count, 0, count - 1)))


def expand_back(grads, weights, slopes):
    rows = slopes[0].shape[0]
    steps = slopes[0].shape[1] // TILE
    counts = [len(pieces) for pieces in weights]
    operands, specs = [], []
    for at, (left, rights) in enumerate(zip(grads, weights)):
        operands += [left] * len(rights) + [*rights]
        specs += [
            pl.BlockSpec((rows, right.shape[0]), lambda j, piece=piece: (0, piece))
            for piece, right in enumerate(rights)
        ]
        specs += [among(steps, at, (right.shape[0], TILE)) for right in rights]

    def body(*refs):
        *ins, first_slope, second_slope, out_ref, sum_ref = refs
        j = pl.program_id(0)
        for at, slope_ref in enumerate((first_slope, second_slope)):
            first = 2 * sum(counts[:at])
            lefts, rights = ins[first : first + counts[at]], ins[first + counts[at] :][: counts[at]]

            @pl.when(j // steps == at)
            def _(lefts=lefts, rights=rights, slope_ref=slope_ref):
                value = sum(mm(left[...], right[...]) for left, right in zip(lefts, rights))
                value = (value * slope_ref[...].astype(F32)).astype(BF16)
                out_ref[...] = value
                sum_ref[...] = jnp.sum(value.astype(F32), 0, keepdims=True)

    count = 2 * steps
    return run(
        body,
        (*operands, *slopes),
        [((rows, count * TILE), BF16), ((1, count * TILE), F32)],
        (count,),
        specs + [among(steps, at, (rows, TILE)) for at in range(2)],
        [pl.BlockSpec((rows, TILE), lambda j: (0, j)), pl.BlockSpec((1, TILE), lambda j: (0, j))],
    )


def contract_first(d_pre, mine, other):
    rows, count = d_pre.shape
    half = mine.shape[0]
    count = count // 2

    def body(d_ref, mine_ref, other_ref, out_ref):
        @pl.when(pl.program_id(0) == 0)
        def _():
            out_ref[...] = jnp.zeros_like(out_ref)

        out_ref[:, :half] += mm_turned(d_ref[...], mine_ref[...])
        out_ref[:, half:] += mm_turned(d_ref[...], other_ref[...])

    weights = pl.BlockSpec((half, TILE), lambda j: (0, j + 1))
    return run(
        body,
        (d_pre, mine, other),
        [((rows, 2 * half), F32)],
        (count // TILE,),
        [pl.BlockSpec((rows, TILE), lambda j: (0, j)), weights, weights],
        [fixed((rows, 2 * half))],
    )[0]


def contract_second(d_pre, weights, partial_sum, middle, d_result, vectors):
    rows, count = d_pre.shape
    half = weights[0][0].shape[0]
    width = 2 * half
    steps = count // 2 // TILE

    def body(
        d_ref, mine_ref, other_ref, wa_ref, wa2_ref, wb_ref, wb2_ref, sum_ref, mid_ref, res_ref,
        vec_ref, dm_ref, low_ref, high_ref, outa_ref, outb_ref, grads_ref, total,
    ):
        j = pl.program_id(0)

        @pl.when(j == 0)
        def _():
            total[...] = sum_ref[...]

        total[:, :half] += mm_turned(d_ref[...], mine_ref[...])
        total[:, half:] += mm_turned(d_ref[...], other_ref[...])

        @pl.when(j == steps - 1)
        def _():
            d_values, d_gain, d_shift = norm_back(total[...], mid_ref[...], vec_ref[2:3, :])
            result_grad = res_ref[...].astype(F32)
            d_middle = result_grad + d_values
            branch = d_middle.astype(BF16)
            dm_ref[...] = d_middle
            first, second = branch[:, :half], branch[:, half:]
            low_ref[...] = first.T
            high_ref[...] = second.T
            outa_ref[...] = (mm(first, wa_ref[...]) + mm(second, wa2_ref[...])).astype(BF16)
            outb_ref[...] = (mm(first, wb_ref[...]) + mm(second, wb2_ref[...])).astype(BF16)
            grads_ref[0:1, :] = d_gain
            grads_ref[1:2, :] = d_shift
            grads_ref[2:3, :] = jnp.sum(branch.astype(F32), 0, keepdims=True)
            grads_ref[3:4, :] = jnp.sum(result_grad, 0, keepdims=True)

    tile = pl.BlockSpec((half, TILE), lambda j: (0, j + 1))
    block = pl.BlockSpec((half, TILE), lambda j: (0, 0))
    return run(
        body,
        (d_pre, *weights[1], *weights[0], *weights[1], partial_sum, middle, d_result, vectors),
        [((rows, width), F32)]
        + [((half, rows), BF16)] * 2
        + [((rows, TILE), BF16)] * 2
        + [((8, width), F32)],
        (steps,),
        [pl.BlockSpec((rows, TILE), lambda j: (0, steps + j)), tile, tile]
        + [block] * 4
        + [fixed((rows, width))] * 3
        + [fixed(vectors.shape)],
        [fixed((rows, width))]
        + [fixed((half, rows))] * 2
        + [fixed((rows, TILE))] * 2
        + [fixed((8, width))],
        [pltpu.VMEM((rows, width), F32)],
    )


def input_back_first(d_projected, mine, other):
    rows = d_projected.shape[1]
    half = mine.shape[0]

    def body(d_ref, mine_ref, other_ref, out_ref):
        @pl.when(pl.program_id(0) == 0)
        def _():
            out_ref[...] = jnp.zeros_like(out_ref)

        out_ref[:, :half] += mm_turned(d_ref[0], mine_ref[...])
        out_ref[:, half:] += mm_turned(d_ref[0], other_ref[...])

    weights = pl.BlockSpec((half, TILE), lambda j: (0, j))
    return run(
        body,
        (d_projected, mine, other),
        [((rows, 2 * half), F32)],
        (3,),
        [pl.BlockSpec((1, rows, TILE), lambda j: (j, 0, 0)), weights, weights],
        [fixed((rows, 2 * half))],
    )[0]


def input_back_second(
    d_projected, mine, other, partial_sum, inputs, d_middle, grads, head_sums, d_pre_sums, vectors, to_relative
):
    rows = d_projected.shape[1]
    half = mine.shape[0]
    width = 2 * half

    def body(
        d_ref, mine_ref, other_ref, sum_ref, x_ref, dm_ref, grads_ref, heada_ref, headb_ref, pre_ref,
        vec_ref, turn_ref, out_ref, low_ref, high_ref, total, true_rows, all_rows,
    ):
        j = pl.program_id(0)

        @pl.when(j == 0)
        def _():
            total[...] = sum_ref[...]

        total[:, :half] += mm_turned(d_ref[0], mine_ref[...])
        total[:, half:] += mm_turned(d_ref[0], other_ref[...])

        @pl.when(j == 2)
        def _():
            d_values, d_gain, d_shift = norm_back(total[...], x_ref[...].astype(F32), vec_ref[0:1, :])
            low = (dm_ref[...] + d_values).astype(BF16)
            out_ref[...] = mm_turned(low, turn_ref[...]).astype(BF16)
            true_rows[...] = jnp.zeros_like(true_rows)
            for at, ref in enumerate((heada_ref, headb_ref)):
                true_rows[0:2, at * TILE : (at + 1) * TILE] = ref[0:2, :]
            for part in range(pre_ref.shape[1] // width):
                row = 2 + part
                true_rows[row : row + 1, :] = pre_ref[:, part * width : (part + 1) * width]
            turned = sum(mm(part, turn_ref[...]) for part in pieces(true_rows[...]))
            all_rows[...] = jnp.zeros_like(all_rows)
            all_rows[0:1, :] = d_gain
            all_rows[1:2, :] = d_shift
            all_rows[2:4, :] = grads_ref[0:2, :]
            all_rows[4:6, :] = turned[0:2]
            all_rows[6:8, :] = grads_ref[2:4, :]
            all_rows[8:14, :] = turned[2:8]
            columns = all_rows[...].T
            low_ref[...] = columns[:half]
            high_ref[...] = columns[half:]

    weights = pl.BlockSpec((half, TILE), lambda j: (0, j))
    operands = (
        d_projected,
        mine,
        other,
        partial_sum,
        inputs,
        d_middle,
        grads,
        *head_sums,
        d_pre_sums,
        vectors,
        to_relative,
    )
    return run(
        body,
        operands,
        [((rows, width), BF16)] + [((half, PAIR), F32)] * 2,
        (3,),
        [pl.BlockSpec((1, rows, TILE), lambda j: (j, 0, 0)), weights, weights]
        + [fixed(operand.shape) for operand in operands[3:]],
        [fixed((rows, width))] + [fixed((half, PAIR))] * 2,
        [pltpu.VMEM((rows, width), F32), pltpu.VMEM((8, width), F32), pltpu.VMEM((PAIR, width), F32)],
    )


def contract_hidden(hidden, weights, ranges, total):
    for ref, places in zip(weights, ranges):
        value = mm_turned(hidden[...], ref[...])
        first = 0
        for low, high in places:
            total[:, low:high] += value[:, first : first + high - low]
            first += high - low


def finish_first(middle, hidden, weights, vectors, ranges):
    rows, width = middle.shape
    steps = hidden.shape[1] // TILE

    def body(hidden_ref, *refs):
        *weight_refs, mid_ref, vec_ref, out_ref = refs

        @pl.when(pl.program_id(0) == 0)
        def _():
            out_ref[...] = mid_ref[...] + vec_ref[7:8, :]

        contract_hidden(hidden_ref, weight_refs, ranges, out_ref)

    columns = pl.BlockSpec((rows, TILE), lambda j: (0, j))
    return run(
        body,
        (hidden, *weights, middle, vectors),
        [((rows, width), F32)],
        (steps,),
        [columns]
        + [pl.BlockSpec((right.shape[0], TILE), lambda j: (0, j)) for right in weights]
        + [fixed((rows, width)), fixed(vectors.shape)],
        [fixed((rows, width))],
    )[0]


def finish_second(partial_sum, hidden, weights, to_relative, counts, ranges):
    rows, width = partial_sum.shape
    steps = hidden.shape[1] // TILE

    def body(count_ref, hidden_ref, *refs):
        *weight_refs, sum_ref, turn_ref, out_ref, total = refs

        @pl.when(pl.program_id(0) == 0)
        def _():
            total[...] = sum_ref[...]

        contract_hidden(hidden_ref, weight_refs, ranges, total)

        @pl.when(pl.program_id(0) == steps - 1)
        def _():
            kept = lax.broadcasted_iota(jnp.int32, (rows, 1), 0) < count_ref[0]
            low = jnp.where(kept, total[...], 0.0).astype(BF16)
            out_ref[...] = mm_turned(low, turn_ref[...]).astype(BF16)

    columns = pl.BlockSpec((rows, TILE), lambda j: (0, j))
    return run(
        body,
        (counts, hidden, *weights, partial_sum, to_relative),
        [((rows, width), BF16)],
        (steps,),
        [pl.BlockSpec(memory_space=pltpu.SMEM), columns]
        + [pl.BlockSpec((right.shape[0], TILE), lambda j: (0, j)) for right in weights]
        + [fixed((rows, width)), fixed(to_relative.shape)],
        [fixed((rows, width))],
        [pltpu.VMEM((rows, width), F32)],
    )[0]


def product(slowest, tiles, extra=()):
    count, rows = tiles[0][0].shape
    operands, specs = [], []
    for *both, width, place in tiles:
        operands += both
        specs += [fixed((count, rows))] * 2
        shape = (1,) * (len(place) - 2) + (rows, width)
        specs += [pl.BlockSpec(shape, lambda j, place=place: place)] * 2
    width = sum(tile[4] for tile in tiles)
    full = width + (extra[0].shape[1] if extra else 0)
    operands += extra
    specs += [fixed(operand.shape) for operand in extra]

    def body(*refs):
        *ins, sent_ref, kept_ref = refs
        first = 0
        for at, tile in enumerate(tiles):
            left, left_other, right, right_other = (
                ref[0] if len(ref.shape) == 3 else ref[...] for ref in ins[4 * at : 4 * at + 4]
            )
            value = (mm(left, right) + mm(left_other, right_other)).astype(BF16)
            columns = slice(first, first + tile[4])
            first += tile[4]
            cut_rows(value, slowest, sent_ref, kept_ref, columns)
        if extra:
            value = (ins[-2][...] + ins[-1][...]).astype(BF16)
            cut_rows(value, slowest, sent_ref, kept_ref, slice(width, full))

    out = (count // 2, full)
    return run(body, operands, [(out, BF16)] * 2, (1,), specs, [fixed(out)] * 2)


def cut_rows(value, slowest, sent_ref, kept_ref, columns):
    part = value.shape[0] // 2 // slowest
    for group in range(slowest):
        low = 2 * group * part
        rows = slice(group * part, (group + 1) * part)
        kept_ref[rows, columns] = value[low : low + part]
        sent_ref[rows, columns] = value[low + part : low + 2 * part]


def product_wide(slowest, first, width, left, left_other, right, right_other):
    rows = right.shape[0]
    count = left.shape[0]

    def body(left_ref, left_other_ref, right_ref, right_other_ref, sent_ref, kept_ref):
        value = mm(left_ref[...], right_ref[...]) + mm(left_other_ref[...], right_other_ref[...])
        cut_rows(value.astype(BF16), slowest, sent_ref, kept_ref, slice(None))

    columns = pl.BlockSpec((rows, TILE), lambda j: (0, first // TILE + j))
    out_columns = pl.BlockSpec((count // 2, TILE), lambda j: (0, j))
    return run(
        body,
        (left, left_other, right, right_other),
        [((count // 2, width), BF16, "hbm")] * 2,
        (width // TILE,),
        [fixed(left.shape)] * 2 + [columns] * 2,
        [out_columns] * 2,
    )


def added(first, second, kind=BF16):
    return (first.astype(F32) + second.astype(F32)).astype(kind)


def halved(pairs, joined):
    half = pairs[0][0].shape[0] // 2
    widths = [mine.shape[1] for mine, _ in pairs]
    if half % 16:
        totals = [added(*pair) for pair in pairs]
        if joined:
            totals = [jnp.concatenate(totals, 1)]
        return [(total[half:], total[:half]) for total in totals]

    def body(*refs):
        ins, outs = refs[: 2 * len(pairs)], refs[2 * len(pairs) :]
        for at in range(len(pairs)):
            mine, got = ins[2 * at], ins[2 * at + 1]
            sent_ref, kept_ref = outs[:2] if joined else outs[2 * at : 2 * at + 2]
            first = sum(widths[:at]) if joined else 0
            columns = slice(first, first + widths[at])
            sent_ref[:, columns] = added(mine[half:, :], got[half:, :])
            kept_ref[:, columns] = added(mine[:half, :], got[:half, :])

    out_widths = [sum(widths)] if joined else widths
    outs = [((half, width), BF16) for width in out_widths for _ in range(2)]
    outs = run(body, [v for pair in pairs for v in pair], outs)
    return [tuple(outs[at : at + 2]) for at in range(0, len(outs), 2)]


def joined(places, middle, count, mine, got):
    wide = mine[0].shape[-1] if len(mine) == 1 else sum(value.shape[-1] for value in mine)
    parts = (slice(0, middle), slice(middle, wide))
    pairs = list(zip(places, mine, got))
    shapes = [(*value.shape[:at], 2, *value.shape[at:]) for at, value, _ in pairs]

    def widths(shape):
        if count == 1:
            return [(*shape[:-1], wide)]
        return [(*shape[:-1], part.stop - part.start) for part in parts]

    out_shapes = shapes if len(mine) == count else widths(shapes[0])
    if mine[0].shape[-2] % 16:
        both = [jnp.stack([value, come], at) for at, value, come in pairs]
        if len(mine) == count:
            return both
        if count == 1:
            rest = both[0].shape[:-1]
            return [jnp.concatenate([value.reshape(*rest, -1) for value in both], -1)]
        return [both[0][..., part] for part in parts]

    def body(*refs):
        outs = refs[2 * len(mine) :]
        for at, (place, value, _) in enumerate(pairs):
            for side in (0, 1):
                ref = refs[at + side * len(mine)]
                lead = (slice(None),) * place + (side,) + (slice(None),) * (value.ndim - 1 - place)
                if len(mine) == count:
                    outs[at][(*lead, slice(None))] = ref[...]
                elif count == 1:
                    outs[0][(*lead, parts[at])] = ref[...]
                else:
                    for out_ref, part in zip(outs, parts):
                        out_ref[(*lead, slice(None))] = ref[..., part]

    return run(body, [*mine, *got], [(shape, BF16) for shape in out_shapes])


def joined_all(bits, middle, blocks):
    rows, wide = blocks[0].shape
    parts = (slice(0, middle), slice(middle, wide))
    shape = (2,) * bits
    if rows % 16:
        whole = jnp.stack(blocks).reshape(*shape, rows, wide)
        return [whole[..., part] for part in parts]

    def body(*refs):
        for at, ref in enumerate(refs[: len(blocks)]):
            lead = tuple(at >> (bits - 1 - bit) & 1 for bit in range(bits))
            for out_ref, part in zip(refs[len(blocks) :], parts):
                out_ref[(*lead, slice(None), slice(None))] = ref[:, part]

    return run(
        body, blocks, [((*shape, rows, part.stop - part.start), BF16) for part in parts]
    )


class Sum:
    def __init__(self, links, firsts):
        self.links = links
        self.left, self.pairs = [], []
        self.z_left = links.z_bits
        for parts, order in zip(firsts, links.orders):
            self.add(parts, order)

    def add(self, parts, order):
        sent, kept = parts
        self.left.append(order[1:])
        self.pairs.append((kept, self.links.exchange(sent, order[0])))

    def step(self, order):
        inner = bool(self.left[0])
        joined = not inner and len(self.pairs) > 1
        parts = order(partial(halved, joined=joined), self.pairs)
        if inner:
            bits = [left[0] for left in self.left]
            self.left = [left[1:] for left in self.left]
        else:
            bits = [self.z_left[0]]
            self.z_left = self.z_left[1:]
        self.pairs = [
            (kept, self.links.exchange(sent, bit)) for (sent, kept), bit in zip(parts, bits)
        ]

    def settle(self, order):
        self.pairs = [(kept, order.settle(got)) for kept, got in self.pairs]

    def total(self):
        return added(*self.pairs[0], F32)


class Gather:
    def __init__(self, links, shards, middle, at_once=False):
        self.links, self.middle = links, middle
        steps = [tuple(reversed(order)) for order in links.orders]
        steps = list(zip(*steps))
        between = len(steps) // 2 if len(shards) == 2 else 0
        z_steps = ["all z"] if at_once else [(bit,) for bit in reversed(links.z_bits)]
        self.steps = steps[:between] + z_steps + steps[between:] + [("c", "c")]
        self.blocks = list(shards)
        self.bits = [(), ()]
        self.send()

    def send(self):
        if self.steps[0] == "all z":
            z_bits = self.links.z_bits
            chosen = [
                [bit for at, bit in enumerate(z_bits) if block >> (len(z_bits) - 1 - at) & 1]
                for block in range(1, 2 ** len(z_bits))
            ]
            self.got = [self.links.exchange(self.blocks[0], *bits) for bits in chosen]
            return
        self.got = [
            self.links.exchange(block, bit) for block, bit in zip(self.blocks, self.steps[0])
        ]

    def join(self, order):
        done, *self.steps = self.steps
        if done == "all z":
            z_bits = self.links.z_bits
            self.bits = [z_bits, z_bits]
            self.blocks = order(
                partial(joined_all, len(z_bits), self.middle), [*self.blocks, *self.got]
            )
            return
        bits = done * 2 if len(done) == 1 else done
        places = []
        for at, bit in enumerate(bits):
            held = sorted((*self.bits[at], bit), key=self.links.bits.index)
            self.bits[at] = tuple(held)
            places.append(held.index(bit))
        self.blocks = order(
            partial(joined, places, self.middle, len(self.steps[0])), self.blocks, self.got
        )
        if self.steps[0][0] == "c":
            self.blocks = [block.reshape(-1, block.shape[-1]) for block in self.blocks]

    def step(self, order):
        self.join(order)
        self.send()

    def settle(self, order):
        self.got = order.settle(self.got)

    def core_early(self, order):
        self.blocks = order.settle(self.blocks)
        self.early = [self.links.exchange(block, "c") for block in self.blocks]

    def core_late(self, order):
        self.got = order.settle(self.got)
        self.late = [self.links.exchange(got, "c") for got in self.got]

    def pieces(self):
        return [
            [values.reshape(-1, values.shape[-1]) for values in four]
            for four in zip(self.blocks, self.got, self.early, self.late)
        ]

    def halves(self):
        return list(zip(self.blocks, self.got))


def last_update(late, last, spans, scale, moments, vector_scale, vector_moments):
    spans, vectors_at = spans
    rows, width = moments[0].shape
    count = vector_moments[0].shape[0]

    def body(*refs):
        late_kept, late_got, last_kept, last_got, scale_ref = refs[:5]
        weight_ref, mean_ref, square_ref, vscale_ref, vector_ref, vmean_ref, vsquare_ref = refs[5:12]
        outs = refs[12:]
        sums = [added(late_kept[...], late_got[...], F32), added(last_kept[...], last_got[...], F32)]
        for of_last, first, place, size in spans:
            columns = slice(place, place + size)
            mean, square, stepped = adam_step(
                weight_ref[:, columns],
                sums[of_last][:, first : first + size],
                mean_ref[:, columns],
                square_ref[:, columns],
                matrix_rate,
                weight_decay,
            )
            outs[0][:, columns] = mean
            outs[1][:, columns] = square
            outs[2][:, columns] = stepped * scale_ref[:, columns]
        grads = sums[1][:, vectors_at : vectors_at + PAIR].T[:count]
        mean, square, stepped = adam_step(
            vector_ref[...], grads, vmean_ref[...], vsquare_ref[...], vector_rate, 0.0
        )
        outs[3][...] = mean
        outs[4][...] = square
        row = lax.broadcasted_iota(jnp.int32, stepped.shape, 0)
        outs[5][...] = jnp.where(row == 4, stepped * vscale_ref[...], stepped)

    return run(
        body,
        (*late, *last, scale, *moments, vector_scale, *vector_moments),
        [((rows, width), F32)] * 3 + [(vector_moments[0].shape, F32)] * 3,
    )


def local(
    links,
    tokens,
    cotangent,
    counts,
    w_qkv,
    w_out,
    w_up,
    w_down,
    vectors,
    mean_qkv,
    mean_out,
    mean_up,
    mean_down,
    mean_vectors,
    square_qkv,
    square_out,
    square_up,
    square_down,
    square_vectors,
):
    seq_count, slot_count, model_width = tokens.shape
    rows = seq_count * slot_count
    head_width = model_width // H
    wide = w_down.shape[0]
    vector_count, shard_width = vectors.shape
    half = model_width // 2
    order = Order()

    low_qkv = w_qkv.astype(BF16)
    thirds = [low_qkv[:, at * half : (at + 1) * half] for at in range(6)]
    shard_vectors = jnp.pad(vectors.astype(BF16).T, ((0, 0), (0, PAIR - vector_count)))
    shard_qkv = jnp.concatenate([*thirds[0::2], shard_vectors, *thirds[1::2]], 1)
    low_out, low_up = w_out.astype(BF16).T, w_up.astype(BF16)
    shard_up = jnp.concatenate(
        [low_out[:, :half], low_up[:, : wide // 2], low_out[:, half:], low_up[:, wide // 2 :]], 1
    )
    shard_down = w_down.astype(BF16).T
    gather_qkv = Gather(links, [shard_qkv], 3 * half + PAIR, True)
    gather_down = Gather(
        links, [shard_down[:, : wide // 2], shard_down[:, wide // 2 :]], wide // 2
    )

    true_rows = (
        links.true_block()[:, None] * shard_width + jnp.arange(shard_width, dtype=jnp.int32)
    ).reshape(1, model_width)
    to_relative = (
        lax.broadcasted_iota(jnp.int32, (model_width, model_width), 0) == true_rows
    ).astype(BF16)
    keep_rows = lax.broadcasted_iota(jnp.int32, (rows, 1), 0) < counts[0]
    d_result = jnp.where(keep_rows, cotangent.reshape(rows, model_width), 0).astype(BF16)
    inputs = mm(tokens.reshape(rows, model_width), to_relative).astype(BF16)
    d_result_turned = mm(d_result, to_relative).astype(BF16)
    d_columns = lax.dot_general(
        to_relative, d_result, (((0,), (1,)), ((), ())), preferred_element_type=F32
    ).astype(BF16)

    def longer(gather, count):
        while len(gather.steps) > count:
            gather.step(order)

    inputs, d_result_turned, d_columns, to_relative = order.settle(
        (inputs, d_result_turned, d_columns, to_relative)
    )
    longer(gather_qkv, 4)
    gather_down.settle(order)
    d_other = order.settle(links.exchange(d_columns[half:], "c"))
    d_mine = d_columns[:half]
    gather_qkv.step(order)
    gather_up = Gather(
        links, [order(lambda values: values + 0, shard_up)], half + wide // 2
    )
    gather_qkv.step(order)
    longer(gather_up, 5)
    gather_up.step(order)
    slowest = [1, 2 ** len(links.y_bits)]
    in_pieces = half // 2 // slowest[1] % PAIR == 0
    ranges_down = []
    for slow in slowest:
        group = half // slow
        cuts = ((0, group // 2), (group // 2, group)) if in_pieces else ((0, group),)
        ranges_down.append(
            [
                [(core + at * group + low, core + at * group + high) for at in range(slow)]
                for core in (0, half)
                for low, high in cuts
            ]
        )
    d_late = order.settle(d_result_turned)
    grads_down = [
        d_result_turned,
        order.settle(
            jnp.concatenate(
                [d_late[:, low:high] for places in ranges_down[1] for low, high in places], 1
            )
        ),
    ]
    gather_qkv.step(order)
    gather_up.step(order)
    longer(gather_down, 5)
    gather_down.step(order)
    halves_qkv = gather_qkv.halves()
    normed_low, normed_high, normed_mine, normed_send, vector_rows, true_vectors = order(
        first_norm, inputs, *halves_qkv[0], to_relative
    )
    normed_other = links.exchange(normed_send, "c")
    projected = [
        order(partial(project, at), normed_low, normed_high, *halves_qkv[at], true_vectors)
        for at in (0, 1)
    ]
    normed_other = order.settle(normed_other)
    gather_up.step(order)
    shared, peak = order(attend, projected, counts)
    gather_down.step(order)
    shared_other = links.exchange(shared, "c")
    peak, peak_got = [peak], []

    def peak_send(bit):
        sent = order.settle(peak[0])
        peak_got.append(links.exchange(sent, bit))

    def peak_take():
        peak[0] = order(jnp.maximum, peak[0], peak_got.pop())

    first_bit, *more_bits = links.bits
    peak_send(first_bit)
    peak_take()
    for bit in more_bits[4:]:
        peak_send(bit)
        peak_take()
    peak_send(more_bits[0])
    gather_up.step(order)
    shared_other = order.settle(shared_other)
    peak_take()
    peak_send(more_bits[1])
    peak_take()
    peak_send(more_bits[2])
    gather_down.step(order)
    peak_take()
    peak_send(more_bits[3])
    halves_up = gather_up.halves()
    middle, normed_two_low, normed_two_high, normed_two_mine, normed_two_send = order(
        second_norm, inputs, shared, halves_up, vector_rows
    )
    peak_take()
    normed_two_other = links.exchange(normed_two_send, "c")
    if in_pieces:
        gather_down.core_early(order)
    hidden, slope, hidden_other = [], [], []
    for at in (0, 1):
        out, out_slope = order(
            partial(expand, at), normed_two_low, normed_two_high, *halves_up[at], true_vectors
        )
        hidden.append(out)
        slope.append(out_slope)
        hidden_other.append(links.exchange(out, "c"))
        if at == 0:
            normed_two_other = order.settle(normed_two_other)
            if in_pieces:
                gather_down.early = order.settle(gather_down.early)

    down_parts = [
        order(
            partial(product_wide, slowest[at], 0, wide // 2),
            d_mine,
            d_other,
            hidden[at],
            hidden_other[at],
        )
        for at in (0, 1)
    ]
    if in_pieces:
        gather_down.core_late(order)
    else:
        gather_down.step(order)
    sum_down = Sum(links, order.settle(down_parts))
    weights_down = gather_down.pieces() if in_pieces else gather_down.halves()
    d_pre, d_pre_sums = order(expand_back, grads_down, weights_down, slope)
    d_pre_other = links.exchange(d_pre, "c")
    partial_sum = order(contract_first, d_pre, *halves_up[0])
    result = order(
        partial(finish_first, ranges=ranges_down[0]), middle, hidden[0], weights_down[0], vector_rows
    )
    for _ in links.orders[0][1:]:
        sum_down.step(order)
    sum_up = Sum(
        links,
        [
            order(
                partial(product_wide, slowest[at], at * wide // 2, wide // 2),
                normed_two_mine,
                normed_two_other,
                d_pre,
                d_pre_other,
            )
            for at in (0, 1)
        ],
    )
    d_middle, d_branch_low, d_branch_high, d_out_one, d_out_two, grads = order(
        contract_second, d_pre, halves_up, partial_sum, middle, d_result_turned, vector_rows
    )
    d_branch_other = links.exchange(d_branch_high, "c")
    sum_down.step(order)
    d_branch_other = order.settle(d_branch_other)
    d_projected, d_projected_other, head_sums = [], [], []
    for at, d_out in enumerate((d_out_one, d_out_two)):
        out, sums = order(attend_back, projected[at], d_out, counts)
        d_projected.append(out)
        d_projected_other.append(links.exchange(out, "c"))
        head_sums.append(sums)


    def out_tile(at):
        return (d_branch_low, d_branch_other, shared, shared_other, half, (0, at))

    def qkv_tile(at, part, width, column):
        return (
            normed_mine,
            normed_other,
            d_projected[at],
            d_projected_other[at],
            width,
            (part, 0, column),
        )

    def late_product(at, tiles, extra=()):
        def call(operands, extra):
            return product(
                slowest[at],
                [(*operands[4 * i : 4 * i + 4], *tile[4:]) for i, tile in enumerate(tiles)],
                extra,
            )

        return order(call, [operand for tile in tiles for operand in tile[:4]], extra)

    partial_sum = order(input_back_first, d_projected[0], *halves_qkv[0])
    for _ in links.z_bits[1:]:
        sum_down.step(order)
    for _ in links.orders[0][1:]:
        sum_up.step(order)
    d_projected_other = order.settle(d_projected_other)
    quarter = half // 2
    sum_late = Sum(
        links,
        [
            late_product(at, [out_tile(at), qkv_tile(0, at, half, 0), qkv_tile(0, 2, quarter, at)])
            for at in (0, 1)
        ],
    )
    token_grad, vectors_low, vectors_high = order(
        input_back_second,
        d_projected[1],
        *halves_qkv[1],
        partial_sum,
        inputs,
        d_middle,
        grads,
        head_sums,
        d_pre_sums,
        vector_rows,
        to_relative,
    )
    token_grad = token_grad.reshape(seq_count, slot_count, model_width)
    sum_down.settle(order)
    vectors_other = links.exchange(vectors_high, "c")
    sum_up.step(order)
    last = [
        late_product(
            at,
            [qkv_tile(1, at, half, 0), qkv_tile(1, 2, quarter, at)],
            ((), (vectors_low, vectors_other))[at],
        )
        for at in (0, 1)
    ]
    sum_last = Sum(links, last)
    result = order(
        partial(finish_second, ranges=ranges_down[1]),
        result,
        hidden[1],
        weights_down[1],
        to_relative,
        counts,
    )
    result_out = result.reshape(seq_count, slot_count, model_width)
    for _ in links.orders[0][1:]:
        sum_late.step(order)
    for _ in links.z_bits[1:]:
        sum_up.step(order)
    for _ in links.orders[0][1:]:
        sum_last.step(order)
    sum_late.step(order)
    sum_last.step(order)
    mean_down, mean_up = order.settle((mean_down, mean_up))
    sum_up.settle(order)
    for _ in links.z_bits[1:]:
        sum_late.step(order)
    head_peak = order.settle(peak[0])[:, 0]
    vectors, mean_vectors, square_vectors, first_col = order.settle(
        (
            vectors,
            mean_vectors,
            square_vectors,
            lax.axis_index(("dp", "fsdp")) * shard_width,
        )
    )
    shrink = jnp.sqrt(clip_limit / jnp.maximum(head_peak, clip_limit))
    head_cols = jnp.repeat(shrink, head_width)
    qkv_scale = jnp.concatenate([head_cols, head_cols, jnp.ones((model_width,), F32)])[None]
    col_head = (first_col + jnp.arange(shard_width, dtype=jnp.int32)) // head_width
    col_shrink = jnp.sum(
        jnp.where(
            col_head[:, None] == jnp.arange(H, dtype=jnp.int32)[None, :], shrink[None, :], 0.0
        ),
        1,
    )[None]
    for _ in links.z_bits[1:]:
        sum_last.step(order)
    sum_late.settle(order)
    spans = (
        (0, half, 0, half),
        (1, 0, half, half),
        (0, half * 3 + quarter, 2 * half, half),
        (1, half + quarter, 3 * half, half),
        (0, 2 * half, 4 * half, quarter),
        (0, 4 * half + quarter, 4 * half + quarter, quarter),
        (1, half, 5 * half, quarter),
        (1, 2 * half + quarter, 5 * half + quarter, quarter),
    )
    vectors_at = 3 * half
    late = sum_late.total()
    reduced_out = jnp.concatenate([late[:, :half], late[:, 2 * half + quarter :][:, :half]], 1).T
    reduced_up = sum_up.total()
    reduced_down = sum_down.total().T
    mean_o, square_o, new_out = adam_step(
        w_out, reduced_out, mean_out, square_out, matrix_rate, weight_decay
    )
    mean_u, square_u, new_up = adam_step(
        w_up, reduced_up, mean_up, square_up, matrix_rate, weight_decay
    )
    mean_d, square_d, new_down = adam_step(
        w_down, reduced_down, mean_down, square_down, matrix_rate, weight_decay
    )
    if shard_width % 8 == 0:
        mean_q, square_q, new_qkv, mean_v, square_v, new_vectors = last_update(
            sum_late.pairs[0],
            sum_last.pairs[0],
            (spans, vectors_at),
            qkv_scale,
            (w_qkv, mean_qkv, square_qkv),
            col_shrink,
            (vectors, mean_vectors, square_vectors),
        )
    else:
        sums = (late, sum_last.total())
        reduced_qkv = jnp.concatenate(
            [sums[which][:, first : first + size] for which, first, _, size in spans], 1
        )
        mean_q, square_q, stepped_qkv = adam_step(
            w_qkv, reduced_qkv, mean_qkv, square_qkv, matrix_rate, weight_decay
        )
        new_qkv = stepped_qkv * qkv_scale
        reduced_vectors = sums[1][:, vectors_at : vectors_at + vector_count].T
        mean_v, square_v, stepped_vectors = adam_step(
            vectors, reduced_vectors, mean_vectors, square_vectors, vector_rate, 0.0
        )
        row_pick = (jnp.arange(vector_count, dtype=jnp.int32) == 4)[:, None]
        new_vectors = jnp.where(row_pick, stepped_vectors * col_shrink, stepped_vectors)
    return (
        result_out,
        token_grad,
        head_peak,
        mean_q,
        square_q,
        new_qkv,
        mean_o,
        square_o,
        new_out,
        mean_u,
        square_u,
        new_up,
        mean_d,
        square_d,
        new_down,
        mean_v,
        square_v,
        new_vectors,
    )


def solution(mesh):
    links = Links(mesh.shape["dp"], mesh.shape["fsdp"])
    return jax.shard_map(
        partial(local, links),
        mesh=mesh,
        in_specs=(
            P(("dp", "fsdp"), None, None),
            P(("dp", "fsdp"), None, None),
            P(("dp", "fsdp")),
            P(("dp", "fsdp"), None),
            P(None, ("dp", "fsdp")),
            P(("dp", "fsdp"), None),
            P(None, ("dp", "fsdp")),
            P(None, ("dp", "fsdp")),
            P(("dp", "fsdp"), None),
            P(None, ("dp", "fsdp")),
            P(("dp", "fsdp"), None),
            P(None, ("dp", "fsdp")),
            P(None, ("dp", "fsdp")),
            P(("dp", "fsdp"), None),
            P(None, ("dp", "fsdp")),
            P(("dp", "fsdp"), None),
            P(None, ("dp", "fsdp")),
            P(None, ("dp", "fsdp")),
        ),
        out_specs=(
            P(("dp", "fsdp"), None, None),
            P(("dp", "fsdp"), None, None),
            P(),
            P(("dp", "fsdp"), None),
            P(("dp", "fsdp"), None),
            P(("dp", "fsdp"), None),
            P(None, ("dp", "fsdp")),
            P(None, ("dp", "fsdp")),
            P(None, ("dp", "fsdp")),
            P(("dp", "fsdp"), None),
            P(("dp", "fsdp"), None),
            P(("dp", "fsdp"), None),
            P(None, ("dp", "fsdp")),
            P(None, ("dp", "fsdp")),
            P(None, ("dp", "fsdp")),
            P(None, ("dp", "fsdp")),
            P(None, ("dp", "fsdp")),
            P(None, ("dp", "fsdp")),
        ),
        check_vma=False,
    )
```

```python
from functools import partial

import jax
import jax.numpy as jnp
import numpy as np
from jax import lax
from jax.experimental import pallas as pl
from jax.experimental.pallas import tpu as pltpu
from jax.sharding import PartitionSpec as P

H = 16
STEP = 10


beta_one = 0.9
beta_two = 0.95
adam_epsilon = 1e-08
weight_decay = 0.1
matrix_rate = 0.1
vector_rate = 0.5
clip_limit = 8.0
norm_epsilon = 1e-06
masked_value = -1e30
TILE = 512
PAIR = 128
HALF_ROOT = 0.5**0.5
DENSITY = 0.3989422804014327
F32 = jnp.float32
BF16 = jnp.bfloat16


def adam_step(weight, gradient, mean_old, square_old, step_rate, decay_rate):
    mean_new = beta_one * mean_old + (1.0 - beta_one) * gradient
    square_new = beta_two * square_old + (1.0 - beta_two) * gradient * gradient
    fix_one = 1.0 - beta_one**STEP
    fix_two = 1.0 - beta_two**STEP
    stepped = weight - step_rate * (
        mean_new / fix_one / (jnp.sqrt(square_new / fix_two) + adam_epsilon) + decay_rate * weight
    )
    return (mean_new, square_new, stepped)


def bit_names(letter, count):
    return tuple(letter + str(at) for at in range(count))


class Links:
    def __init__(self, dp_count, inner_count):
        self.device_count = dp_count * inner_count
        inner_bits = inner_count.bit_length() - 1
        z_bits = bit_names("z", dp_count.bit_length() - 2)
        x_bits = bit_names("x", inner_bits // 2)
        y_bits = bit_names("y", inner_bits - inner_bits // 2)
        self.place = {"c": ("dp", dp_count, 0)}
        self.place.update({bit: ("dp", dp_count, at + 1) for at, bit in enumerate(z_bits)})
        self.place.update({bit: ("fsdp", inner_count, at) for at, bit in enumerate(x_bits)})
        self.place.update(
            {bit: ("fsdp", inner_count, at + len(x_bits)) for at, bit in enumerate(y_bits)}
        )
        self.bits = ("c",) + y_bits + x_bits + z_bits
        self.orders = (y_bits + x_bits, x_bits + y_bits)
        self.z_bits = z_bits
        self.y_bits = y_bits
        self.inner_bits = inner_bits

    def true_block(self):
        masks = []
        for block in range(self.device_count):
            mask = 0
            for at, bit in enumerate(reversed(self.bits)):
                if block >> at & 1:
                    axis, _, place = self.place[bit]
                    mask |= 1 << (place + (self.inner_bits if axis == "dp" else 0))
            masks.append(mask)
        return lax.axis_index(("dp", "fsdp")) ^ jnp.array(masks, jnp.int32)

    def exchange(self, values, *bits):
        axis, count, _ = self.place[bits[0]]
        mask = sum(1 << self.place[bit][2] for bit in bits)
        return lax.ppermute(values, axis, [(at, at ^ mask) for at in range(count)])


class Order:
    def __init__(self):
        self.ended = ()

    def __call__(self, call, *operands):
        operands, _ = lax.optimization_barrier((operands, self.ended))
        result = call(*operands)
        self.ended = result
        return result

    def settle(self, value):
        return self(lambda come: come, value)


def run(body, operands, outs, grid=(), in_specs=None, out_specs=None, scratch=()):
    whole = pl.BlockSpec(memory_space=pltpu.VMEM)
    return pl.pallas_call(
        body,
        out_shape=[
            pltpu.HBM(shape, kind) if hbm else jax.ShapeDtypeStruct(shape, kind)
            for shape, kind, *hbm in outs
        ],
        grid=grid,
        in_specs=in_specs or [whole] * len(operands),
        out_specs=out_specs or [whole] * len(outs),
        scratch_shapes=scratch,
        compiler_params=pltpu.CompilerParams(vmem_limit_bytes=12 * 2**20),
        cost_estimate=pl.CostEstimate(flops=24 * 10**9, bytes_accessed=1000, transcendentals=0),
    )(*operands)


def fixed(shape):
    return pl.BlockSpec(shape, lambda j: (0,) * len(shape))


def mm(first, second):
    return lax.dot_general(first, second, (((1,), (0,)), ((), ())), preferred_element_type=F32)


def mm_turned(first, second):
    return lax.dot_general(first, second, (((1,), (1,)), ((), ())), preferred_element_type=F32)


def mm_rows(first, second):
    return lax.dot_general(first, second, (((0,), (0,)), ((), ())), preferred_element_type=F32)


def pieces(values, count=3):
    out = []
    for _ in range(count):
        piece = values.astype(BF16)
        out.append(piece)
        values = values - piece.astype(F32)
    return out


def normalized(values):
    centered = values - jnp.mean(values, -1, keepdims=True)
    scale = lax.rsqrt(jnp.mean(centered * centered, -1, keepdims=True) + norm_epsilon)
    return centered * scale, scale


def norm_back(grad, values, gain):
    unit, scale = normalized(values)
    inner = grad * gain
    d_values = scale * (
        inner
        - jnp.mean(inner, -1, keepdims=True)
        - unit * jnp.mean(inner * unit, -1, keepdims=True)
    )
    return (
        d_values,
        jnp.sum(grad * unit, 0, keepdims=True),
        jnp.sum(grad, 0, keepdims=True),
    )


def first_norm(inputs, mine, other, to_relative):
    rows, width = inputs.shape
    half = width // 2

    def body(
        x_ref, mine_ref, other_ref, turn_ref, low_ref, high_ref, lowt_ref, hight_ref, rel_ref, true_ref
    ):
        turned = jnp.concatenate(
            [mine_ref[...].astype(F32).T, other_ref[...].astype(F32).T], 1
        )[:16]
        rel_ref[...] = turned
        true_ref[...] = mm_turned(turned.astype(BF16), turn_ref[...])
        unit, _ = normalized(x_ref[...].astype(F32))
        normed = (unit * turned[0:1] + turned[1:2]).astype(BF16)
        low_ref[...] = normed[:, :half]
        high_ref[...] = normed[:, half:]
        lowt_ref[...] = normed[:, :half].T
        hight_ref[...] = normed[:, half:].T

    vectors_at = mine.shape[1] // PAIR - 1
    weights = pl.BlockSpec((half, PAIR), lambda j: (0, vectors_at))
    return run(
        body,
        (inputs, mine, other, to_relative),
        [((rows, half), BF16)] * 2 + [((half, rows), BF16)] * 2 + [((16, width), F32)] * 2,
        (1,),
        [fixed(inputs.shape), weights, weights, fixed(to_relative.shape)],
        [fixed((rows, half))] * 2 + [fixed((half, rows))] * 2 + [fixed((16, width))] * 2,
    )


def project(at, low, high, mine, other, true_vectors):
    rows, half = low.shape

    def body(low_ref, high_ref, mine_ref, other_ref, vec_ref, out_ref):
        j = pl.program_id(0)
        bias = jnp.where(j == 0, vec_ref[4:5, :], jnp.where(j == 2, vec_ref[5:6, :], 0.0))
        value = mm(low_ref[...], mine_ref[...]) + mm(high_ref[...], other_ref[...])
        out_ref[0] = (value + bias).astype(BF16)

    weights = pl.BlockSpec((half, TILE), lambda j: (0, j))
    return run(
        body,
        (low, high, mine, other, true_vectors),
        [((3, rows, TILE), BF16)],
        (3,),
        [fixed(low.shape)] * 2 + [weights] * 2 + [pl.BlockSpec((16, TILE), lambda j: (0, at))],
        [pl.BlockSpec((1, rows, TILE), lambda j: (j, 0, 0))],
    )[0]


def head_mask(rows, side):
    lane = lax.broadcasted_iota(jnp.int32, (rows, PAIR), 1)
    return lane < PAIR // 2 if side == 0 else lane >= PAIR // 2


def attend(projected, counts):
    _, rows, width = projected[0].shape
    steps = width // PAIR

    def body(count_ref, *refs):
        *ins, out_ref, peak_ref = refs
        j = pl.program_id(0)

        def heads(q_ref, k_ref, v_ref):
            count = count_ref[0]
            key_ok = lax.broadcasted_iota(jnp.int32, (rows, rows), 1) < count
            row_ok = lax.broadcasted_iota(jnp.int32, (rows, 1), 0) < count
            queries = q_ref[0]
            out = None
            for side in (0, 1):
                chosen = head_mask(rows, side)
                scores = mm_turned(jnp.where(chosen, queries, 0), k_ref[0]) * (PAIR // 2) ** -0.5
                scores = jnp.where(key_ok, scores, masked_value)
                top = jnp.max(scores, -1, keepdims=True)
                peak = jnp.max(jnp.where(row_ok, top, masked_value))
                peak_ref[pl.ds(j * 2 + side, 1), :] = jnp.full((1, PAIR), peak)
                exponent = jnp.exp(scores - top)
                probs = exponent * (1.0 / jnp.sum(exponent, -1, keepdims=True))
                value = mm(probs.astype(BF16), v_ref[0])
                out = value if side == 0 else jnp.where(chosen, value, out)
            out_ref[...] = out.astype(BF16)

        @pl.when(j < steps)
        def _():
            heads(*ins[:3])

        @pl.when(j >= steps)
        def _():
            heads(*ins[3:])

    def part(index, at):
        return pl.BlockSpec(
            (1, rows, PAIR), lambda j: (index, 0, jnp.clip(j - at * steps, 0, steps - 1))
        )

    return run(
        body,
        (counts, *[projected[0]] * 3, *[projected[1]] * 3),
        [((rows, 2 * width), BF16), ((4 * steps, PAIR), F32)],
        (2 * steps,),
        [pl.BlockSpec(memory_space=pltpu.SMEM)]
        + [part(index, at) for at in (0, 1) for index in range(3)],
        [pl.BlockSpec((rows, PAIR), lambda j: (0, j)), fixed((4 * steps, PAIR))],
    )


def attend_back(projected, d_out, counts):
    _, rows, width = projected.shape
    steps = width // PAIR
    scale = (PAIR // 2) ** -0.5

    def body(count_ref, q_ref, k_ref, v_ref, d_ref, out_ref, sum_ref):
        key_ok = lax.broadcasted_iota(jnp.int32, (rows, rows), 0) < count_ref[0]
        queries, keys, values, grad = q_ref[0], k_ref[0], v_ref[0], d_ref[...]
        parts = [None] * 3
        for side in (0, 1):
            chosen = head_mask(rows, side)
            scores = mm_turned(jnp.where(chosen, keys, 0), queries) * scale
            scores = jnp.where(key_ok, scores, masked_value)
            exponent = jnp.exp(scores - jnp.max(scores, 0, keepdims=True))
            probs = exponent * (1.0 / jnp.sum(exponent, 0, keepdims=True))
            d_probs = mm_turned(jnp.where(chosen, values, 0), grad)
            inner = jnp.sum(probs * d_probs, 0, keepdims=True)
            d_scores = (probs * (d_probs - inner)).astype(BF16)
            new = [
                mm_rows(d_scores, keys) * scale,
                mm(d_scores, queries) * scale,
                mm(probs.astype(BF16), grad),
            ]
            parts = new if side == 0 else [jnp.where(chosen, n, p) for n, p in zip(new, parts)]
        low = [part.astype(BF16) for part in parts]
        for at in range(3):
            out_ref[at] = low[at]
        sum_ref[0:1, :] = jnp.sum(low[0].astype(F32), 0, keepdims=True)
        sum_ref[1:2, :] = jnp.sum(low[2].astype(F32), 0, keepdims=True)

    def part(index):
        return pl.BlockSpec((1, rows, PAIR), lambda j: (index, 0, j))

    columns = pl.BlockSpec((rows, PAIR), lambda j: (0, j))
    return run(
        body,
        (counts, projected, projected, projected, d_out),
        [((3, rows, width), BF16), ((8, width), F32)],
        (steps,),
        [pl.BlockSpec(memory_space=pltpu.SMEM), part(0), part(1), part(2), columns],
        [
            pl.BlockSpec((3, rows, PAIR), lambda j: (0, 0, j)),
            pl.BlockSpec((8, PAIR), lambda j: (0, j)),
        ],
    )


def second_norm(inputs, attended, weights, vectors):
    rows, width = inputs.shape
    half = width // 2

    def body(x_ref, a_ref, b_ref, wa_ref, wa2_ref, wb_ref, wb2_ref, vec_ref, mid_ref, low_ref, high_ref, lowt_ref, hight_ref):
        first, second = a_ref[...], b_ref[...]
        branch = jnp.concatenate(
            [
                mm_turned(first, wa_ref[...]) + mm_turned(second, wb_ref[...]),
                mm_turned(first, wa2_ref[...]) + mm_turned(second, wb2_ref[...]),
            ],
            1,
        )
        middle = x_ref[...].astype(F32) + branch + vec_ref[6:7, :]
        mid_ref[...] = middle
        unit, _ = normalized(middle)
        normed = (unit * vec_ref[2:3, :] + vec_ref[3:4, :]).astype(BF16)
        low_ref[...] = normed[:, :half]
        high_ref[...] = normed[:, half:]
        lowt_ref[...] = normed[:, :half].T
        hight_ref[...] = normed[:, half:].T

    block = pl.BlockSpec((half, TILE), lambda j: (0, 0))
    return run(
        body,
        (inputs, attended, attended, *weights[0], *weights[1], vectors),
        [((rows, width), F32)] + [((rows, half), BF16)] * 2 + [((half, rows), BF16)] * 2,
        (1,),
        [fixed(inputs.shape)]
        + [pl.BlockSpec((rows, TILE), lambda j, at=at: (0, at)) for at in (0, 1)]
        + [block] * 4
        + [fixed(vectors.shape)],
        [fixed((rows, width))] + [fixed((rows, half))] * 2 + [fixed((half, rows))] * 2,
    )


def expand(at, low, high, mine, other, true_vectors):
    rows, half = low.shape
    count = mine.shape[1] - TILE
    per_row = true_vectors.shape[1] // TILE
    first_row = 8 + at * count // true_vectors.shape[1]

    def body(low_ref, high_ref, mine_ref, other_ref, vec_ref, out_ref, slope_ref):
        row = first_row + pl.program_id(0) // per_row
        pre = mm(low_ref[...], mine_ref[...]) + mm(high_ref[...], other_ref[...])
        pre = pre + vec_ref[pl.ds(row, 1), :]
        below = 0.5 * (1.0 + lax.erf(pre * HALF_ROOT))
        out_ref[...] = (pre * below).astype(BF16)
        slope = below + pre * (DENSITY * jnp.exp(-0.5 * pre * pre))
        slope_ref[...] = slope.astype(BF16)

    weights = pl.BlockSpec((half, TILE), lambda j: (0, j + 1))
    columns = pl.BlockSpec((rows, TILE), lambda j: (0, j))
    return run(
        body,
        (low, high, mine, other, true_vectors),
        [((rows, count), BF16), ((rows, count), BF16, "hbm")],
        (count // TILE,),
        [fixed(low.shape)] * 2
        + [weights] * 2
        + [pl.BlockSpec((16, TILE), lambda j: (0, j % per_row))],
        [columns, columns],
    )


def among(count, at, shape):
    return pl.BlockSpec(shape, lambda j: (0, jnp.clip(j - at * count, 0, count - 1)))


def expand_back(grads, weights, slopes):
    rows = slopes[0].shape[0]
    steps = slopes[0].shape[1] // TILE
    counts = [len(pieces) for pieces in weights]
    operands, specs = [], []
    for at, (left, rights) in enumerate(zip(grads, weights)):
        operands += [left] * len(rights) + [*rights]
        specs += [
            pl.BlockSpec((rows, right.shape[0]), lambda j, piece=piece: (0, piece))
            for piece, right in enumerate(rights)
        ]
        specs += [among(steps, at, (right.shape[0], TILE)) for right in rights]

    def body(*refs):
        *ins, first_slope, second_slope, out_ref, sum_ref = refs
        j = pl.program_id(0)
        for at, slope_ref in enumerate((first_slope, second_slope)):
            first = 2 * sum(counts[:at])
            lefts, rights = ins[first : first + counts[at]], ins[first + counts[at] :][: counts[at]]

            @pl.when(j // steps == at)
            def _(lefts=lefts, rights=rights, slope_ref=slope_ref):
                value = sum(mm(left[...], right[...]) for left, right in zip(lefts, rights))
                value = (value * slope_ref[...].astype(F32)).astype(BF16)
                out_ref[...] = value
                sum_ref[...] = jnp.sum(value.astype(F32), 0, keepdims=True)

    count = 2 * steps
    return run(
        body,
        (*operands, *slopes),
        [((rows, count * TILE), BF16), ((1, count * TILE), F32)],
        (count,),
        specs + [among(steps, at, (rows, TILE)) for at in range(2)],
        [pl.BlockSpec((rows, TILE), lambda j: (0, j)), pl.BlockSpec((1, TILE), lambda j: (0, j))],
    )


def contract_first(d_pre, mine, other):
    rows, count = d_pre.shape
    half = mine.shape[0]
    count = count // 2

    def body(d_ref, mine_ref, other_ref, out_ref):
        @pl.when(pl.program_id(0) == 0)
        def _():
            out_ref[...] = jnp.zeros_like(out_ref)

        out_ref[:, :half] += mm_turned(d_ref[...], mine_ref[...])
        out_ref[:, half:] += mm_turned(d_ref[...], other_ref[...])

    weights = pl.BlockSpec((half, TILE), lambda j: (0, j + 1))
    return run(
        body,
        (d_pre, mine, other),
        [((rows, 2 * half), F32)],
        (count // TILE,),
        [pl.BlockSpec((rows, TILE), lambda j: (0, j)), weights, weights],
        [fixed((rows, 2 * half))],
    )[0]


def contract_second(d_pre, weights, partial_sum, middle, d_result, vectors):
    rows, count = d_pre.shape
    half = weights[0][0].shape[0]
    width = 2 * half
    steps = count // 2 // TILE

    def body(
        d_ref, mine_ref, other_ref, wa_ref, wa2_ref, wb_ref, wb2_ref, sum_ref, mid_ref, res_ref,
        vec_ref, dm_ref, low_ref, high_ref, outa_ref, outb_ref, grads_ref, total,
    ):
        j = pl.program_id(0)

        @pl.when(j == 0)
        def _():
            total[...] = sum_ref[...]

        total[:, :half] += mm_turned(d_ref[...], mine_ref[...])
        total[:, half:] += mm_turned(d_ref[...], other_ref[...])

        @pl.when(j == steps - 1)
        def _():
            d_values, d_gain, d_shift = norm_back(total[...], mid_ref[...], vec_ref[2:3, :])
            result_grad = res_ref[...].astype(F32)
            d_middle = result_grad + d_values
            branch = d_middle.astype(BF16)
            dm_ref[...] = d_middle
            first, second = branch[:, :half], branch[:, half:]
            low_ref[...] = first.T
            high_ref[...] = second.T
            outa_ref[...] = (mm(first, wa_ref[...]) + mm(second, wa2_ref[...])).astype(BF16)
            outb_ref[...] = (mm(first, wb_ref[...]) + mm(second, wb2_ref[...])).astype(BF16)
            grads_ref[0:1, :] = d_gain
            grads_ref[1:2, :] = d_shift
            grads_ref[2:3, :] = jnp.sum(branch.astype(F32), 0, keepdims=True)
            grads_ref[3:4, :] = jnp.sum(result_grad, 0, keepdims=True)

    tile = pl.BlockSpec((half, TILE), lambda j: (0, j + 1))
    block = pl.BlockSpec((half, TILE), lambda j: (0, 0))
    return run(
        body,
        (d_pre, *weights[1], *weights[0], *weights[1], partial_sum, middle, d_result, vectors),
        [((rows, width), F32)]
        + [((half, rows), BF16)] * 2
        + [((rows, TILE), BF16)] * 2
        + [((8, width), F32)],
        (steps,),
        [pl.BlockSpec((rows, TILE), lambda j: (0, steps + j)), tile, tile]
        + [block] * 4
        + [fixed((rows, width))] * 3
        + [fixed(vectors.shape)],
        [fixed((rows, width))]
        + [fixed((half, rows))] * 2
        + [fixed((rows, TILE))] * 2
        + [fixed((8, width))],
        [pltpu.VMEM((rows, width), F32)],
    )


def input_back_first(d_projected, mine, other):
    rows = d_projected.shape[1]
    half = mine.shape[0]

    def body(d_ref, mine_ref, other_ref, out_ref):
        @pl.when(pl.program_id(0) == 0)
        def _():
            out_ref[...] = jnp.zeros_like(out_ref)

        out_ref[:, :half] += mm_turned(d_ref[0], mine_ref[...])
        out_ref[:, half:] += mm_turned(d_ref[0], other_ref[...])

    weights = pl.BlockSpec((half, TILE), lambda j: (0, j))
    return run(
        body,
        (d_projected, mine, other),
        [((rows, 2 * half), F32)],
        (3,),
        [pl.BlockSpec((1, rows, TILE), lambda j: (j, 0, 0)), weights, weights],
        [fixed((rows, 2 * half))],
    )[0]


def input_back_second(
    d_projected, mine, other, partial_sum, inputs, d_middle, grads, head_sums, d_pre_sums, vectors, to_relative
):
    rows = d_projected.shape[1]
    half = mine.shape[0]
    width = 2 * half

    def body(
        d_ref, mine_ref, other_ref, sum_ref, x_ref, dm_ref, grads_ref, heada_ref, headb_ref, pre_ref,
        vec_ref, turn_ref, out_ref, low_ref, high_ref, total, true_rows, all_rows,
    ):
        j = pl.program_id(0)

        @pl.when(j == 0)
        def _():
            total[...] = sum_ref[...]

        total[:, :half] += mm_turned(d_ref[0], mine_ref[...])
        total[:, half:] += mm_turned(d_ref[0], other_ref[...])

        @pl.when(j == 2)
        def _():
            d_values, d_gain, d_shift = norm_back(total[...], x_ref[...].astype(F32), vec_ref[0:1, :])
            low = (dm_ref[...] + d_values).astype(BF16)
            out_ref[...] = mm_turned(low, turn_ref[...]).astype(BF16)
            true_rows[...] = jnp.zeros_like(true_rows)
            for at, ref in enumerate((heada_ref, headb_ref)):
                true_rows[0:2, at * TILE : (at + 1) * TILE] = ref[0:2, :]
            for part in range(pre_ref.shape[1] // width):
                row = 2 + part
                true_rows[row : row + 1, :] = pre_ref[:, part * width : (part + 1) * width]
            turned = sum(mm(part, turn_ref[...]) for part in pieces(true_rows[...]))
            all_rows[...] = jnp.zeros_like(all_rows)
            all_rows[0:1, :] = d_gain
            all_rows[1:2, :] = d_shift
            all_rows[2:4, :] = grads_ref[0:2, :]
            all_rows[4:6, :] = turned[0:2]
            all_rows[6:8, :] = grads_ref[2:4, :]
            all_rows[8:14, :] = turned[2:8]
            columns = all_rows[...].T
            low_ref[...] = columns[:half]
            high_ref[...] = columns[half:]

    weights = pl.BlockSpec((half, TILE), lambda j: (0, j))
    operands = (
        d_projected,
        mine,
        other,
        partial_sum,
        inputs,
        d_middle,
        grads,
        *head_sums,
        d_pre_sums,
        vectors,
        to_relative,
    )
    return run(
        body,
        operands,
        [((rows, width), BF16)] + [((half, PAIR), F32)] * 2,
        (3,),
        [pl.BlockSpec((1, rows, TILE), lambda j: (j, 0, 0)), weights, weights]
        + [fixed(operand.shape) for operand in operands[3:]],
        [fixed((rows, width))] + [fixed((half, PAIR))] * 2,
        [pltpu.VMEM((rows, width), F32), pltpu.VMEM((8, width), F32), pltpu.VMEM((PAIR, width), F32)],
    )


def contract_hidden(hidden, weights, ranges, total):
    for ref, places in zip(weights, ranges):
        value = mm_turned(hidden[...], ref[...])
        first = 0
        for low, high in places:
            total[:, low:high] += value[:, first : first + high - low]
            first += high - low


def finish_first(middle, hidden, weights, vectors, ranges):
    rows, width = middle.shape
    steps = hidden.shape[1] // TILE

    def body(hidden_ref, *refs):
        *weight_refs, mid_ref, vec_ref, out_ref = refs

        @pl.when(pl.program_id(0) == 0)
        def _():
            out_ref[...] = mid_ref[...] + vec_ref[7:8, :]

        contract_hidden(hidden_ref, weight_refs, ranges, out_ref)

    columns = pl.BlockSpec((rows, TILE), lambda j: (0, j))
    return run(
        body,
        (hidden, *weights, middle, vectors),
        [((rows, width), F32)],
        (steps,),
        [columns]
        + [pl.BlockSpec((right.shape[0], TILE), lambda j: (0, j)) for right in weights]
        + [fixed((rows, width)), fixed(vectors.shape)],
        [fixed((rows, width))],
    )[0]


def finish_second(partial_sum, hidden, weights, to_relative, counts, ranges):
    rows, width = partial_sum.shape
    steps = hidden.shape[1] // TILE

    def body(count_ref, hidden_ref, *refs):
        *weight_refs, sum_ref, turn_ref, out_ref, total = refs

        @pl.when(pl.program_id(0) == 0)
        def _():
            total[...] = sum_ref[...]

        contract_hidden(hidden_ref, weight_refs, ranges, total)

        @pl.when(pl.program_id(0) == steps - 1)
        def _():
            kept = lax.broadcasted_iota(jnp.int32, (rows, 1), 0) < count_ref[0]
            low = jnp.where(kept, total[...], 0.0).astype(BF16)
            out_ref[...] = mm_turned(low, turn_ref[...]).astype(BF16)

    columns = pl.BlockSpec((rows, TILE), lambda j: (0, j))
    return run(
        body,
        (counts, hidden, *weights, partial_sum, to_relative),
        [((rows, width), BF16)],
        (steps,),
        [pl.BlockSpec(memory_space=pltpu.SMEM), columns]
        + [pl.BlockSpec((right.shape[0], TILE), lambda j: (0, j)) for right in weights]
        + [fixed((rows, width)), fixed(to_relative.shape)],
        [fixed((rows, width))],
        [pltpu.VMEM((rows, width), F32)],
    )[0]


def product(slowest, tiles, extra=()):
    count, rows = tiles[0][0].shape
    operands, specs = [], []
    for *both, width, place in tiles:
        operands += both
        specs += [fixed((count, rows))] * 2
        shape = (1,) * (len(place) - 2) + (rows, width)
        specs += [pl.BlockSpec(shape, lambda j, place=place: place)] * 2
    width = sum(tile[4] for tile in tiles)
    full = width + (extra[0].shape[1] if extra else 0)
    operands += extra
    specs += [fixed(operand.shape) for operand in extra]

    def body(*refs):
        *ins, sent_ref, kept_ref = refs
        first = 0
        for at, tile in enumerate(tiles):
            left, left_other, right, right_other = (
                ref[0] if len(ref.shape) == 3 else ref[...] for ref in ins[4 * at : 4 * at + 4]
            )
            value = (mm(left, right) + mm(left_other, right_other)).astype(BF16)
            columns = slice(first, first + tile[4])
            first += tile[4]
            cut_rows(value, slowest, sent_ref, kept_ref, columns)
        if extra:
            value = (ins[-2][...] + ins[-1][...]).astype(BF16)
            cut_rows(value, slowest, sent_ref, kept_ref, slice(width, full))

    out = (count // 2, full)
    return run(body, operands, [(out, BF16)] * 2, (1,), specs, [fixed(out)] * 2)


def cut_rows(value, slowest, sent_ref, kept_ref, columns):
    part = value.shape[0] // 2 // slowest
    for group in range(slowest):
        low = 2 * group * part
        rows = slice(group * part, (group + 1) * part)
        kept_ref[rows, columns] = value[low : low + part]
        sent_ref[rows, columns] = value[low + part : low + 2 * part]


def product_wide(slowest, first, width, left, left_other, right, right_other):
    rows = right.shape[0]
    count = left.shape[0]

    def body(left_ref, left_other_ref, right_ref, right_other_ref, sent_ref, kept_ref):
        value = mm(left_ref[...], right_ref[...]) + mm(left_other_ref[...], right_other_ref[...])
        cut_rows(value.astype(BF16), slowest, sent_ref, kept_ref, slice(None))

    columns = pl.BlockSpec((rows, TILE), lambda j: (0, first // TILE + j))
    out_columns = pl.BlockSpec((count // 2, TILE), lambda j: (0, j))
    return run(
        body,
        (left, left_other, right, right_other),
        [((count // 2, width), BF16, "hbm")] * 2,
        (width // TILE,),
        [fixed(left.shape)] * 2 + [columns] * 2,
        [out_columns] * 2,
    )


def added(first, second, kind=BF16):
    return (first.astype(F32) + second.astype(F32)).astype(kind)


def halved(pairs, joined):
    half = pairs[0][0].shape[0] // 2
    widths = [mine.shape[1] for mine, _ in pairs]
    if half % 16:
        totals = [added(*pair) for pair in pairs]
        if joined:
            totals = [jnp.concatenate(totals, 1)]
        return [(total[half:], total[:half]) for total in totals]

    def body(*refs):
        ins, outs = refs[: 2 * len(pairs)], refs[2 * len(pairs) :]
        for at in range(len(pairs)):
            mine, got = ins[2 * at], ins[2 * at + 1]
            sent_ref, kept_ref = outs[:2] if joined else outs[2 * at : 2 * at + 2]
            first = sum(widths[:at]) if joined else 0
            columns = slice(first, first + widths[at])
            sent_ref[:, columns] = added(mine[half:, :], got[half:, :])
            kept_ref[:, columns] = added(mine[:half, :], got[:half, :])

    out_widths = [sum(widths)] if joined else widths
    outs = [((half, width), BF16) for width in out_widths for _ in range(2)]
    outs = run(body, [v for pair in pairs for v in pair], outs)
    return [tuple(outs[at : at + 2]) for at in range(0, len(outs), 2)]


def joined(places, middle, count, mine, got):
    wide = mine[0].shape[-1] if len(mine) == 1 else sum(value.shape[-1] for value in mine)
    parts = (slice(0, middle), slice(middle, wide))
    pairs = list(zip(places, mine, got))
    shapes = [(*value.shape[:at], 2, *value.shape[at:]) for at, value, _ in pairs]

    def widths(shape):
        if count == 1:
            return [(*shape[:-1], wide)]
        return [(*shape[:-1], part.stop - part.start) for part in parts]

    out_shapes = shapes if len(mine) == count else widths(shapes[0])
    if mine[0].shape[-2] % 16:
        both = [jnp.stack([value, come], at) for at, value, come in pairs]
        if len(mine) == count:
            return both
        if count == 1:
            rest = both[0].shape[:-1]
            return [jnp.concatenate([value.reshape(*rest, -1) for value in both], -1)]
        return [both[0][..., part] for part in parts]

    def body(*refs):
        outs = refs[2 * len(mine) :]
        for at, (place, value, _) in enumerate(pairs):
            for side in (0, 1):
                ref = refs[at + side * len(mine)]
                lead = (slice(None),) * place + (side,) + (slice(None),) * (value.ndim - 1 - place)
                if len(mine) == count:
                    outs[at][(*lead, slice(None))] = ref[...]
                elif count == 1:
                    outs[0][(*lead, parts[at])] = ref[...]
                else:
                    for out_ref, part in zip(outs, parts):
                        out_ref[(*lead, slice(None))] = ref[..., part]

    return run(body, [*mine, *got], [(shape, BF16) for shape in out_shapes])


def joined_all(bits, middle, blocks):
    rows, wide = blocks[0].shape
    parts = (slice(0, middle), slice(middle, wide))
    shape = (2,) * bits
    if rows % 16:
        whole = jnp.stack(blocks).reshape(*shape, rows, wide)
        return [whole[..., part] for part in parts]

    def body(*refs):
        for at, ref in enumerate(refs[: len(blocks)]):
            lead = tuple(at >> (bits - 1 - bit) & 1 for bit in range(bits))
            for out_ref, part in zip(refs[len(blocks) :], parts):
                out_ref[(*lead, slice(None), slice(None))] = ref[:, part]

    return run(
        body, blocks, [((*shape, rows, part.stop - part.start), BF16) for part in parts]
    )


class Sum:
    def __init__(self, links, firsts):
        self.links = links
        self.left, self.pairs = [], []
        self.z_left = links.z_bits
        for parts, order in zip(firsts, links.orders):
            self.add(parts, order)

    def add(self, parts, order):
        sent, kept = parts
        self.left.append(order[1:])
        self.pairs.append((kept, self.links.exchange(sent, order[0])))

    def step(self, order):
        inner = bool(self.left[0])
        joined = not inner and len(self.pairs) > 1
        parts = order(partial(halved, joined=joined), self.pairs)
        if inner:
            bits = [left[0] for left in self.left]
            self.left = [left[1:] for left in self.left]
        else:
            bits = [self.z_left[0]]
            self.z_left = self.z_left[1:]
        self.pairs = [
            (kept, self.links.exchange(sent, bit)) for (sent, kept), bit in zip(parts, bits)
        ]

    def settle(self, order):
        self.pairs = [(kept, order.settle(got)) for kept, got in self.pairs]

    def total(self):
        return added(*self.pairs[0], F32)


class Gather:
    def __init__(self, links, shards, middle, at_once=False):
        self.links, self.middle = links, middle
        steps = [tuple(reversed(order)) for order in links.orders]
        steps = list(zip(*steps))
        between = len(steps) // 2 if len(shards) == 2 else 0
        z_steps = ["all z"] if at_once else [(bit,) for bit in reversed(links.z_bits)]
        self.steps = steps[:between] + z_steps + steps[between:] + [("c", "c")]
        self.blocks = list(shards)
        self.bits = [(), ()]
        self.send()

    def send(self):
        if self.steps[0] == "all z":
            z_bits = self.links.z_bits
            chosen = [
                [bit for at, bit in enumerate(z_bits) if block >> (len(z_bits) - 1 - at) & 1]
                for block in range(1, 2 ** len(z_bits))
            ]
            self.got = [self.links.exchange(self.blocks[0], *bits) for bits in chosen]
            return
        self.got = [
            self.links.exchange(block, bit) for block, bit in zip(self.blocks, self.steps[0])
        ]

    def join(self, order):
        done, *self.steps = self.steps
        if done == "all z":
            z_bits = self.links.z_bits
            self.bits = [z_bits, z_bits]
            self.blocks = order(
                partial(joined_all, len(z_bits), self.middle), [*self.blocks, *self.got]
            )
            return
        bits = done * 2 if len(done) == 1 else done
        places = []
        for at, bit in enumerate(bits):
            held = sorted((*self.bits[at], bit), key=self.links.bits.index)
            self.bits[at] = tuple(held)
            places.append(held.index(bit))
        self.blocks = order(
            partial(joined, places, self.middle, len(self.steps[0])), self.blocks, self.got
        )
        if self.steps[0][0] == "c":
            self.blocks = [block.reshape(-1, block.shape[-1]) for block in self.blocks]

    def step(self, order):
        self.join(order)
        self.send()

    def settle(self, order):
        self.got = order.settle(self.got)

    def core_early(self, order):
        self.blocks = order.settle(self.blocks)
        self.early = [self.links.exchange(block, "c") for block in self.blocks]

    def core_late(self, order):
        self.got = order.settle(self.got)
        self.late = [self.links.exchange(got, "c") for got in self.got]

    def pieces(self):
        return [
            [values.reshape(-1, values.shape[-1]) for values in four]
            for four in zip(self.blocks, self.got, self.early, self.late)
        ]

    def halves(self):
        return list(zip(self.blocks, self.got))


def last_update(late, last, spans, scale, moments, vector_scale, vector_moments):
    spans, vectors_at = spans
    rows, width = moments[0].shape
    count = vector_moments[0].shape[0]

    def body(*refs):
        late_kept, late_got, last_kept, last_got, scale_ref = refs[:5]
        weight_ref, mean_ref, square_ref, vscale_ref, vector_ref, vmean_ref, vsquare_ref = refs[5:12]
        outs = refs[12:]
        sums = [added(late_kept[...], late_got[...], F32), added(last_kept[...], last_got[...], F32)]
        for of_last, first, place, size in spans:
            columns = slice(place, place + size)
            mean, square, stepped = adam_step(
                weight_ref[:, columns],
                sums[of_last][:, first : first + size],
                mean_ref[:, columns],
                square_ref[:, columns],
                matrix_rate,
                weight_decay,
            )
            outs[0][:, columns] = mean
            outs[1][:, columns] = square
            outs[2][:, columns] = stepped * scale_ref[:, columns]
        grads = sums[1][:, vectors_at : vectors_at + PAIR].T[:count]
        mean, square, stepped = adam_step(
            vector_ref[...], grads, vmean_ref[...], vsquare_ref[...], vector_rate, 0.0
        )
        outs[3][...] = mean
        outs[4][...] = square
        row = lax.broadcasted_iota(jnp.int32, stepped.shape, 0)
        outs[5][...] = jnp.where(row == 4, stepped * vscale_ref[...], stepped)

    return run(
        body,
        (*late, *last, scale, *moments, vector_scale, *vector_moments),
        [((rows, width), F32)] * 3 + [(vector_moments[0].shape, F32)] * 3,
    )


def local(
    links,
    tokens,
    cotangent,
    counts,
    w_qkv,
    w_out,
    w_up,
    w_down,
    vectors,
    mean_qkv,
    mean_out,
    mean_up,
    mean_down,
    mean_vectors,
    square_qkv,
    square_out,
    square_up,
    square_down,
    square_vectors,
):
    seq_count, slot_count, model_width = tokens.shape
    rows = seq_count * slot_count
    head_width = model_width // H
    wide = w_down.shape[0]
    vector_count, shard_width = vectors.shape
    half = model_width // 2
    order = Order()

    low_qkv = w_qkv.astype(BF16)
    thirds = [low_qkv[:, at * half : (at + 1) * half] for at in range(6)]
    shard_vectors = jnp.pad(vectors.astype(BF16).T, ((0, 0), (0, PAIR - vector_count)))
    shard_qkv = jnp.concatenate([*thirds[0::2], shard_vectors, *thirds[1::2]], 1)
    low_out, low_up = w_out.astype(BF16).T, w_up.astype(BF16)
    shard_up = jnp.concatenate(
        [low_out[:, :half], low_up[:, : wide // 2], low_out[:, half:], low_up[:, wide // 2 :]], 1
    )
    shard_down = w_down.astype(BF16).T
    gather_qkv = Gather(links, [shard_qkv], 3 * half + PAIR, True)
    gather_down = Gather(
        links, [shard_down[:, : wide // 2], shard_down[:, wide // 2 :]], wide // 2
    )

    true_rows = (
        links.true_block()[:, None] * shard_width + jnp.arange(shard_width, dtype=jnp.int32)
    ).reshape(1, model_width)
    to_relative = (
        lax.broadcasted_iota(jnp.int32, (model_width, model_width), 0) == true_rows
    ).astype(BF16)
    keep_rows = lax.broadcasted_iota(jnp.int32, (rows, 1), 0) < counts[0]
    d_result = jnp.where(keep_rows, cotangent.reshape(rows, model_width), 0).astype(BF16)
    inputs = mm(tokens.reshape(rows, model_width), to_relative).astype(BF16)
    d_result_turned = mm(d_result, to_relative).astype(BF16)
    d_columns = lax.dot_general(
        to_relative, d_result, (((0,), (1,)), ((), ())), preferred_element_type=F32
    ).astype(BF16)

    def longer(gather, count):
        while len(gather.steps) > count:
            gather.step(order)

    inputs, d_result_turned, d_columns, to_relative = order.settle(
        (inputs, d_result_turned, d_columns, to_relative)
    )
    longer(gather_qkv, 4)
    gather_down.settle(order)
    d_other = order.settle(links.exchange(d_columns[half:], "c"))
    d_mine = d_columns[:half]
    gather_qkv.step(order)
    gather_up = Gather(
        links, [order(lambda values: values + 0, shard_up)], half + wide // 2
    )
    gather_qkv.step(order)
    longer(gather_up, 5)
    gather_up.step(order)
    slowest = [1, 2 ** len(links.y_bits)]
    in_pieces = half // 2 // slowest[1] % PAIR == 0
    ranges_down = []
    for slow in slowest:
        group = half // slow
        cuts = ((0, group // 2), (group // 2, group)) if in_pieces else ((0, group),)
        ranges_down.append(
            [
                [(core + at * group + low, core + at * group + high) for at in range(slow)]
                for core in (0, half)
                for low, high in cuts
            ]
        )
    d_late = order.settle(d_result_turned)
    grads_down = [
        d_result_turned,
        order.settle(
            jnp.concatenate(
                [d_late[:, low:high] for places in ranges_down[1] for low, high in places], 1
            )
        ),
    ]
    gather_qkv.step(order)
    gather_up.step(order)
    longer(gather_down, 5)
    gather_down.step(order)
    halves_qkv = gather_qkv.halves()
    normed_low, normed_high, normed_mine, normed_send, vector_rows, true_vectors = order(
        first_norm, inputs, *halves_qkv[0], to_relative
    )
    normed_other = links.exchange(normed_send, "c")
    projected = [
        order(partial(project, at), normed_low, normed_high, *halves_qkv[at], true_vectors)
        for at in (0, 1)
    ]
    normed_other = order.settle(normed_other)
    gather_up.step(order)
    shared, peak = order(attend, projected, counts)
    gather_down.step(order)
    shared_other = links.exchange(shared, "c")
    peak, peak_got = [peak], []

    def peak_send(bit):
        sent = order.settle(peak[0])
        peak_got.append(links.exchange(sent, bit))

    def peak_take():
        peak[0] = order(jnp.maximum, peak[0], peak_got.pop())

    first_bit, *more_bits = links.bits
    peak_send(first_bit)
    peak_take()
    for bit in more_bits[4:]:
        peak_send(bit)
        peak_take()
    peak_send(more_bits[0])
    gather_up.step(order)
    shared_other = order.settle(shared_other)
    peak_take()
    peak_send(more_bits[1])
    peak_take()
    peak_send(more_bits[2])
    gather_down.step(order)
    peak_take()
    peak_send(more_bits[3])
    halves_up = gather_up.halves()
    middle, normed_two_low, normed_two_high, normed_two_mine, normed_two_send = order(
        second_norm, inputs, shared, halves_up, vector_rows
    )
    peak_take()
    normed_two_other = links.exchange(normed_two_send, "c")
    if in_pieces:
        gather_down.core_early(order)
    hidden, slope, hidden_other = [], [], []
    for at in (0, 1):
        out, out_slope = order(
            partial(expand, at), normed_two_low, normed_two_high, *halves_up[at], true_vectors
        )
        hidden.append(out)
        slope.append(out_slope)
        hidden_other.append(links.exchange(out, "c"))
        if at == 0:
            normed_two_other = order.settle(normed_two_other)
            if in_pieces:
                gather_down.early = order.settle(gather_down.early)

    down_parts = [
        order(
            partial(product_wide, slowest[at], 0, wide // 2),
            d_mine,
            d_other,
            hidden[at],
            hidden_other[at],
        )
        for at in (0, 1)
    ]
    if in_pieces:
        gather_down.core_late(order)
    else:
        gather_down.step(order)
    sum_down = Sum(links, order.settle(down_parts))
    weights_down = gather_down.pieces() if in_pieces else gather_down.halves()
    d_pre, d_pre_sums = order(expand_back, grads_down, weights_down, slope)
    d_pre_other = links.exchange(d_pre, "c")
    partial_sum = order(contract_first, d_pre, *halves_up[0])
    result = order(
        partial(finish_first, ranges=ranges_down[0]), middle, hidden[0], weights_down[0], vector_rows
    )
    for _ in links.orders[0][1:]:
        sum_down.step(order)
    sum_up = Sum(
        links,
        [
            order(
                partial(product_wide, slowest[at], at * wide // 2, wide // 2),
                normed_two_mine,
                normed_two_other,
                d_pre,
                d_pre_other,
            )
            for at in (0, 1)
        ],
    )
    d_middle, d_branch_low, d_branch_high, d_out_one, d_out_two, grads = order(
        contract_second, d_pre, halves_up, partial_sum, middle, d_result_turned, vector_rows
    )
    d_branch_other = links.exchange(d_branch_high, "c")
    sum_down.step(order)
    d_branch_other = order.settle(d_branch_other)
    d_projected, d_projected_other, head_sums = [], [], []
    for at, d_out in enumerate((d_out_one, d_out_two)):
        out, sums = order(attend_back, projected[at], d_out, counts)
        d_projected.append(out)
        d_projected_other.append(links.exchange(out, "c"))
        head_sums.append(sums)


    def out_tile(at):
        return (d_branch_low, d_branch_other, shared, shared_other, half, (0, at))

    def qkv_tile(at, part, width, column):
        return (
            normed_mine,
            normed_other,
            d_projected[at],
            d_projected_other[at],
            width,
            (part, 0, column),
        )

    def late_product(at, tiles, extra=()):
        def call(operands, extra):
            return product(
                slowest[at],
                [(*operands[4 * i : 4 * i + 4], *tile[4:]) for i, tile in enumerate(tiles)],
                extra,
            )

        return order(call, [operand for tile in tiles for operand in tile[:4]], extra)

    partial_sum = order(input_back_first, d_projected[0], *halves_qkv[0])
    for _ in links.z_bits[1:]:
        sum_down.step(order)
    d_projected_other = order.settle(d_projected_other)
    quarter = half // 2
    sum_late = Sum(
        links,
        [
            late_product(at, [out_tile(at), qkv_tile(0, at, half, 0), qkv_tile(0, 2, quarter, at)])
            for at in (0, 1)
        ],
    )
    for _ in links.orders[0][1:]:
        sum_up.step(order)
    token_grad, vectors_low, vectors_high = order(
        input_back_second,
        d_projected[1],
        *halves_qkv[1],
        partial_sum,
        inputs,
        d_middle,
        grads,
        head_sums,
        d_pre_sums,
        vector_rows,
        to_relative,
    )
    token_grad = token_grad.reshape(seq_count, slot_count, model_width)
    sum_down.settle(order)
    vectors_other = links.exchange(vectors_high, "c")
    sum_up.step(order)
    last = [
        late_product(
            at,
            [qkv_tile(1, at, half, 0), qkv_tile(1, 2, quarter, at)],
            ((), (vectors_low, vectors_other))[at],
        )
        for at in (0, 1)
    ]
    sum_last = Sum(links, last)
    result = order(
        partial(finish_second, ranges=ranges_down[1]),
        result,
        hidden[1],
        weights_down[1],
        to_relative,
        counts,
    )
    result_out = result.reshape(seq_count, slot_count, model_width)
    for _ in links.orders[0][1:]:
        sum_late.step(order)
    for _ in links.z_bits[1:]:
        sum_up.step(order)
    for _ in links.orders[0][1:]:
        sum_last.step(order)
    sum_late.step(order)
    sum_last.step(order)
    mean_down, mean_up = order.settle((mean_down, mean_up))
    sum_up.settle(order)
    for _ in links.z_bits[1:]:
        sum_late.step(order)
    head_peak = order.settle(peak[0])[:, 0]
    vectors, mean_vectors, square_vectors, first_col = order.settle(
        (
            vectors,
            mean_vectors,
            square_vectors,
            lax.axis_index(("dp", "fsdp")) * shard_width,
        )
    )
    shrink = jnp.sqrt(clip_limit / jnp.maximum(head_peak, clip_limit))
    head_cols = jnp.repeat(shrink, head_width)
    qkv_scale = jnp.concatenate([head_cols, head_cols, jnp.ones((model_width,), F32)])[None]
    col_head = (first_col + jnp.arange(shard_width, dtype=jnp.int32)) // head_width
    col_shrink = jnp.sum(
        jnp.where(
            col_head[:, None] == jnp.arange(H, dtype=jnp.int32)[None, :], shrink[None, :], 0.0
        ),
        1,
    )[None]
    for _ in links.z_bits[1:]:
        sum_last.step(order)
    sum_late.settle(order)
    spans = (
        (0, half, 0, half),
        (1, 0, half, half),
        (0, half * 3 + quarter, 2 * half, half),
        (1, half + quarter, 3 * half, half),
        (0, 2 * half, 4 * half, quarter),
        (0, 4 * half + quarter, 4 * half + quarter, quarter),
        (1, half, 5 * half, quarter),
        (1, 2 * half + quarter, 5 * half + quarter, quarter),
    )
    vectors_at = 3 * half
    late = sum_late.total()
    reduced_out = jnp.concatenate([late[:, :half], late[:, 2 * half + quarter :][:, :half]], 1).T
    reduced_up = sum_up.total()
    reduced_down = sum_down.total().T
    mean_o, square_o, new_out = adam_step(
        w_out, reduced_out, mean_out, square_out, matrix_rate, weight_decay
    )
    mean_u, square_u, new_up = adam_step(
        w_up, reduced_up, mean_up, square_up, matrix_rate, weight_decay
    )
    mean_d, square_d, new_down = adam_step(
        w_down, reduced_down, mean_down, square_down, matrix_rate, weight_decay
    )
    if shard_width % 8 == 0:
        mean_q, square_q, new_qkv, mean_v, square_v, new_vectors = last_update(
            sum_late.pairs[0],
            sum_last.pairs[0],
            (spans, vectors_at),
            qkv_scale,
            (w_qkv, mean_qkv, square_qkv),
            col_shrink,
            (vectors, mean_vectors, square_vectors),
        )
    else:
        sums = (late, sum_last.total())
        reduced_qkv = jnp.concatenate(
            [sums[which][:, first : first + size] for which, first, _, size in spans], 1
        )
        mean_q, square_q, stepped_qkv = adam_step(
            w_qkv, reduced_qkv, mean_qkv, square_qkv, matrix_rate, weight_decay
        )
        new_qkv = stepped_qkv * qkv_scale
        reduced_vectors = sums[1][:, vectors_at : vectors_at + vector_count].T
        mean_v, square_v, stepped_vectors = adam_step(
            vectors, reduced_vectors, mean_vectors, square_vectors, vector_rate, 0.0
        )
        row_pick = (jnp.arange(vector_count, dtype=jnp.int32) == 4)[:, None]
        new_vectors = jnp.where(row_pick, stepped_vectors * col_shrink, stepped_vectors)
    return (
        result_out,
        token_grad,
        head_peak,
        mean_q,
        square_q,
        new_qkv,
        mean_o,
        square_o,
        new_out,
        mean_u,
        square_u,
        new_up,
        mean_d,
        square_d,
        new_down,
        mean_v,
        square_v,
        new_vectors,
    )


def solution(mesh):
    links = Links(mesh.shape["dp"], mesh.shape["fsdp"])
    return jax.shard_map(
        partial(local, links),
        mesh=mesh,
        in_specs=(
            P(("dp", "fsdp"), None, None),
            P(("dp", "fsdp"), None, None),
            P(("dp", "fsdp")),
            P(("dp", "fsdp"), None),
            P(None, ("dp", "fsdp")),
            P(("dp", "fsdp"), None),
            P(None, ("dp", "fsdp")),
            P(None, ("dp", "fsdp")),
            P(("dp", "fsdp"), None),
            P(None, ("dp", "fsdp")),
            P(("dp", "fsdp"), None),
            P(None, ("dp", "fsdp")),
            P(None, ("dp", "fsdp")),
            P(("dp", "fsdp"), None),
            P(None, ("dp", "fsdp")),
            P(("dp", "fsdp"), None),
            P(None, ("dp", "fsdp")),
            P(None, ("dp", "fsdp")),
        ),
        out_specs=(
            P(("dp", "fsdp"), None, None),
            P(("dp", "fsdp"), None, None),
            P(),
            P(("dp", "fsdp"), None),
            P(("dp", "fsdp"), None),
            P(("dp", "fsdp"), None),
            P(None, ("dp", "fsdp")),
            P(None, ("dp", "fsdp")),
            P(None, ("dp", "fsdp")),
            P(("dp", "fsdp"), None),
            P(("dp", "fsdp"), None),
            P(("dp", "fsdp"), None),
            P(None, ("dp", "fsdp")),
            P(None, ("dp", "fsdp")),
            P(None, ("dp", "fsdp")),
            P(None, ("dp", "fsdp")),
            P(None, ("dp", "fsdp")),
            P(None, ("dp", "fsdp")),
        ),
        check_vma=False,
    )
```
